128 devices in a mesh: wide: 32 (over z, x, core), narrow: 4 (over y).
Axes of the slice: x: 4, y: 4, z: 4, core: 2. Of those that a mesh axis runs over, the one named last changes fastest.
Arguments:
- features: bfloat16 [65536, 256], P(('wide', 'narrow')), may hold values from -6 to 6
- neighbours: int32 [65536, 8], P(('wide', 'narrow')), may hold values from 0 to 2047
- code_ids: int32 [65536, 16], P(('wide', 'narrow')), may hold values from 0 to 4095
- assignment: int32 [65536], P(('wide', 'narrow')), may hold values from 0 to 4095
- cotangent: bfloat16 [65536, 256], P(('wide', 'narrow')), may hold values from -6 to 6
- code_sums: float32 [4096, 256], replicated, may hold values from -24 to 24
- code_counts: float32 [4096], replicated, may hold values from 1 to 10
- self_weight: bfloat16 [256, 256], replicated, may hold values from -0.375 to 0.375
- neighbour_weight: bfloat16 [256, 256], replicated, may hold values from -0.375 to 0.375
Outputs:
- output: bfloat16 [65536, 256], P(('wide', 'narrow'))
- feature_grad: bfloat16 [65536, 256], P(('wide', 'narrow'))
- self_grad: float32 [256, 256], replicated
- neighbour_grad: float32 [256, 256], replicated
- new_codebook: float32 [4096, 256], P(('wide', 'narrow'))
- code_grad: float32 [4096, 256], P(('wide', 'narrow'))
The draws below stay inside these ranges and needn't reach their ends.
All inputs are finite; a program needn't handle non-finite values.
Results may differ from the reference program's by a relative error of at most 0.0075.
Values may be sent and summed in bfloat16 or wider, within the bound.
A program may use at most 128 MiB of HBM per device.

```python
import math
import jax
import jax.numpy as jnp

F = 256
H = 256
K = 4096
NODES_DEV = 512
NB = 8
NC = 16
GROUP_ROWS = 2048
NODES = 65536
N_NARROW = 4


def touch_ends(drawn, stream_key, least, high):
    spot = [jax.random.randint(jax.random.fold_in(stream_key, axis), (), 0, length) for axis, length in enumerate(drawn.shape)]
    longest = drawn.shape.index(max(drawn.shape))
    neighbour = spot[:longest] + [(spot[longest] + 1) % drawn.shape[longest]] + spot[longest + 1:]
    return drawn.at[tuple(spot)].set(least).at[tuple(neighbour)].set(high)


def steps_of(key, shape, cuts, low, top_value):
    loudness = 1.0
    for axis_at, blocks in cuts:
        heights = jax.random.uniform(jax.random.fold_in(jax.random.fold_in(key, 6), axis_at), (blocks,), jnp.float32, low / len(cuts), top_value / len(cuts))
        loudness = loudness * jnp.repeat(jnp.exp(heights), shape[axis_at] // blocks).reshape((-1,) + (1,) * (len(shape) - 1 - axis_at))
    return loudness


def bell_draw(own_key, dims, width, most, pieces=(), kind=jnp.bfloat16):
    entries = width * jax.random.normal(own_key, dims, jnp.float32)
    if pieces:
        entries = entries * steps_of(own_key, dims, pieces, -0.22, 0.18)
    return jnp.clip(entries, -most, most).astype(kind)


def setup_inputs(seed: int = 0) -> dict:
    streams_of = jax.random.split(jax.random.key(seed), 10)
    features = bell_draw(streams_of[0], (NODES, F), 1.0, 6.0, ((0, 128),))
    neighbours = touch_ends(jax.random.randint(streams_of[1], (NODES, NB), 0, GROUP_ROWS), jax.random.fold_in(streams_of[1], 1), 0, GROUP_ROWS - 1).astype(jnp.int32)
    code_ids = touch_ends(jax.random.randint(streams_of[2], (NODES, NC), 0, K), jax.random.fold_in(streams_of[2], 1), 0, K - 1).astype(jnp.int32)
    assignment = touch_ends(jax.random.randint(streams_of[3], (NODES,), 0, K), jax.random.fold_in(streams_of[3], 1), 0, K - 1).astype(jnp.int32)
    cotangent = bell_draw(streams_of[4], (NODES, H), 1.0, 6.0, ((0, 128),))
    code_sums = bell_draw(streams_of[5], (K, F), 4.0, 24.0, (), jnp.float32)
    code_counts = jnp.clip(jnp.exp(jax.random.uniform(streams_of[6], (K,), jnp.float32, math.log(1.0), math.log(10.0))), 1.0, 10.0)
    self_weight = bell_draw(streams_of[7], (F, H), F ** -0.5, 0.375)
    neighbour_weight = bell_draw(streams_of[8], (F, H), F ** -0.5, 0.375)
    return dict(features=features, neighbours=neighbours, code_ids=code_ids, assignment=assignment, cotangent=cotangent, code_sums=code_sums, code_counts=code_counts, self_weight=self_weight, neighbour_weight=neighbour_weight)


decay_rate = 0.5


def reference(features, neighbours, code_ids, assignment, cotangent, code_sums, code_counts, self_weight, neighbour_weight):
    node_total = features.shape[0]
    group_size = NODES_DEV * N_NARROW
    group_base = (jnp.arange(node_total, dtype=jnp.int32) // group_size) * group_size
    feats_wide = features.astype(jnp.float32)
    near = jnp.zeros((node_total, features.shape[1]), jnp.float32)
    for slot_index in range(NB):
        near = near + feats_wide[group_base + neighbours[:, slot_index]]
    codebook = (code_sums / code_counts[:, None]).astype(jnp.bfloat16)
    code_wide = codebook.astype(jnp.float32)
    far = jnp.zeros((node_total, features.shape[1]), jnp.float32)
    for pick_index in range(NC):
        far = far + code_wide[code_ids[:, pick_index]]
    agg = (near / NB + far / NC).astype(jnp.bfloat16)
    hidden = jnp.dot(features, self_weight, preferred_element_type=jnp.float32) + jnp.dot(agg, neighbour_weight, preferred_element_type=jnp.float32)
    output = (hidden * jax.nn.sigmoid(hidden)).astype(jnp.bfloat16)
    sigma = jax.nn.sigmoid(hidden)
    hidden_grad = (cotangent.astype(jnp.float32) * sigma * (1.0 + hidden * (1.0 - sigma))).astype(jnp.bfloat16)
    self_grad = jnp.dot(features.T, hidden_grad, preferred_element_type=jnp.float32)
    neighbour_grad = jnp.dot(agg.T, hidden_grad, preferred_element_type=jnp.float32)
    agg_grad = jnp.dot(hidden_grad, neighbour_weight.T, preferred_element_type=jnp.float32).astype(jnp.bfloat16)
    spread_term = agg_grad.astype(jnp.float32) / NB
    feature_grad = jnp.dot(hidden_grad, self_weight.T, preferred_element_type=jnp.float32)
    for slot_index in range(NB):
        feature_grad = feature_grad.at[group_base + neighbours[:, slot_index]].add(spread_term)
    feature_grad = feature_grad.astype(jnp.bfloat16)
    code_total = code_sums.shape[0]
    code_grad = jnp.zeros(code_sums.shape, jnp.float32)
    for pick_index in range(NC):
        code_grad = code_grad + jax.ops.segment_sum(agg_grad.astype(jnp.float32), code_ids[:, pick_index], num_segments=code_total)
    code_grad = code_grad / NC
    assigned_sum = jax.ops.segment_sum(feats_wide, assignment, num_segments=code_total)
    assigned_count = jax.ops.segment_sum(jnp.ones((node_total,), jnp.float32), assignment, num_segments=code_total)
    new_codebook = (decay_rate * code_sums + (1.0 - decay_rate) * assigned_sum) / (decay_rate * code_counts + (1.0 - decay_rate) * assigned_count)[:, None]
    return output, feature_grad, self_grad, neighbour_grad, new_codebook, code_grad
```

```python
import functools

import jax
import jax.numpy as jnp
from jax import lax
from jax.experimental import pallas as pl
from jax.experimental.pallas import tpu as pltpu
from jax.sharding import PartitionSpec as P

MESH = pl.DeviceIdType.MESH
F32, BF16, I32 = jnp.float32, jnp.bfloat16, jnp.int32
decay_rate = 0.5
IDX_ROWS = 32
NIBBLES = 0x0F0F0F0F


def dot(a, b):
    return jnp.dot(a, b, preferred_element_type=F32)


def dot_nt(a, b):
    return lax.dot_general(a, b, (((1,), (1,)), ((), ())), preferred_element_type=F32)


def dot_tn(a, b):
    return lax.dot_general(a, b, (((0,), (0,)), ((), ())), preferred_element_type=F32)


def words_of(spots, his, vals):
    word = None
    for hi, val in zip(his, vals):
        term = jnp.where(spots == hi, val, 0)
        word = term if word is None else word + term
    return word


def fields_of(words):
    even = odd = None
    for word in words:
        low, high = word & NIBBLES, (word >> 4) & NIBBLES
        even = low if even is None else even + low
        odd = high if odd is None else odd + high
    out = []
    for field in range(8):
        part = (even, odd)[field % 2]
        shift = 8 * (field // 2)
        if shift:
            part = part >> shift
        if shift < 24:
            part = part & 255
        out.append(part.astype(F32).astype(BF16))
    return out


def kernel(
    wide, narrow, shard,
    feat, nb_t, code_t, assign, cot, sums_hbm, counts, ws, wn,
    out, fgrad, sgrad, ngrad, newcb, cgrad,
    sums, codebook, featg, daggg, idxg, ids_nt, idx_pad, tab_far, tab_near, tab_code, tab_ret, tab_asn,
    hi_t, val_t, hi_r, val_r, row_a, far, near, hid, dz_all, agg_all, acc, ret,
    wg_f, wg_tx, wg_rx, wgb_tx, wgb_rx, wgc, wgd, as_f, as_cnt, as_tx, as_rx, asb_tx, asb_rx,
    cg_tx, cg_rx, cgb_tx, cgb_rx, cnt_col,
    sums_sem, f_s, f_r, d_s, d_r, i_s, i_r, wa_s, wa_r, wb_s, wb_r, wc_s, wc_r, wd_s, wd_r,
    aa_s, aa_r, ab_s, ab_r, ca_s, ca_r, cb_s, cb_r,
):
    n = feat.shape[0]
    half = n // 2
    chips = wide // 2
    codes = sums.shape[0]
    mine = codes // narrow
    own_half = mine // 2
    grp = n * narrow
    w = lax.axis_index("wide")
    y = lax.axis_index("narrow")
    core = w % 2
    chip = w // 2
    y_right, y_left, y_far = (y + 1) % narrow, (y + 3) % narrow, (y + 2) % narrow
    other = chip * 2 + (1 - core)

    def chip_dev(step):
        return ((chip + step) % chips) * 2 + core

    def rcopy(src, dst, ssem, rsem, dev):
        return pltpu.make_async_remote_copy(
            src_ref=src, dst_ref=dst, send_sem=ssem, recv_sem=rsem, device_id=dev, device_id_type=MESH
        )

    sums_copy = pltpu.make_async_copy(sums_hbm, sums, sums_sem)
    sums_copy.start()

    barrier = pltpu.get_barrier_semaphore()
    for peer in (y_right, y_left, y_far):
        pl.semaphore_signal(barrier, inc=1, device_id=(w, peer), device_id_type=MESH)

    def greet(step, carry):
        pl.semaphore_signal(barrier, inc=1, device_id=((w + step) % wide, y), device_id_type=MESH)
        return carry

    lax.fori_loop(1, wide, greet, 0)

    featg[pl.ds(0, n), :] = feat[...]
    idxg[0, 0:8, :] = nb_t[...]
    idxg[0, 8:24, :] = code_t[...]
    idxg[0, 24:32, :] = jnp.broadcast_to(assign[...], (8, n))
    idx_pad[...] = jnp.zeros_like(idx_pad)
    nb_own = nb_t[...]
    node_bits = n.bit_length() - 1
    slot_of = ((nb_own >> node_bits) - y) & (narrow - 1)
    idx_pad[0:8, :] = (slot_of << node_bits) | (nb_own & (n - 1))
    idx_pad[8:24, :] = code_t[...]
    ids_nt[...] = jnp.transpose(idx_pad[...])

    pl.semaphore_wait(barrier, narrow - 1 + wide - 1)

    def low(slot):
        return pl.ds(slot * n, half)

    def high(slot):
        return pl.ds(slot * n + half, half)

    def gather_copies(buf, ssem, rsem):
        right, left = (w, y_right), (w, y_left)

        def make(src, dst, at, dev):
            return rcopy(buf.at[src, :], buf.at[dst, :], ssem.at[at], rsem.at[at], dev)

        return (
            make(low(0), low(3), 0, right),
            make(high(0), high(1), 1, left),
            make(high(0), high(3), 2, right),
            make(low(0), low(1), 3, left),
            make(low(3), low(2), 4, right),
            make(high(1), high(2), 5, left),
        )

    def arrived(buf, ssem, rsem, at):
        region = (low(3), high(1), high(3), low(1), low(2), high(2))[at]
        rcopy(buf.at[region, :], buf.at[region, :], ssem.at[at], rsem.at[at], (w, y_right)).wait_recv()

    f_copies = gather_copies(featg, f_s, f_r)
    for at in range(4):
        f_copies[at].start()
    i_copies = []
    for at, (peer, slot) in enumerate(((y_right, 3), (y_left, 1), (y_far, 2))):
        i_copies.append(rcopy(idxg.at[0], idxg.at[slot], i_s.at[at], i_r.at[at], (w, peer)))
        i_copies[-1].start()

    far_spots = codes // 8
    far_bits = far_spots.bit_length() - 1
    near_spots = grp // 8
    near_bits = near_spots.bit_length() - 1

    def far_tile(tile, carry):
        rows = pl.ds(pl.multiple_of(tile * 16, 16), 16)
        ids = ids_nt[rows, :]
        hi = ids & (far_spots - 1)
        val = jnp.int32(1) << ((ids >> far_bits) * 4)
        his = [jnp.broadcast_to(hi[:, 8 + j : 9 + j], (16, 128)) for j in range(16)]
        vals = [jnp.broadcast_to(val[:, 8 + j : 9 + j], (16, 128)) for j in range(16)]
        for part in range(far_spots // 128):
            spots = lax.broadcasted_iota(I32, (16, 128), 1) + part * 128
            words = (words_of(spots, his[:8], vals[:8]), words_of(spots, his[8:], vals[8:]))
            for field, counts_part in enumerate(fields_of(words)):
                tab_far[rows, pl.ds(field * far_spots + part * 128, 128)] = counts_part
        return carry

    def near_tile(tile, carry):
        rows = pl.ds(pl.multiple_of(tile * 16, 16), 16)
        ids = ids_nt[rows, :]
        hi = ids & (near_spots - 1)
        val = jnp.int32(1) << ((ids >> near_bits) * 4)
        his = [jnp.broadcast_to(hi[:, j : j + 1], (16, 128)) for j in range(8)]
        vals = [jnp.broadcast_to(val[:, j : j + 1], (16, 128)) for j in range(8)]
        for part in range(near_spots // 128):
            spots = lax.broadcasted_iota(I32, (16, 128), 1) + part * 128
            words = (words_of(spots, his, vals),)
            for field, counts_part in enumerate(fields_of(words)):
                tab_near[rows, pl.ds(field * near_spots + part * 128, 128)] = counts_part
        return carry

    def book_block(block, carry):
        rows = pl.ds(pl.multiple_of(block * 128, 128), 128)
        inverse = 1.0 / counts[pl.ds(block, 1), :]
        column = jnp.transpose(jnp.broadcast_to(inverse, (128, 128)))
        for part in range(sums.shape[1] // 128):
            lanes = pl.ds(part * 128, 128)
            codebook[rows, lanes] = (sums[rows, lanes] * column).astype(BF16)
        return carry

    lax.fori_loop(0, n // 32, far_tile, 0)
    arrived(featg, f_s, f_r, 0)
    f_copies[4].start()
    arrived(featg, f_s, f_r, 1)
    f_copies[5].start()
    lax.fori_loop(n // 32, n // 16, far_tile, 0)
    sums_copy.wait()
    lax.fori_loop(0, codes // 128, book_block, 0)
    far[...] = dot(tab_far[...], codebook[...]) * (1.0 / 16)
    lax.fori_loop(0, n // 16, near_tile, 0)
    hid[...] = dot(feat[...], ws[...])
    near[...] = dot(tab_near[:, 0:n], feat[...])
    arrived(featg, f_s, f_r, 2)
    near[...] += dot(tab_near[:, 3 * n : 4 * n], featg[3 * n : 4 * n, :])
    arrived(featg, f_s, f_r, 3)
    near[...] += dot(tab_near[:, n : 2 * n], featg[n : 2 * n, :])
    arrived(featg, f_s, f_r, 4)
    arrived(featg, f_s, f_r, 5)

    d_copies = gather_copies(daggg, d_s, d_r)
    for at in range(2):
        rows = pl.ds(at * half, half)
        total = near[rows, :] + dot(tab_near[rows, 2 * n : 3 * n], featg[2 * n : 3 * n, :])
        agg = (total * (1.0 / 8) + far[rows, :]).astype(BF16)
        agg_all[rows, :] = agg
        z = hid[rows, :] + dot(agg, wn[...])
        s = jax.nn.sigmoid(z)
        out[rows, :] = (z * s).astype(BF16)
        dz = (cot[rows, :].astype(F32) * s * (1.0 + z * (1.0 - s))).astype(BF16)
        dz_all[rows, :] = dz
        daggg[rows, :] = dot_nt(dz, wn[...]).astype(BF16)
        d_copies[(0, 1)[at]].start()
        d_copies[(3, 2)[at]].start()

    def weight_half(which, x):
        wg_f[which] = dot_tn(x, dz_all[...])

    weight_half(0, feat[...])
    weight_half(1, agg_all[...])
    wg_tx[...] = wg_f[1 - core].astype(BF16)
    wa = rcopy(wg_tx, wg_rx, wa_s, wa_r, (other, y))
    wa.start()

    for at in range(3):
        i_copies[at].wait_recv()
    shard_bits = shard.bit_length() - 1
    narrow_bits = narrow.bit_length() - 1
    mine_spots = mine // 8
    mine_bits = mine_spots.bit_length() - 1
    ret_spots = n // 8
    ret_bits = ret_spots.bit_length() - 1

    def place(k):
        kw = k >> (shard_bits + narrow_bits)
        row = ((((kw & 1) ^ core) * chips + (((kw >> 1) - chip) & (chips - 1))) << shard_bits) | (k & (shard - 1))
        return row, ((k >> shard_bits) & (narrow - 1)) == y

    for slot in range(narrow):
        lanes = pl.ds(slot * n, n)
        ids = idxg[slot, 0:8, :]
        hi_r[:, lanes] = ids & (ret_spots - 1)
        local = ids & (n - 1)
        val_r[:, lanes] = jnp.where((ids >> node_bits) == y, jnp.int32(1) << ((local >> ret_bits) * 4), 0)
        row, hit = place(idxg[slot, 8:24, :])
        hi_t[:, lanes] = row & (mine_spots - 1)
        val_t[:, lanes] = jnp.where(hit, jnp.int32(1) << ((row >> mine_bits) * 4), 0)
        row, hit = place(idxg[slot, 24:32, :])
        row_a[:, lanes] = jnp.where(hit, row, -1)

    def asn_tile(tile, carry):
        lanes = pl.ds(pl.multiple_of(tile * 128, 128), 128)
        row = jnp.broadcast_to(row_a[0:1, lanes], (16, 128))
        for part in range(mine // 16):
            spots = lax.broadcasted_iota(I32, (16, 128), 0) + part * 16
            tab_asn[pl.ds(part * 16, 16), lanes] = jnp.where(row == spots, 1.0, 0.0).astype(BF16)
        return carry

    def code_tile(tile, carry):
        lanes = pl.ds(pl.multiple_of(tile * 128, 128), 128)
        his = [jnp.broadcast_to(hi_t[j : j + 1, lanes], (16, 128)) for j in range(16)]
        vals = [jnp.broadcast_to(val_t[j : j + 1, lanes], (16, 128)) for j in range(16)]
        for part in range(mine_spots // 16):
            spots = lax.broadcasted_iota(I32, (16, 128), 0) + part * 16
            words = (words_of(spots, his[:8], vals[:8]), words_of(spots, his[8:], vals[8:]))
            for field, counts_part in enumerate(fields_of(words)):
                tab_code[pl.ds(field * mine_spots + part * 16, 16), lanes] = counts_part
        return carry

    def ret_tile(tile, carry):
        lanes = pl.ds(pl.multiple_of(tile * 128, 128), 128)
        his = [jnp.broadcast_to(hi_r[j : j + 1, lanes], (16, 128)) for j in range(8)]
        vals = [jnp.broadcast_to(val_r[j : j + 1, lanes], (16, 128)) for j in range(8)]
        for part in range(ret_spots // 16):
            spots = lax.broadcasted_iota(I32, (16, 128), 0) + part * 16
            words = (words_of(spots, his, vals),)
            for field, counts_part in enumerate(fields_of(words)):
                tab_ret[pl.ds(field * ret_spots + part * 16, 16), lanes] = counts_part
        return carry

    def split_count(count):
        big = jnp.floor(count * (1.0 / 256)) * 256.0
        lane = lax.broadcasted_iota(I32, count.shape, 1)
        return jnp.where(lane < 64, big, count - big).astype(BF16)

    def join_count(pair):
        pair = pair.astype(F32)
        return pair + pltpu.roll(pair, 64, 1)

    width = feat.shape[1]
    lax.fori_loop(0, grp // 128, asn_tile, 0)
    as_f[...] = dot(tab_asn[...], featg[...])
    as_cnt[...] = dot(tab_asn[...], jnp.ones((grp, 128), BF16))
    as_tx[:, 0:width] = as_f[own_half:, :].astype(BF16)
    as_tx[:, width:] = split_count(as_cnt[own_half:, :])
    aa = rcopy(as_tx, as_rx, aa_s, aa_r, (other, y))
    aa.start()

    tiles = grp // 128
    lax.fori_loop(0, tiles // 4, code_tile, 0)

    arrived(daggg, d_s, d_r, 0)
    d_copies[4].start()
    arrived(daggg, d_s, d_r, 1)
    d_copies[5].start()

    wa.wait_recv()
    wg_own = wg_f[core] + wg_rx[...].astype(F32)
    wg_f[core] = wg_own
    wgb_tx[...] = wg_own.astype(BF16)
    part_rows = wg_own.shape[0] // chips

    def wg_rows(step):
        return pl.ds(pl.multiple_of(((chip + step) % chips) * part_rows, part_rows), part_rows)

    wb = {}
    for step in range(1, chips):
        wb[step] = rcopy(
            wgb_tx.at[wg_rows(step), :], wgb_rx.at[step], wb_s.at[step], wb_r.at[step], (chip_dev(step), y)
        )
        wb[step].start()

    aa.wait_recv()
    as_f[0:own_half, :] += as_rx[:, 0:width].astype(F32)
    as_cnt[0:own_half, :] += join_count(as_rx[:, width:])
    ab = {}
    for step in range(chips):
        rows = pl.ds(step * shard, shard)
        asb_tx[step, :, 0:width] = as_f[rows, :].astype(BF16)
        asb_tx[step, :, width:] = split_count(as_cnt[rows, :])
        if step:
            ab[step] = rcopy(asb_tx.at[step], asb_rx.at[step], ab_s.at[step], ab_r.at[step], (chip_dev(step), y))
            ab[step].start()

    lax.fori_loop(tiles // 4, tiles // 2, code_tile, 0)

    for step in range(1, chips):
        wb[step].wait_recv()
    share = wg_f[core, wg_rows(0), :]
    for step in range(1, chips):
        share = share + wgb_rx[step].astype(F32)
    wgc[0] = share
    wc = []
    for at, (peer, slot) in enumerate(((y_right, 3), (y_left, 1), (y_far, 2))):
        wc.append(rcopy(wgc.at[0], wgc.at[slot], wc_s.at[at], wc_r.at[at], (w, peer)))
        wc[-1].start()

    lax.fori_loop(tiles // 2, tiles, code_tile, 0)

    for at in range(3):
        wc[at].wait_recv()

    def share_rows(dev):
        return pl.ds(pl.multiple_of((dev % 2) * wg_own.shape[0] + (dev // 2) * part_rows, part_rows), part_rows)

    wgd[share_rows(w), :] = (wgc[0] + wgc[1] + wgc[2] + wgc[3]).astype(BF16)

    def spread(step, carry):
        rcopy(
            wgd.at[share_rows(w), :], wgd.at[share_rows(w), :], wd_s.at[step], wd_r.at[step], ((w + step) % wide, y)
        ).start()
        return carry

    lax.fori_loop(1, wide, spread, 0)

    lax.fori_loop(0, tiles, ret_tile, 0)

    own_sum = as_f[0:shard, :]
    own_cnt = as_cnt[0:shard, :]
    for step in range(1, chips):
        ab[step].wait_recv()
        own_sum = own_sum + asb_rx[step, :, 0:width].astype(F32)
        own_cnt = own_cnt + join_count(asb_rx[step, :, width:])
    first = (w * narrow + y) * shard
    cnt_row = counts[pl.ds(first // 128, 1), :]
    cnt_col[...] = jnp.transpose(jnp.broadcast_to(cnt_row, (128, 128)))
    if shard <= 128:
        old_cnt = cnt_col[pl.ds(pl.multiple_of(first % 128, shard), shard), :]
    else:
        old_cnt = jnp.concatenate(
            [jnp.transpose(jnp.broadcast_to(counts[pl.ds(first // 128 + b, 1), :], (128, 128))) for b in range(shard // 128)], 0
        )
    scale = 1.0 / (decay_rate * old_cnt + (1.0 - decay_rate) * own_cnt)
    old = sums[pl.ds(pl.multiple_of(first, shard), shard), :]
    for part in range(width // 128):
        lanes = slice(part * 128, part * 128 + 128)
        newcb[:, lanes] = (decay_rate * old[:, lanes] + (1.0 - decay_rate) * own_sum[:, lanes]) * scale

    ret[...] = dot_nt(dz_all[...], ws[...])
    acc[...] = dot(tab_code[:, 0:n], daggg[0:n, :])
    ret[...] += dot(tab_ret[:, 0:n], daggg[0:n, :]) * (1.0 / 8)
    arrived(daggg, d_s, d_r, 2)
    acc[...] += dot(tab_code[:, 3 * n : 4 * n], daggg[3 * n : 4 * n, :])
    ret[...] += dot(tab_ret[:, 3 * n : 4 * n], daggg[3 * n : 4 * n, :]) * (1.0 / 8)
    arrived(daggg, d_s, d_r, 3)
    acc[...] += dot(tab_code[:, n : 2 * n], daggg[n : 2 * n, :])
    ret[...] += dot(tab_ret[:, n : 2 * n], daggg[n : 2 * n, :]) * (1.0 / 8)
    arrived(daggg, d_s, d_r, 4)
    arrived(daggg, d_s, d_r, 5)
    last = daggg[2 * n : 3 * n, :]
    cg_tx[...] = ((acc[own_half:, :] + dot(tab_code[own_half:, 2 * n : 3 * n], last)) * (1.0 / 16)).astype(BF16)
    ca = rcopy(cg_tx, cg_rx, ca_s, ca_r, (other, y))
    ca.start()
    acc[0:own_half, :] = (acc[0:own_half, :] + dot(tab_code[0:own_half, 2 * n : 3 * n], last)) * (1.0 / 16)
    fgrad[...] = (ret[...] + dot(tab_ret[:, 2 * n : 3 * n], last) * (1.0 / 8)).astype(BF16)
    ca.wait_recv()
    cb = {}
    for step in range(1, chips):
        rows = pl.ds(step * shard, shard)
        cgb_tx[step] = (acc[rows, :] + cg_rx[rows, :].astype(F32)).astype(BF16)
        cb[step] = rcopy(cgb_tx.at[step], cgb_rx.at[step], cb_s.at[step], cb_r.at[step], (chip_dev(step), y))
        cb[step].start()

    def gathered(step, carry):
        source = (w + wide - step) % wide
        rcopy(
            wgd.at[share_rows(source), :], wgd.at[share_rows(source), :], wd_s.at[step], wd_r.at[step], (source, y)
        ).wait_recv()
        return carry

    lax.fori_loop(1, wide, gathered, 0)
    wrows = wg_own.shape[0]
    sgrad[...] = wgd[0:wrows, :].astype(F32)
    ngrad[...] = wgd[wrows:, :].astype(F32)

    own = acc[0:shard, :] + cg_rx[0:shard, :].astype(F32)
    for step in range(1, chips):
        cb[step].wait_recv()
        own = own + cgb_rx[step].astype(F32)
    cgrad[...] = own

    for copy in (*f_copies, *d_copies, *i_copies, wa, aa, ca, *wc):
        copy.wait_send()
    for step in range(1, chips):
        wb[step].wait_send()
        ab[step].wait_send()
        cb[step].wait_send()

    def sent(step, carry):
        rcopy(
            wgd.at[share_rows(w), :], wgd.at[share_rows(w), :], wd_s.at[step], wd_r.at[step], ((w + step) % wide, y)
        ).wait_send()
        return carry

    lax.fori_loop(1, wide, sent, 0)


def on_device(
    wide, narrow,
    features, neighbours, code_ids, assignment, cotangent, code_sums, code_counts, self_weight, neighbour_weight,
):
    n, width = features.shape
    codes = code_sums.shape[0]
    chips = wide // 2
    shard = codes // (wide * narrow)
    mine = codes // narrow
    grp = n * narrow
    vm = pl.BlockSpec(memory_space=pltpu.VMEM)
    dma = pltpu.SemaphoreType.DMA
    wide_rows = self_weight.shape[0]
    scratch = [
        pltpu.VMEM((codes, width), F32),
        pltpu.VMEM((codes, width), BF16),
        pltpu.VMEM((grp, width), BF16),
        pltpu.VMEM((grp, width), BF16),
        pltpu.VMEM((narrow, IDX_ROWS, n), I32),
        pltpu.VMEM((n, 128), I32),
        pltpu.VMEM((128, n), I32),
        pltpu.VMEM((n, codes), BF16),
        pltpu.VMEM((n, grp), BF16),
        pltpu.VMEM((mine, grp), BF16),
        pltpu.VMEM((n, grp), BF16),
        pltpu.VMEM((mine, grp), BF16),
        pltpu.VMEM((16, grp), I32),
        pltpu.VMEM((16, grp), I32),
        pltpu.VMEM((8, grp), I32),
        pltpu.VMEM((8, grp), I32),
        pltpu.VMEM((8, grp), I32),
        pltpu.VMEM((n, width), F32),
        pltpu.VMEM((n, width), F32),
        pltpu.VMEM((n, width), F32),
        pltpu.VMEM((n, width), BF16),
        pltpu.VMEM((n, width), BF16),
        pltpu.VMEM((mine, width), F32),
        pltpu.VMEM((n, width), F32),
        pltpu.VMEM((2, wide_rows, width), F32),
        pltpu.VMEM((wide_rows, width), BF16),
        pltpu.VMEM((wide_rows, width), BF16),
        pltpu.VMEM((wide_rows, width), BF16),
        pltpu.VMEM((chips, wide_rows // chips, width), BF16),
        pltpu.VMEM((narrow, wide_rows // chips, width), F32),
        pltpu.VMEM((2 * wide_rows, width), BF16),
        pltpu.VMEM((mine, width), F32),
        pltpu.VMEM((mine, 128), F32),
        pltpu.VMEM((mine // 2, width + 128), BF16),
        pltpu.VMEM((mine // 2, width + 128), BF16),
        pltpu.VMEM((chips, shard, width + 128), BF16),
        pltpu.VMEM((chips, shard, width + 128), BF16),
        pltpu.VMEM((mine // 2, width), BF16),
        pltpu.VMEM((mine // 2, width), BF16),
        pltpu.VMEM((chips, shard, width), BF16),
        pltpu.VMEM((chips, shard, width), BF16),
        pltpu.VMEM((128, 128), F32),
        dma,
        dma((6,)), dma((6,)), dma((6,)), dma((6,)), dma((3,)), dma((3,)),
        dma, dma, dma((chips,)), dma((chips,)), dma((3,)), dma((3,)), dma((wide,)), dma((wide,)),
        dma, dma, dma((chips,)), dma((chips,)), dma, dma, dma((chips,)), dma((chips,)),
    ]
    return pl.pallas_call(
        functools.partial(kernel, wide, narrow, shard),
        out_shape=(
            jax.ShapeDtypeStruct((n, width), BF16),
            jax.ShapeDtypeStruct((n, width), BF16),
            jax.ShapeDtypeStruct(self_weight.shape, F32),
            jax.ShapeDtypeStruct(neighbour_weight.shape, F32),
            jax.ShapeDtypeStruct((shard, width), F32),
            jax.ShapeDtypeStruct((shard, width), F32),
        ),
        in_specs=[vm] * 5 + [pl.BlockSpec(memory_space=pl.ANY)] + [vm] * 3,
        out_specs=(vm,) * 6,
        scratch_shapes=scratch,
        compiler_params=pltpu.CompilerParams(
            collective_id=0, has_side_effects=True, vmem_limit_bytes=58 * 1024 * 1024
        ),
    )(
        features, neighbours.T, code_ids.T, assignment.reshape(1, n), cotangent,
        code_sums, code_counts.reshape(codes // 128, 128), self_weight, neighbour_weight,
    )


def solution(mesh):
    both = ("wide", "narrow")
    return jax.shard_map(
        functools.partial(on_device, mesh.shape["wide"], mesh.shape["narrow"]),
        mesh=mesh,
        in_specs=(P(both, None), P(both, None), P(both, None), P(both), P(both, None), P(), P(), P(), P()),
        out_specs=(P(both, None), P(both, None), P(), P(), P(both, None), P(both, None)),
        check_vma=False,
    )
```

```python
import functools

import jax
import jax.numpy as jnp
from jax import lax
from jax.experimental import pallas as pl
from jax.experimental.pallas import tpu as pltpu
from jax.sharding import PartitionSpec as P

MESH = pl.DeviceIdType.MESH
F32, BF16, I32 = jnp.float32, jnp.bfloat16, jnp.int32
decay_rate = 0.5
IDX_ROWS = 32
NIBBLES = 0x0F0F0F0F


def dot(a, b):
    return jnp.dot(a, b, preferred_element_type=F32)


def dot_nt(a, b):
    return lax.dot_general(a, b, (((1,), (1,)), ((), ())), preferred_element_type=F32)


def dot_tn(a, b):
    return lax.dot_general(a, b, (((0,), (0,)), ((), ())), preferred_element_type=F32)


def words_of(spots, his, vals):
    word = None
    for hi, val in zip(his, vals):
        term = jnp.where(spots == hi, val, 0)
        word = term if word is None else word + term
    return word


def fields_of(words):
    even = odd = None
    for word in words:
        low, high = word & NIBBLES, (word >> 4) & NIBBLES
        even = low if even is None else even + low
        odd = high if odd is None else odd + high
    out = []
    for field in range(8):
        part = (even, odd)[field % 2]
        shift = 8 * (field // 2)
        if shift:
            part = part >> shift
        if shift < 24:
            part = part & 255
        out.append(part.astype(F32).astype(BF16))
    return out


def kernel(
    wide, narrow, shard,
    feat_hbm, nb_hbm, code_hbm, assign_hbm, cot_hbm, sums_hbm, counts_hbm, ws_hbm, wn_hbm,
    out_hbm, fgrad_hbm, sgrad_hbm, ngrad_hbm, newcb_hbm, cgrad_hbm,
    cot, sums, counts, ws, wn, out, fgrad, wgrads, newcb, cgrad,
    codebook, featg, daggg, idxg, tab_far, tab_near, tab_code, tab_ret, tab_asn,
    hi_f, val_f, hi_n, val_n, hi_t, val_t, hi_r, val_r, row_a, far, near, hid, dz_all, agg_all, acc, ret,
    wg_f, wg_tx, wg_rx, wgb_tx, wgb_rx, wgc, wgd, as_f, as_cnt, as_acc, as_tx, as_rx, asb_tx, asb_rx,
    cg_tx, cg_rx, cgb_tx, cgb_rx, cnt_col,
    in_sem, out_sem, f_s, f_r, d_s, d_r, i_s, i_r, wa_s, wa_r, wb_s, wb_r, wc_s, wc_r, wd_s, wd_r,
    aa_s, aa_r, ab_s, ab_r, ca_s, ca_r, cb_s, cb_r,
):
    n = cot.shape[0]
    half = n // 2
    chips = wide // 2
    codes = sums.shape[0]
    mine = codes // narrow
    own_half = mine // 2
    grp = n * narrow
    w = lax.axis_index("wide")
    y = lax.axis_index("narrow")
    core = w % 2
    chip = w // 2
    y_right, y_left, y_far = (y + 1) % narrow, (y + 3) % narrow, (y + 2) % narrow
    other = chip * 2 + (1 - core)

    def chip_dev(step):
        return ((chip + step) % chips) * 2 + core

    def rcopy(src, dst, ssem, rsem, dev):
        return pltpu.make_async_remote_copy(
            src_ref=src, dst_ref=dst, send_sem=ssem, recv_sem=rsem, device_id=dev, device_id_type=MESH
        )

    feat = featg.at[pl.ds(0, n), :]
    idxg[0, 24:32, :] = jnp.zeros((8, n), I32)
    fetched = [
        pltpu.make_async_copy(src, dst, in_sem.at[at])
        for at, (src, dst) in enumerate(
            (
                (feat_hbm, feat),
                (nb_hbm, idxg.at[0, pl.ds(0, 8), :]),
                (code_hbm, idxg.at[0, pl.ds(8, 16), :]),
                (assign_hbm, idxg.at[0, pl.ds(24, 1), :]),
                (counts_hbm, counts),
                (sums_hbm, sums),
                (ws_hbm, ws),
                (wn_hbm, wn),
                (cot_hbm, cot),
            )
        )
    ]
    for copy in fetched:
        copy.start()

    barrier = pltpu.get_barrier_semaphore()
    for peer in (y_right, y_left, y_far):
        pl.semaphore_signal(barrier, inc=1, device_id=(w, peer), device_id_type=MESH)

    def greet(step, carry):
        pl.semaphore_signal(barrier, inc=1, device_id=((w + step) % wide, y), device_id_type=MESH)
        return carry

    lax.fori_loop(1, wide, greet, 0)
    for at in range(4):
        fetched[at].wait()
    pl.semaphore_wait(barrier, narrow - 1 + wide - 1)

    def low(slot):
        return pl.ds(slot * n, half)

    def high(slot):
        return pl.ds(slot * n + half, half)

    def gather_copies(buf, ssem, rsem):
        right, left = (w, y_right), (w, y_left)

        def make(src, dst, at, dev):
            return rcopy(buf.at[src, :], buf.at[dst, :], ssem.at[at], rsem.at[at], dev)

        return (
            make(low(0), low(3), 0, right),
            make(high(0), high(1), 1, left),
            make(high(0), high(3), 2, right),
            make(low(0), low(1), 3, left),
            make(low(3), low(2), 4, right),
            make(high(1), high(2), 5, left),
        )

    def arrived(buf, ssem, rsem, at):
        region = (low(3), high(1), high(3), low(1), low(2), high(2))[at]
        rcopy(buf.at[region, :], buf.at[region, :], ssem.at[at], rsem.at[at], (w, y_right)).wait_recv()

    f_copies = gather_copies(featg, f_s, f_r)
    for at in range(4):
        f_copies[at].start()
    i_copies = []
    for at, (peer, slot) in enumerate(((y_right, 3), (y_left, 1), (y_far, 2))):
        i_copies.append(rcopy(idxg.at[0], idxg.at[slot], i_s.at[at], i_r.at[at], (w, peer)))
        i_copies[-1].start()

    def table(tab, his_ref, vals_ref, spots_in, lane_at, first_spot):
        lanes = pl.ds(pl.multiple_of(lane_at, 128), 128)
        picks = his_ref.shape[0]
        his = [jnp.broadcast_to(his_ref[j : j + 1, lanes], (16, 128)) for j in range(picks)]
        vals = [jnp.broadcast_to(vals_ref[j : j + 1, lanes], (16, 128)) for j in range(picks)]
        base = lax.broadcasted_iota(I32, (16, 128), 0) + first_spot
        for part in range(min(spots_in, 128) // 16):
            spots = base + part * 16
            words = [words_of(spots, his[at : at + 8], vals[at : at + 8]) for at in range(0, picks, 8)]
            for field, counts_part in enumerate(fields_of(words)):
                row = pl.multiple_of(field * spots_in + part * 16 + first_spot, 16)
                tab[pl.ds(row, 16), lanes] = counts_part

    far_spots = codes // 8
    far_bits = far_spots.bit_length() - 1
    near_spots = grp // 8
    near_bits = near_spots.bit_length() - 1
    node_bits = n.bit_length() - 1
    own_ids = idxg[0, 8:24, :]
    hi_f[...] = own_ids & (far_spots - 1)
    val_f[...] = jnp.int32(1) << ((own_ids >> far_bits) * 4)
    own_ids = idxg[0, 0:8, :]
    own_ids = ((((own_ids >> node_bits) - y) & (narrow - 1)) << node_bits) | (own_ids & (n - 1))
    hi_n[...] = own_ids & (near_spots - 1)
    val_n[...] = jnp.int32(1) << ((own_ids >> near_bits) * 4)

    def far_tile(tile, carry):
        table(tab_far, hi_f, val_f, far_spots, (tile // (far_spots // 128)) * 128, (tile % (far_spots // 128)) * 128)
        return carry

    def near_tile(tile, carry):
        table(tab_near, hi_n, val_n, near_spots, (tile // (near_spots // 128)) * 128, (tile % (near_spots // 128)) * 128)
        return carry

    far_tiles = (n // 128) * (far_spots // 128)
    lax.fori_loop(0, far_tiles // 2, far_tile, 0)
    arrived(featg, f_s, f_r, 0)
    f_copies[4].start()
    arrived(featg, f_s, f_r, 1)
    f_copies[5].start()
    lax.fori_loop(far_tiles // 2, far_tiles, far_tile, 0)
    width = sums.shape[1]
    for at in range(4, 9):
        fetched[at].wait()
    blocks = codes // 128
    inverse = jnp.transpose(jnp.concatenate([1.0 / counts[...]] * (128 // blocks), 0))
    for block in range(blocks):
        column = jnp.broadcast_to(inverse[:, block : block + 1], (128, 128))
        for part in range(width // 128):
            at = (slice(block * 128, block * 128 + 128), slice(part * 128, part * 128 + 128))
            codebook[at] = (sums[at] * column).astype(BF16)
    far[...] = dot_tn(tab_far[...], codebook[...]) * (1.0 / 16)
    lax.fori_loop(0, (n // 128) * (near_spots // 128), near_tile, 0)
    hid[...] = dot(feat[...], ws[...])
    near[...] = dot_tn(tab_near[0:n, :], feat[...])
    arrived(featg, f_s, f_r, 2)
    near[...] += dot_tn(tab_near[3 * n : 4 * n, :], featg[3 * n : 4 * n, :])
    arrived(featg, f_s, f_r, 3)
    near[...] += dot_tn(tab_near[n : 2 * n, :], featg[n : 2 * n, :])
    arrived(featg, f_s, f_r, 4)
    arrived(featg, f_s, f_r, 5)

    d_copies = gather_copies(daggg, d_s, d_r)
    for at in range(2):
        rows = pl.ds(at * half, half)
        total = near[rows, :] + dot_tn(tab_near[2 * n : 3 * n, at * half : at * half + half], featg[2 * n : 3 * n, :])
        agg = (total * (1.0 / 8) + far[rows, :]).astype(BF16)
        agg_all[rows, :] = agg
        z = hid[rows, :] + dot(agg, wn[...])
        s = jax.nn.sigmoid(z)
        out[rows, :] = (z * s).astype(BF16)
        dz = (cot[rows, :].astype(F32) * s * (1.0 + z * (1.0 - s))).astype(BF16)
        dz_all[rows, :] = dz
        daggg[rows, :] = dot_nt(dz, wn[...]).astype(BF16)
        d_copies[(0, 1)[at]].start()
        d_copies[(3, 2)[at]].start()
    written = [
        pltpu.make_async_copy(src, dst, out_sem.at[at])
        for at, (src, dst) in enumerate(
            (
                (out, out_hbm), (fgrad, fgrad_hbm), (wgrads.at[0], sgrad_hbm),
                (wgrads.at[1], ngrad_hbm), (newcb, newcb_hbm), (cgrad, cgrad_hbm),
            )
        )
    ]
    written[0].start()

    def weight_half(which, x):
        wg_f[which] = dot_tn(x, dz_all[...])

    weight_half(0, feat[...])
    weight_half(1, agg_all[...])
    wg_tx[...] = wg_f[1 - core].astype(BF16)
    wa = rcopy(wg_tx, wg_rx, wa_s, wa_r, (other, y))
    wa.start()

    for at in range(3):
        i_copies[at].wait_recv()
    shard_bits = shard.bit_length() - 1
    narrow_bits = narrow.bit_length() - 1
    mine_spots = mine // 8
    mine_bits = mine_spots.bit_length() - 1
    ret_spots = n // 8
    ret_bits = ret_spots.bit_length() - 1

    def place(k):
        kw = k >> (shard_bits + narrow_bits)
        row = ((((kw & 1) ^ core) * chips + (((kw >> 1) - chip) & (chips - 1))) << shard_bits) | (k & (shard - 1))
        return row, ((k >> shard_bits) & (narrow - 1)) == y

    for slot in range(narrow):
        lanes = pl.ds(slot * n, n)
        ids = idxg[slot, 0:8, :]
        hi_r[:, lanes] = ids & (ret_spots - 1)
        local = ids & (n - 1)
        val_r[:, lanes] = jnp.where((ids >> node_bits) == y, jnp.int32(1) << ((local >> ret_bits) * 4), 0)
        row, hit = place(idxg[slot, 8:24, :])
        hi_t[:, lanes] = row & (mine_spots - 1)
        val_t[:, lanes] = jnp.where(hit, jnp.int32(1) << ((row >> mine_bits) * 4), 0)
        row, hit = place(idxg[slot, 24:32, :])
        row_a[:, lanes] = jnp.where(hit, row, -1)

    def asn_part(part, carry):
        rows = pl.ds(pl.multiple_of(part * 16, 16), 16)
        spots = lax.broadcasted_iota(I32, (16, 128), 0) + part * 16
        total = None
        for tile in range(grp // 128):
            lanes = slice(tile * 128, tile * 128 + 128)
            hit = jnp.where(jnp.broadcast_to(row_a[0:1, lanes], (16, 128)) == spots, 1.0, 0.0)
            tab_asn[rows, lanes] = hit.astype(BF16)
            total = hit if total is None else total + hit
        as_acc[rows, :] = total.astype(BF16)
        return carry

    def code_tile(tile, carry):
        table(tab_code, hi_t, val_t, mine_spots, tile * 128, 0)
        return carry

    def ret_tile(tile, carry):
        table(tab_ret, hi_r, val_r, ret_spots, tile * 128, 0)
        return carry

    def split_count(count):
        big = jnp.floor(count * (1.0 / 256)) * 256.0
        lane = lax.broadcasted_iota(I32, count.shape, 1)
        return jnp.where(lane < 64, big, count - big).astype(BF16)

    def join_count(pair):
        pair = pair.astype(F32)
        return pair + pltpu.roll(pair, 64, 1)

    lax.fori_loop(0, mine // 16, asn_part, 0)
    as_f[...] = dot(tab_asn[...], featg[...])
    as_cnt[...] = dot(as_acc[...], jnp.ones((128, 128), BF16))
    as_tx[:, 0:width] = as_f[own_half:, :].astype(BF16)
    as_tx[:, width:] = split_count(as_cnt[own_half:, :])
    aa = rcopy(as_tx, as_rx, aa_s, aa_r, (other, y))
    aa.start()

    tiles = grp // 128
    lax.fori_loop(0, tiles // 4, code_tile, 0)

    arrived(daggg, d_s, d_r, 0)
    d_copies[4].start()
    arrived(daggg, d_s, d_r, 1)
    d_copies[5].start()

    wa.wait_recv()
    wg_own = wg_f[core] + wg_rx[...].astype(F32)
    wg_f[core] = wg_own
    wgb_tx[...] = wg_own.astype(BF16)
    part_rows = wg_own.shape[0] // chips

    def wg_rows(step):
        return pl.ds(pl.multiple_of(((chip + step) % chips) * part_rows, part_rows), part_rows)

    wb = {}
    for step in range(1, chips):
        wb[step] = rcopy(
            wgb_tx.at[wg_rows(step), :], wgb_rx.at[step], wb_s.at[step], wb_r.at[step], (chip_dev(step), y)
        )
        wb[step].start()

    aa.wait_recv()
    as_f[0:own_half, :] += as_rx[:, 0:width].astype(F32)
    as_cnt[0:own_half, :] += join_count(as_rx[:, width:])
    ab = {}
    for step in range(chips):
        rows = pl.ds(step * shard, shard)
        asb_tx[step, :, 0:width] = as_f[rows, :].astype(BF16)
        asb_tx[step, :, width:] = split_count(as_cnt[rows, :])
        if step:
            ab[step] = rcopy(asb_tx.at[step], asb_rx.at[step], ab_s.at[step], ab_r.at[step], (chip_dev(step), y))
            ab[step].start()

    lax.fori_loop(tiles // 4, tiles // 2, code_tile, 0)

    for step in range(1, chips):
        wb[step].wait_recv()
    share = wg_f[core, wg_rows(0), :]
    for step in range(1, chips):
        share = share + wgb_rx[step].astype(F32)
    wgc[0] = share
    wc = []
    for at, (peer, slot) in enumerate(((y_right, 3), (y_left, 1), (y_far, 2))):
        wc.append(rcopy(wgc.at[0], wgc.at[slot], wc_s.at[at], wc_r.at[at], (w, peer)))
        wc[-1].start()

    lax.fori_loop(tiles // 2, tiles, code_tile, 0)

    for at in range(3):
        wc[at].wait_recv()

    def share_rows(dev):
        return pl.ds(pl.multiple_of((dev % 2) * wg_own.shape[0] + (dev // 2) * part_rows, part_rows), part_rows)

    wgd[share_rows(w), :] = (wgc[0] + wgc[1] + wgc[2] + wgc[3]).astype(BF16)

    def spread(step, carry):
        rcopy(
            wgd.at[share_rows(w), :], wgd.at[share_rows(w), :], wd_s.at[step], wd_r.at[step], ((w + step) % wide, y)
        ).start()
        return carry

    lax.fori_loop(1, wide, spread, 0)

    lax.fori_loop(0, tiles, ret_tile, 0)

    own_sum = as_f[0:shard, :]
    own_cnt = as_cnt[0:shard, :]
    for step in range(1, chips):
        ab[step].wait_recv()
        own_sum = own_sum + asb_rx[step, :, 0:width].astype(F32)
        own_cnt = own_cnt + join_count(asb_rx[step, :, width:])
    first = (w * narrow + y) * shard
    cnt_row = counts[pl.ds(first // 128, 1), :]
    cnt_col[...] = jnp.transpose(jnp.broadcast_to(cnt_row, (128, 128)))
    if shard <= 128:
        old_cnt = cnt_col[pl.ds(pl.multiple_of(first % 128, shard), shard), :]
    else:
        old_cnt = jnp.concatenate(
            [jnp.transpose(jnp.broadcast_to(counts[pl.ds(first // 128 + b, 1), :], (128, 128))) for b in range(shard // 128)], 0
        )
    scale = 1.0 / (decay_rate * old_cnt + (1.0 - decay_rate) * own_cnt)
    old = sums[pl.ds(pl.multiple_of(first, shard), shard), :]
    for part in range(width // 128):
        lanes = slice(part * 128, part * 128 + 128)
        newcb[:, lanes] = (decay_rate * old[:, lanes] + (1.0 - decay_rate) * own_sum[:, lanes]) * scale
    written[4].start()

    ret[...] = dot_nt(dz_all[...], ws[...])
    acc[...] = dot(tab_code[:, 0:n], daggg[0:n, :])
    ret[...] += dot(tab_ret[:, 0:n], daggg[0:n, :]) * (1.0 / 8)
    arrived(daggg, d_s, d_r, 2)
    acc[...] += dot(tab_code[:, 3 * n : 4 * n], daggg[3 * n : 4 * n, :])
    ret[...] += dot(tab_ret[:, 3 * n : 4 * n], daggg[3 * n : 4 * n, :]) * (1.0 / 8)
    arrived(daggg, d_s, d_r, 3)
    acc[...] += dot(tab_code[:, n : 2 * n], daggg[n : 2 * n, :])
    ret[...] += dot(tab_ret[:, n : 2 * n], daggg[n : 2 * n, :]) * (1.0 / 8)
    arrived(daggg, d_s, d_r, 4)
    arrived(daggg, d_s, d_r, 5)
    last = daggg[2 * n : 3 * n, :]
    cg_tx[...] = ((acc[own_half:, :] + dot(tab_code[own_half:, 2 * n : 3 * n], last)) * (1.0 / 16)).astype(BF16)
    ca = rcopy(cg_tx, cg_rx, ca_s, ca_r, (other, y))
    ca.start()
    acc[0:own_half, :] = (acc[0:own_half, :] + dot(tab_code[0:own_half, 2 * n : 3 * n], last)) * (1.0 / 16)
    fgrad[...] = (ret[...] + dot(tab_ret[:, 2 * n : 3 * n], last) * (1.0 / 8)).astype(BF16)
    written[1].start()
    ca.wait_recv()
    cb = {}
    for step in range(1, chips):
        rows = pl.ds(step * shard, shard)
        cgb_tx[step] = (acc[rows, :] + cg_rx[rows, :].astype(F32)).astype(BF16)
        cb[step] = rcopy(cgb_tx.at[step], cgb_rx.at[step], cb_s.at[step], cb_r.at[step], (chip_dev(step), y))
        cb[step].start()

    def gathered(step, carry):
        source = (w + wide - step) % wide
        rcopy(
            wgd.at[share_rows(source), :], wgd.at[share_rows(source), :], wd_s.at[step], wd_r.at[step], (source, y)
        ).wait_recv()
        return carry

    lax.fori_loop(1, wide, gathered, 0)
    wrows = wg_own.shape[0]
    wgrads[0] = wgd[0:wrows, :].astype(F32)
    wgrads[1] = wgd[wrows:, :].astype(F32)
    written[2].start()
    written[3].start()

    own = acc[0:shard, :] + cg_rx[0:shard, :].astype(F32)
    for step in range(1, chips):
        cb[step].wait_recv()
        own = own + cgb_rx[step].astype(F32)
    cgrad[...] = own
    written[5].start()

    for copy in (*f_copies, *d_copies, *i_copies, wa, aa, ca, *wc):
        copy.wait_send()
    for step in range(1, chips):
        wb[step].wait_send()
        ab[step].wait_send()
        cb[step].wait_send()

    def sent(step, carry):
        rcopy(
            wgd.at[share_rows(w), :], wgd.at[share_rows(w), :], wd_s.at[step], wd_r.at[step], ((w + step) % wide, y)
        ).wait_send()
        return carry

    lax.fori_loop(1, wide, sent, 0)
    for copy in written:
        copy.wait()


def copy_kernel(*refs):
    count = len(refs) // 2
    copies = [pltpu.make_async_copy(refs[at], refs[count + at], refs[-1].at[at]) for at in range(count)]
    for copy in copies:
        copy.start()
    for copy in copies:
        copy.wait()


def on_device(
    wide, narrow,
    features, neighbours, code_ids, assignment, cotangent, code_sums, code_counts, self_weight, neighbour_weight,
):
    n, width = features.shape
    codes = code_sums.shape[0]
    chips = wide // 2
    shard = codes // (wide * narrow)
    mine = codes // narrow
    grp = n * narrow
    hbm = pl.BlockSpec(memory_space=pl.ANY)
    dma = pltpu.SemaphoreType.DMA
    wide_rows = self_weight.shape[0]
    scratch = [
        pltpu.VMEM((n, width), BF16),
        pltpu.VMEM((codes, width), F32),
        pltpu.VMEM((codes // 128, 128), F32),
        pltpu.VMEM(self_weight.shape, BF16),
        pltpu.VMEM(neighbour_weight.shape, BF16),
        pltpu.VMEM((n, width), BF16),
        pltpu.VMEM((n, width), BF16),
        pltpu.VMEM((2, *self_weight.shape), F32),
        pltpu.VMEM((shard, width), F32),
        pltpu.VMEM((shard, width), F32),
        pltpu.VMEM((codes, width), BF16),
        pltpu.VMEM((grp, width), BF16),
        pltpu.VMEM((grp, width), BF16),
        pltpu.VMEM((narrow, IDX_ROWS, n), I32),
        pltpu.VMEM((codes, n), BF16),
        pltpu.VMEM((grp, n), BF16),
        pltpu.VMEM((mine, grp), BF16),
        pltpu.VMEM((n, grp), BF16),
        pltpu.VMEM((mine, grp), BF16),
        pltpu.VMEM((16, n), I32),
        pltpu.VMEM((16, n), I32),
        pltpu.VMEM((8, n), I32),
        pltpu.VMEM((8, n), I32),
        pltpu.VMEM((16, grp), I32),
        pltpu.VMEM((16, grp), I32),
        pltpu.VMEM((8, grp), I32),
        pltpu.VMEM((8, grp), I32),
        pltpu.VMEM((8, grp), I32),
        pltpu.VMEM((n, width), F32),
        pltpu.VMEM((n, width), F32),
        pltpu.VMEM((n, width), F32),
        pltpu.VMEM((n, width), BF16),
        pltpu.VMEM((n, width), BF16),
        pltpu.VMEM((mine, width), F32),
        pltpu.VMEM((n, width), F32),
        pltpu.VMEM((2, wide_rows, width), F32),
        pltpu.VMEM((wide_rows, width), BF16),
        pltpu.VMEM((wide_rows, width), BF16),
        pltpu.VMEM((wide_rows, width), BF16),
        pltpu.VMEM((chips, wide_rows // chips, width), BF16),
        pltpu.VMEM((narrow, wide_rows // chips, width), F32),
        pltpu.VMEM((2 * wide_rows, width), BF16),
        pltpu.VMEM((mine, width), F32),
        pltpu.VMEM((mine, 128), F32),
        pltpu.VMEM((mine, 128), BF16),
        pltpu.VMEM((mine // 2, width + 128), BF16),
        pltpu.VMEM((mine // 2, width + 128), BF16),
        pltpu.VMEM((chips, shard, width + 128), BF16),
        pltpu.VMEM((chips, shard, width + 128), BF16),
        pltpu.VMEM((mine // 2, width), BF16),
        pltpu.VMEM((mine // 2, width), BF16),
        pltpu.VMEM((chips, shard, width), BF16),
        pltpu.VMEM((chips, shard, width), BF16),
        pltpu.VMEM((128, 128), F32),
        dma((9,)), dma((6,)),
        dma((6,)), dma((6,)), dma((6,)), dma((6,)), dma((3,)), dma((3,)),
        dma, dma, dma((chips,)), dma((chips,)), dma((3,)), dma((3,)), dma((wide,)), dma((wide,)),
        dma, dma, dma((chips,)), dma((chips,)), dma, dma, dma((chips,)), dma((chips,)),
    ]
    shapes = (
        jax.ShapeDtypeStruct((n, width), BF16),
        jax.ShapeDtypeStruct((n, width), BF16),
        jax.ShapeDtypeStruct(self_weight.shape, F32),
        jax.ShapeDtypeStruct(neighbour_weight.shape, F32),
        jax.ShapeDtypeStruct((shard, width), F32),
        jax.ShapeDtypeStruct((shard, width), F32),
    )
    results = pl.pallas_call(
        functools.partial(kernel, wide, narrow, shard),
        out_shape=shapes,
        in_specs=[hbm] * 9,
        out_specs=(hbm,) * 6,
        scratch_shapes=scratch,
        compiler_params=pltpu.CompilerParams(
            collective_id=0, has_side_effects=True, vmem_limit_bytes=58 * 1024 * 1024
        ),
    )(
        features, neighbours.T, code_ids.T, assignment.reshape(1, n), cotangent,
        code_sums, code_counts.reshape(codes // 128, 128), self_weight, neighbour_weight,
    )
    return pl.pallas_call(
        copy_kernel,
        out_shape=shapes,
        in_specs=[hbm] * 6,
        out_specs=(hbm,) * 6,
        scratch_shapes=[dma((6,))],
        compiler_params=pltpu.CompilerParams(vmem_limit_bytes=62 * 1024 * 1024),
    )(*results)


def solution(mesh):
    both = ("wide", "narrow")
    return jax.shard_map(
        functools.partial(on_device, mesh.shape["wide"], mesh.shape["narrow"]),
        mesh=mesh,
        in_specs=(P(both, None), P(both, None), P(both, None), P(both), P(both, None), P(), P(), P(), P()),
        out_specs=(P(both, None), P(both, None), P(), P(), P(both, None), P(both, None)),
        check_vma=False,
    )
```

```python
import functools

import jax
import jax.numpy as jnp
from jax import lax
from jax.experimental import pallas as pl
from jax.experimental.pallas import tpu as pltpu
from jax.sharding import PartitionSpec as P

MESH = pl.DeviceIdType.MESH
F32, BF16, I32 = jnp.float32, jnp.bfloat16, jnp.int32
decay_rate = 0.5
IDX_ROWS = 32
NIBBLES = 0x0F0F0F0F


def dot(a, b):
    return jnp.dot(a, b, preferred_element_type=F32)


def dot_nt(a, b):
    return lax.dot_general(a, b, (((1,), (1,)), ((), ())), preferred_element_type=F32)


def dot_tn(a, b):
    return lax.dot_general(a, b, (((0,), (0,)), ((), ())), preferred_element_type=F32)


def words_of(spots, his, vals):
    word = None
    for hi, val in zip(his, vals):
        term = jnp.where(spots == hi, val, 0)
        word = term if word is None else word + term
    return word


def fields_of(words):
    even = odd = None
    for word in words:
        low, high = word & NIBBLES, (word >> 4) & NIBBLES
        even = low if even is None else even + low
        odd = high if odd is None else odd + high
    out = []
    for field in range(8):
        part = (even, odd)[field % 2]
        shift = 8 * (field // 2)
        if shift:
            part = part >> shift
        if shift < 24:
            part = part & 255
        out.append(part.astype(F32).astype(BF16))
    return out


def kernel(
    wide, narrow, shard,
    feat_hbm, nb_hbm, code_hbm, assign_hbm, cot_hbm, sums_hbm, counts_hbm, ws_hbm, wn_hbm,
    out, fgrad, sgrad, ngrad, newcb, cgrad,
    cot, sums, counts, ws, wn,
    codebook, featg, daggg, idx_own, idxg, tab_far, tab_near, tab_code, tab_ret, tab_asn,
    hi_f, val_f, hi_n, val_n, hi_t, val_t, hi_r, val_r, row_a, far, near, hid, dz_all, agg_all, acc, ret,
    wg_f, wg_tx, wg_rx, wgb_tx, wgb_rx, wgc, wgd, as_f, as_cnt, as_acc, as_tx, as_rx, asb_tx, asb_rx,
    cg_tx, cg_rx, cgb_tx, cgb_rx, cnt_col,
    in_sem, f_s, f_r, d_s, d_r, i_s, i_r, wa_s, wa_r, wb_s, wb_r, wc_s, wc_r, wd_s, wd_r,
    aa_s, aa_r, ab_s, ab_r, ca_s, ca_r, cb_s, cb_r,
):
    n = cot.shape[0]
    half = n // 2
    chips = wide // 2
    codes = sums.shape[0]
    mine = codes // narrow
    own_half = mine // 2
    grp = n * narrow
    w = lax.axis_index("wide")
    y = lax.axis_index("narrow")
    core = w % 2
    chip = w // 2
    y_right, y_left, y_far = (y + 1) % narrow, (y + 3) % narrow, (y + 2) % narrow
    other = chip * 2 + (1 - core)

    def chip_dev(step):
        return ((chip + step) % chips) * 2 + core

    def rcopy(src, dst, ssem, rsem, dev):
        return pltpu.make_async_remote_copy(
            src_ref=src, dst_ref=dst, send_sem=ssem, recv_sem=rsem, device_id=dev, device_id_type=MESH
        )

    feat = featg.at[pl.ds(0, n), :]
    idx_own[24:32, :] = jnp.zeros((8, n), I32)
    fetched = [
        pltpu.make_async_copy(src, dst, in_sem.at[at])
        for at, (src, dst) in enumerate(
            (
                (feat_hbm, feat),
                (nb_hbm, idx_own.at[pl.ds(0, 8), :]),
                (code_hbm, idx_own.at[pl.ds(8, 16), :]),
                (assign_hbm, idx_own.at[pl.ds(24, 1), :]),
                (counts_hbm, counts),
                (sums_hbm, sums),
                (ws_hbm, ws),
                (wn_hbm, wn),
                (cot_hbm, cot),
            )
        )
    ]
    for copy in fetched:
        copy.start()

    barrier = pltpu.get_barrier_semaphore()
    for peer in (y_right, y_left, y_far):
        pl.semaphore_signal(barrier, inc=1, device_id=(w, peer), device_id_type=MESH)

    def greet(step, carry):
        pl.semaphore_signal(barrier, inc=1, device_id=((w + step) % wide, y), device_id_type=MESH)
        return carry

    lax.fori_loop(1, wide, greet, 0)
    for at in range(4):
        fetched[at].wait()
    pl.semaphore_wait(barrier, narrow - 1 + wide - 1)

    def low(slot):
        return pl.ds(slot * n, half)

    def high(slot):
        return pl.ds(slot * n + half, half)

    def gather_copies(buf, ssem, rsem):
        right, left = (w, y_right), (w, y_left)

        def make(src, dst, at, dev):
            return rcopy(buf.at[src, :], buf.at[dst, :], ssem.at[at], rsem.at[at], dev)

        return (
            make(low(0), low(3), 0, right),
            make(high(0), high(1), 1, left),
            make(high(0), high(3), 2, right),
            make(low(0), low(1), 3, left),
            make(low(3), low(2), 4, right),
            make(high(1), high(2), 5, left),
        )

    def arrived(buf, ssem, rsem, at):
        region = (low(3), high(1), high(3), low(1), low(2), high(2))[at]
        rcopy(buf.at[region, :], buf.at[region, :], ssem.at[at], rsem.at[at], (w, y_right)).wait_recv()

    f_copies = gather_copies(featg, f_s, f_r)
    for at in range(4):
        f_copies[at].start()
    idxg[0] = idx_own[...].astype(jnp.int16)
    i_copies = [
        rcopy(idxg.at[0], idxg.at[slot], i_s.at[at], i_r.at[at], (w, peer))
        for at, (peer, slot) in enumerate(((y_right, 3), (y_left, 1), (y_far, 2)))
    ]

    def table(tab, his_ref, vals_ref, spots_in, lane_at, first_spot):
        lanes = pl.ds(pl.multiple_of(lane_at, 128), 128)
        picks = his_ref.shape[0]
        his = [jnp.broadcast_to(his_ref[j : j + 1, lanes], (16, 128)) for j in range(picks)]
        vals = [jnp.broadcast_to(vals_ref[j : j + 1, lanes], (16, 128)) for j in range(picks)]
        base = lax.broadcasted_iota(I32, (16, 128), 0) + first_spot
        for part in range(min(spots_in, 128) // 16):
            spots = base + part * 16
            words = [words_of(spots, his[at : at + 8], vals[at : at + 8]) for at in range(0, picks, 8)]
            for field, counts_part in enumerate(fields_of(words)):
                row = pl.multiple_of(field * spots_in + part * 16 + first_spot, 16)
                tab[pl.ds(row, 16), lanes] = counts_part

    far_spots = codes // 8
    far_bits = far_spots.bit_length() - 1
    near_spots = grp // 8
    near_bits = near_spots.bit_length() - 1
    node_bits = n.bit_length() - 1
    own_ids = idx_own[8:24, :]
    hi_f[...] = own_ids & (far_spots - 1)
    val_f[...] = jnp.int32(1) << ((own_ids >> far_bits) * 4)
    own_ids = idx_own[0:8, :]
    own_ids = ((((own_ids >> node_bits) - y) & (narrow - 1)) << node_bits) | (own_ids & (n - 1))
    hi_n[...] = own_ids & (near_spots - 1)
    val_n[...] = jnp.int32(1) << ((own_ids >> near_bits) * 4)

    def far_tile(tile, carry):
        table(tab_far, hi_f, val_f, far_spots, (tile // (far_spots // 128)) * 128, (tile % (far_spots // 128)) * 128)
        return carry

    def near_tile(tile, carry):
        table(tab_near, hi_n, val_n, near_spots, (tile // (near_spots // 128)) * 128, (tile % (near_spots // 128)) * 128)
        return carry

    far_tiles = (n // 128) * (far_spots // 128)
    lax.fori_loop(0, far_tiles // 2, far_tile, 0)
    arrived(featg, f_s, f_r, 0)
    f_copies[4].start()
    arrived(featg, f_s, f_r, 1)
    f_copies[5].start()
    for copy in i_copies:
        copy.start()
    lax.fori_loop(far_tiles // 2, far_tiles, far_tile, 0)
    width = sums.shape[1]
    for at in range(4, 9):
        fetched[at].wait()
    blocks = codes // 128
    inverse = jnp.transpose(jnp.concatenate([1.0 / counts[...]] * (128 // blocks), 0))
    for block in range(blocks):
        column = jnp.broadcast_to(inverse[:, block : block + 1], (128, 128))
        for part in range(width // 128):
            at = (slice(block * 128, block * 128 + 128), slice(part * 128, part * 128 + 128))
            codebook[at] = (sums[at] * column).astype(BF16)
    far[...] = jnp.zeros_like(far)
    near_tiles = (n // 128) * (near_spots // 128)
    step_codes = codes // near_tiles

    def near_step(tile, carry):
        near_tile(tile, 0)
        rows = pl.ds(pl.multiple_of(tile * step_codes, step_codes), step_codes)
        far[...] += dot_tn(tab_far[rows, :], codebook[rows, :])
        return carry

    lax.fori_loop(0, near_tiles, near_step, 0)
    hid[...] = dot(feat[...], ws[...])
    near[...] = dot_tn(tab_near[0:n, :], feat[...])
    arrived(featg, f_s, f_r, 2)
    near[...] += dot_tn(tab_near[3 * n : 4 * n, :], featg[3 * n : 4 * n, :])
    arrived(featg, f_s, f_r, 3)
    near[...] += dot_tn(tab_near[n : 2 * n, :], featg[n : 2 * n, :])
    arrived(featg, f_s, f_r, 4)
    arrived(featg, f_s, f_r, 5)

    d_copies = gather_copies(daggg, d_s, d_r)
    for at in range(2):
        rows = pl.ds(at * half, half)
        total = near[rows, :] + dot_tn(tab_near[2 * n : 3 * n, at * half : at * half + half], featg[2 * n : 3 * n, :])
        agg = (total * (1.0 / 8) + far[rows, :] * (1.0 / 16)).astype(BF16)
        agg_all[rows, :] = agg
        z = hid[rows, :] + dot(agg, wn[...])
        s = jax.nn.sigmoid(z)
        out[rows, :] = (z * s).astype(BF16)
        dz = (cot[rows, :].astype(F32) * s * (1.0 + z * (1.0 - s))).astype(BF16)
        dz_all[rows, :] = dz
        daggg[rows, :] = dot_nt(dz, wn[...]).astype(BF16)
        d_copies[(0, 1)[at]].start()
        d_copies[(3, 2)[at]].start()

    def weight_half(which, x):
        wg_f[which] = dot_tn(x, dz_all[...])

    weight_half(0, feat[...])
    weight_half(1, agg_all[...])
    wg_tx[...] = wg_f[1 - core].astype(BF16)
    wa = rcopy(wg_tx, wg_rx, wa_s, wa_r, (other, y))
    wa.start()

    for at in range(3):
        i_copies[at].wait_recv()
    shard_bits = shard.bit_length() - 1
    narrow_bits = narrow.bit_length() - 1
    mine_spots = mine // 8
    mine_bits = mine_spots.bit_length() - 1
    ret_spots = n // 8
    ret_bits = ret_spots.bit_length() - 1

    def place(k):
        kw = k >> (shard_bits + narrow_bits)
        row = ((((kw & 1) ^ core) * chips + (((kw >> 1) - chip) & (chips - 1))) << shard_bits) | (k & (shard - 1))
        return row, ((k >> shard_bits) & (narrow - 1)) == y

    for slot in range(narrow):
        lanes = pl.ds(slot * n, n)
        ids = idxg[slot, 0:8, :]
        hi_r[:, lanes] = ids & (ret_spots - 1)
        local = ids & (n - 1)
        val_r[:, lanes] = jnp.where((ids >> node_bits) == y, jnp.int32(1) << ((local >> ret_bits) * 4), 0)
        row, hit = place(idxg[slot, 8:24, :])
        hi_t[:, lanes] = row & (mine_spots - 1)
        val_t[:, lanes] = jnp.where(hit, jnp.int32(1) << ((row >> mine_bits) * 4), 0)
        row, hit = place(idxg[slot, 24:32, :])
        row_a[:, lanes] = jnp.where(hit, row, -1)

    def asn_part(part, carry):
        rows = pl.ds(pl.multiple_of(part * 16, 16), 16)
        spots = lax.broadcasted_iota(I32, (16, 128), 0) + part * 16
        total = None
        for tile in range(grp // 128):
            lanes = slice(tile * 128, tile * 128 + 128)
            hit = jnp.where(jnp.broadcast_to(row_a[0:1, lanes], (16, 128)) == spots, 1.0, 0.0)
            tab_asn[rows, lanes] = hit.astype(BF16)
            total = hit if total is None else total + hit
        as_acc[rows, :] = total.astype(BF16)
        return carry

    def code_tile(tile, carry):
        table(tab_code, hi_t, val_t, mine_spots, tile * 128, 0)
        return carry

    def ret_tile(tile, carry):
        table(tab_ret, hi_r, val_r, ret_spots, tile * 128, 0)
        return carry

    def split_count(count):
        big = jnp.floor(count * (1.0 / 256)) * 256.0
        lane = lax.broadcasted_iota(I32, count.shape, 1)
        return jnp.where(lane < 64, big, count - big).astype(BF16)

    def join_count(pair):
        pair = pair.astype(F32)
        return pair + pltpu.roll(pair, 64, 1)

    lax.fori_loop(0, mine // 16, asn_part, 0)

    wa.wait_recv()
    wg_own = wg_f[core] + wg_rx[...].astype(F32)
    wg_f[core] = wg_own
    wgb_tx[...] = wg_own.astype(BF16)
    wrows = wg_own.shape[0]
    part_rows = wrows // chips

    def wg_rows(step):
        return pl.ds(pl.multiple_of(((chip + step) % chips) * part_rows, part_rows), part_rows)

    wb = {}
    for step in range(1, chips):
        wb[step] = rcopy(
            wgb_tx.at[wg_rows(step), :], wgb_rx.at[step], wb_s.at[step], wb_r.at[step], (chip_dev(step), y)
        )
        wb[step].start()

    as_f[...] = jnp.zeros_like(as_f)

    def code_step(step, carry):
        code_tile(2 * step, 0)
        code_tile(2 * step + 1, 0)
        nodes = pl.ds(pl.multiple_of(step * 256, 256), 256)
        as_f[...] += dot(tab_asn[:, nodes], featg[nodes, :])
        return carry

    steps = grp // 256
    lax.fori_loop(0, steps // 2, code_step, 0)
    arrived(daggg, d_s, d_r, 0)
    d_copies[4].start()
    arrived(daggg, d_s, d_r, 1)
    d_copies[5].start()
    lax.fori_loop(steps // 2, steps, code_step, 0)

    as_cnt[...] = dot(as_acc[...], jnp.ones((128, 128), BF16))
    as_tx[:, 0:width] = as_f[own_half:, :].astype(BF16)
    as_tx[:, width:] = split_count(as_cnt[own_half:, :])
    aa = rcopy(as_tx, as_rx, aa_s, aa_r, (other, y))
    aa.start()

    lax.fori_loop(0, grp // 128, ret_tile, 0)

    for step in range(1, chips):
        wb[step].wait_recv()
    share = wg_f[core, wg_rows(0), :]
    for step in range(1, chips):
        share = share + wgb_rx[step].astype(F32)
    wgc[0] = share
    wc = []
    for at, (peer, slot) in enumerate(((y_right, 3), (y_left, 1), (y_far, 2))):
        wc.append(rcopy(wgc.at[0], wgc.at[slot], wc_s.at[at], wc_r.at[at], (w, peer)))
        wc[-1].start()

    aa.wait_recv()
    as_f[0:own_half, :] += as_rx[:, 0:width].astype(F32)
    as_cnt[0:own_half, :] += join_count(as_rx[:, width:])
    ab = {}
    for step in range(chips):
        rows = pl.ds(step * shard, shard)
        asb_tx[step, :, 0:width] = as_f[rows, :].astype(BF16)
        asb_tx[step, :, width:] = split_count(as_cnt[rows, :])
        if step:
            ab[step] = rcopy(asb_tx.at[step], asb_rx.at[step], ab_s.at[step], ab_r.at[step], (chip_dev(step), y))
            ab[step].start()

    arrived(daggg, d_s, d_r, 2)
    arrived(daggg, d_s, d_r, 3)
    acc[...] = dot(tab_code[:, 0 : 2 * n], daggg[0 : 2 * n, :]) + dot(tab_code[:, 3 * n :], daggg[3 * n :, :])
    ret[...] = dot_nt(dz_all[...], ws[...]) + (1.0 / 8) * (
        dot(tab_ret[:, 0 : 2 * n], daggg[0 : 2 * n, :]) + dot(tab_ret[:, 3 * n :], daggg[3 * n :, :])
    )
    arrived(daggg, d_s, d_r, 4)
    arrived(daggg, d_s, d_r, 5)
    last = daggg[2 * n : 3 * n, :]
    cg_tx[...] = ((acc[own_half:, :] + dot(tab_code[own_half:, 2 * n : 3 * n], last)) * (1.0 / 16)).astype(BF16)
    ca = rcopy(cg_tx, cg_rx, ca_s, ca_r, (other, y))
    ca.start()
    acc[0:own_half, :] = (acc[0:own_half, :] + dot(tab_code[0:own_half, 2 * n : 3 * n], last)) * (1.0 / 16)

    for at in range(3):
        wc[at].wait_recv()

    def share_rows(dev):
        return pl.ds(pl.multiple_of((dev % 2) * wrows + (dev // 2) * part_rows, part_rows), part_rows)

    wgd[share_rows(w), :] = (wgc[0] + wgc[1] + wgc[2] + wgc[3]).astype(BF16)

    def spread(step, carry):
        rcopy(
            wgd.at[share_rows(w), :], wgd.at[share_rows(w), :], wd_s.at[step], wd_r.at[step], ((w + step) % wide, y)
        ).start()
        return carry

    lax.fori_loop(1, wide, spread, 0)

    ca.wait_recv()
    cb = {}
    for step in range(1, chips):
        rows = pl.ds(step * shard, shard)
        cgb_tx[step] = (acc[rows, :] + cg_rx[rows, :].astype(F32)).astype(BF16)
        cb[step] = rcopy(cgb_tx.at[step], cgb_rx.at[step], cb_s.at[step], cb_r.at[step], (chip_dev(step), y))
        cb[step].start()

    fgrad[...] = (ret[...] + dot(tab_ret[:, 2 * n : 3 * n], last) * (1.0 / 8)).astype(BF16)

    own_sum = as_f[0:shard, :]
    own_cnt = as_cnt[0:shard, :]
    for step in range(1, chips):
        ab[step].wait_recv()
        own_sum = own_sum + asb_rx[step, :, 0:width].astype(F32)
        own_cnt = own_cnt + join_count(asb_rx[step, :, width:])
    first = (w * narrow + y) * shard
    cnt_row = counts[pl.ds(first // 128, 1), :]
    cnt_col[...] = jnp.transpose(jnp.broadcast_to(cnt_row, (128, 128)))
    if shard <= 128:
        old_cnt = cnt_col[pl.ds(pl.multiple_of(first % 128, shard), shard), :]
    else:
        old_cnt = jnp.concatenate(
            [jnp.transpose(jnp.broadcast_to(counts[pl.ds(first // 128 + b, 1), :], (128, 128))) for b in range(shard // 128)], 0
        )
    scale = 1.0 / (decay_rate * old_cnt + (1.0 - decay_rate) * own_cnt)
    old = sums[pl.ds(pl.multiple_of(first, shard), shard), :]
    for part in range(width // 128):
        lanes = slice(part * 128, part * 128 + 128)
        newcb[:, lanes] = (decay_rate * old[:, lanes] + (1.0 - decay_rate) * own_sum[:, lanes]) * scale

    def gathered(step, carry):
        source = (w + wide - step) % wide
        rcopy(
            wgd.at[share_rows(source), :], wgd.at[share_rows(source), :], wd_s.at[step], wd_r.at[step], (source, y)
        ).wait_recv()
        return carry

    lax.fori_loop(1, wide, gathered, 0)
    sgrad[...] = wgd[0:wrows, :].astype(F32)
    ngrad[...] = wgd[wrows:, :].astype(F32)

    own = acc[0:shard, :] + cg_rx[0:shard, :].astype(F32)
    for step in range(1, chips):
        cb[step].wait_recv()
        own = own + cgb_rx[step].astype(F32)
    cgrad[...] = own

    for copy in (*f_copies, *d_copies, *i_copies, wa, aa, ca, *wc):
        copy.wait_send()
    for step in range(1, chips):
        wb[step].wait_send()
        ab[step].wait_send()
        cb[step].wait_send()

    def sent(step, carry):
        rcopy(
            wgd.at[share_rows(w), :], wgd.at[share_rows(w), :], wd_s.at[step], wd_r.at[step], ((w + step) % wide, y)
        ).wait_send()
        return carry

    lax.fori_loop(1, wide, sent, 0)


def copy_kernel(count, *refs):
    copies = [pltpu.make_async_copy(refs[at], refs[count + at], refs[-1].at[at]) for at in range(count)]
    for copy in copies:
        copy.start()
    for copy in copies:
        copy.wait()


def on_device(
    wide, narrow,
    features, neighbours, code_ids, assignment, cotangent, code_sums, code_counts, self_weight, neighbour_weight,
):
    n, width = features.shape
    codes = code_sums.shape[0]
    chips = wide // 2
    shard = codes // (wide * narrow)
    mine = codes // narrow
    grp = n * narrow
    hbm = pl.BlockSpec(memory_space=pltpu.HBM)
    dma = pltpu.SemaphoreType.DMA
    wide_rows = self_weight.shape[0]
    scratch = [
        pltpu.VMEM((n, width), BF16),
        pltpu.VMEM((codes, width), F32),
        pltpu.VMEM((codes // 128, 128), F32),
        pltpu.VMEM(self_weight.shape, BF16),
        pltpu.VMEM(neighbour_weight.shape, BF16),
        pltpu.VMEM((codes, width), BF16),
        pltpu.VMEM((grp, width), BF16),
        pltpu.VMEM((grp, width), BF16),
        pltpu.VMEM((IDX_ROWS, n), I32),
        pltpu.VMEM((narrow, IDX_ROWS, n), jnp.int16),
        pltpu.VMEM((codes, n), BF16),
        pltpu.VMEM((grp, n), BF16),
        pltpu.VMEM((mine, grp), BF16),
        pltpu.VMEM((n, grp), BF16),
        pltpu.VMEM((mine, grp), BF16),
        pltpu.VMEM((16, n), I32),
        pltpu.VMEM((16, n), I32),
        pltpu.VMEM((8, n), I32),
        pltpu.VMEM((8, n), I32),
        pltpu.VMEM((16, grp), I32),
        pltpu.VMEM((16, grp), I32),
        pltpu.VMEM((8, grp), I32),
        pltpu.VMEM((8, grp), I32),
        pltpu.VMEM((8, grp), I32),
        pltpu.VMEM((n, width), F32),
        pltpu.VMEM((n, width), F32),
        pltpu.VMEM((n, width), F32),
        pltpu.VMEM((n, width), BF16),
        pltpu.VMEM((n, width), BF16),
        pltpu.VMEM((mine, width), F32),
        pltpu.VMEM((n, width), F32),
        pltpu.VMEM((2, wide_rows, width), F32),
        pltpu.VMEM((wide_rows, width), BF16),
        pltpu.VMEM((wide_rows, width), BF16),
        pltpu.VMEM((wide_rows, width), BF16),
        pltpu.VMEM((chips, wide_rows // chips, width), BF16),
        pltpu.VMEM((narrow, wide_rows // chips, width), F32),
        pltpu.VMEM((2 * wide_rows, width), BF16),
        pltpu.VMEM((mine, width), F32),
        pltpu.VMEM((mine, 128), F32),
        pltpu.VMEM((mine, 128), BF16),
        pltpu.VMEM((mine // 2, width + 128), BF16),
        pltpu.VMEM((mine // 2, width + 128), BF16),
        pltpu.VMEM((chips, shard, width + 128), BF16),
        pltpu.VMEM((chips, shard, width + 128), BF16),
        pltpu.VMEM((mine // 2, width), BF16),
        pltpu.VMEM((mine // 2, width), BF16),
        pltpu.VMEM((chips, shard, width), BF16),
        pltpu.VMEM((chips, shard, width), BF16),
        pltpu.VMEM((128, 128), F32),
        dma((9,)),
        dma((6,)), dma((6,)), dma((6,)), dma((6,)), dma((3,)), dma((3,)),
        dma, dma, dma((chips,)), dma((chips,)), dma((3,)), dma((3,)), dma((wide,)), dma((wide,)),
        dma, dma, dma((chips,)), dma((chips,)), dma, dma, dma((chips,)), dma((chips,)),
    ]
    shapes = (
        jax.ShapeDtypeStruct((n, width), BF16),
        jax.ShapeDtypeStruct((n, width), BF16),
        jax.ShapeDtypeStruct(self_weight.shape, F32),
        jax.ShapeDtypeStruct(neighbour_weight.shape, F32),
        jax.ShapeDtypeStruct((shard, width), F32),
        jax.ShapeDtypeStruct((shard, width), F32),
    )
    vm = pl.BlockSpec(memory_space=pltpu.VMEM)
    operands = (
        features, neighbours.T, code_ids.T, assignment.reshape(1, n), cotangent,
        code_sums, code_counts.reshape(codes // 128, 128), self_weight, neighbour_weight,
    )
    results = pl.pallas_call(
        functools.partial(kernel, wide, narrow, shard),
        out_shape=tuple(pltpu.VMEM(shape.shape, shape.dtype) for shape in shapes),
        in_specs=[hbm] * 9,
        out_specs=(vm,) * 6,
        scratch_shapes=scratch,
        compiler_params=pltpu.CompilerParams(
            collective_id=0, has_side_effects=True, vmem_limit_bytes=48 * 1024 * 1024
        ),
    )(*(pltpu.with_memory_space_constraint(operand, pltpu.HBM) for operand in operands))
    return pl.pallas_call(
        functools.partial(copy_kernel, len(shapes)),
        out_shape=shapes,
        in_specs=[vm] * 6,
        out_specs=(hbm,) * 6,
        scratch_shapes=[dma((6,))],
        compiler_params=pltpu.CompilerParams(vmem_limit_bytes=8 * 1024 * 1024),
    )(*results)


def solution(mesh):
    both = ("wide", "narrow")
    return jax.shard_map(
        functools.partial(on_device, mesh.shape["wide"], mesh.shape["narrow"]),
        mesh=mesh,
        in_specs=(P(both, None), P(both, None), P(both, None), P(both), P(both, None), P(), P(), P(), P()),
        out_specs=(P(both, None), P(both, None), P(), P(), P(both, None), P(both, None)),
        check_vma=False,
    )
```

```python
import functools

import jax
import jax.numpy as jnp
from jax import lax
from jax.experimental import pallas as pl
from jax.experimental.pallas import tpu as pltpu
from jax.sharding import PartitionSpec as P

MESH = pl.DeviceIdType.MESH
F32, BF16, I32 = jnp.float32, jnp.bfloat16, jnp.int32
decay_rate = 0.5
IDX_ROWS = 32
NIBBLES = 0x0F0F0F0F


def dot(a, b):
    return jnp.dot(a, b, preferred_element_type=F32)


def dot_nt(a, b):
    return lax.dot_general(a, b, (((1,), (1,)), ((), ())), preferred_element_type=F32)


def dot_tn(a, b):
    return lax.dot_general(a, b, (((0,), (0,)), ((), ())), preferred_element_type=F32)


def words_of(spots, his, vals):
    word = None
    for hi, val in zip(his, vals):
        term = jnp.where(spots == hi, val, 0)
        word = term if word is None else word + term
    return word


def fields_of(words):
    even = odd = None
    for word in words:
        low, high = word & NIBBLES, (word >> 4) & NIBBLES
        even = low if even is None else even + low
        odd = high if odd is None else odd + high
    out = []
    for field in range(8):
        part = (even, odd)[field % 2]
        shift = 8 * (field // 2)
        if shift:
            part = part >> shift
        if shift < 24:
            part = part & 255
        out.append(part.astype(F32).astype(BF16))
    return out


def kernel(
    wide, narrow, shard,
    feat_hbm, nb_hbm, code_hbm, assign_hbm, cot_hbm, sums_hbm, counts_hbm, ws_hbm, wn_hbm,
    out, fgrad, sgrad, ngrad, newcb, cgrad,
    cot, sums, counts, ws, wn,
    codebook, featg, daggg, idx_own, idxg, tab_far, tab_near, tab_code, tab_ret, tab_asn,
    hi_f, val_f, hi_n, val_n, hi_t, val_t, hi_r, val_r, row_a, far, near, hid, dz_all, agg_all, acc,
    wg_f, wg_tx, wg_rx, wgb_tx, wgb_rx, wgc, wgd, as_f, as_cnt, as_acc, as_tx, as_rx, asb_tx, asb_rx,
    cg_tx, cg_rx, cgb_tx, cgb_rx, cnt_col,
    in_sem, f_s, f_r, d_s, d_r, i_s, i_r, wa_s, wa_r, wb_s, wb_r, wc_s, wc_r, wd_s, wd_r, we_s, we_r,
    aa_s, aa_r, ab_s, ab_r, ca_s, ca_r, cb_s, cb_r,
):
    n = cot.shape[0]
    half = n // 2
    chips = wide // 2
    codes = sums.shape[0]
    mine = codes // narrow
    own_half = mine // 2
    grp = n * narrow
    w = lax.axis_index("wide")
    y = lax.axis_index("narrow")
    core = w % 2
    chip = w // 2
    y_right, y_left, y_far = (y + 1) % narrow, (y + 3) % narrow, (y + 2) % narrow
    other = chip * 2 + (1 - core)

    x_chips = min(4, chips)
    z_chips = chips // x_chips
    chip_z, chip_x = chip // x_chips, chip % x_chips

    def chip_at(step, sign=1):
        step_z, step_x = step // x_chips, step % x_chips
        at_z = (chip_z + (step_z if sign > 0 else z_chips - step_z)) % z_chips
        at_x = (chip_x + (step_x if sign > 0 else x_chips - step_x)) % x_chips
        return at_z * x_chips + at_x

    def chip_dev(step):
        return chip_at(step) * 2 + core

    def hops(step):
        step_z, step_x = step // x_chips, step % x_chips
        return min(step_z, z_chips - step_z) + min(step_x, x_chips - step_x)

    steps_out = sorted(range(1, chips), key=lambda step: -hops(step))

    def rcopy(src, dst, ssem, rsem, dev):
        return pltpu.make_async_remote_copy(
            src_ref=src, dst_ref=dst, send_sem=ssem, recv_sem=rsem, device_id=dev, device_id_type=MESH
        )

    feat = featg.at[pl.ds(0, n), :]
    idx_own[24:32, :] = jnp.zeros((8, n), I32)
    fetched = [
        pltpu.make_async_copy(src, dst, in_sem.at[at])
        for at, (src, dst) in enumerate(
            (
                (feat_hbm, feat),
                (nb_hbm, idx_own.at[pl.ds(0, 8), :]),
                (code_hbm, idx_own.at[pl.ds(8, 16), :]),
                (assign_hbm, idx_own.at[pl.ds(24, 1), :]),
                (counts_hbm, counts),
                (sums_hbm, sums),
                (ws_hbm, ws),
                (wn_hbm, wn),
                (cot_hbm, cot),
            )
        )
    ]
    for copy in fetched:
        copy.start()

    barrier = pltpu.get_barrier_semaphore()
    for peer in (y_right, y_left, y_far):
        pl.semaphore_signal(barrier, inc=1, device_id=(w, peer), device_id_type=MESH)

    for peer in (*(chip_dev(step) for step in steps_out), other):
        pl.semaphore_signal(barrier, inc=1, device_id=(peer, y), device_id_type=MESH)
    for at in range(4):
        fetched[at].wait()
    pl.semaphore_wait(barrier, narrow - 1 + chips)

    def low(slot):
        return pl.ds(slot * n, half)

    def high(slot):
        return pl.ds(slot * n + half, half)

    def gather_copies(buf, ssem, rsem):
        right, left = (w, y_right), (w, y_left)

        def make(src, dst, at, dev):
            return rcopy(buf.at[src, :], buf.at[dst, :], ssem.at[at], rsem.at[at], dev)

        return (
            make(low(0), low(3), 0, right),
            make(high(0), high(1), 1, left),
            make(high(0), high(3), 2, right),
            make(low(0), low(1), 3, left),
            make(low(3), low(2), 4, right),
            make(high(1), high(2), 5, left),
        )

    def arrived(buf, ssem, rsem, at):
        region = (low(3), high(1), high(3), low(1), low(2), high(2))[at]
        rcopy(buf.at[region, :], buf.at[region, :], ssem.at[at], rsem.at[at], (w, y_right)).wait_recv()

    f_copies = gather_copies(featg, f_s, f_r)
    for at in range(4):
        f_copies[at].start()
    idxg[0] = idx_own[...].astype(jnp.int16)
    i_copies = [
        rcopy(idxg.at[0], idxg.at[slot], i_s.at[at], i_r.at[at], (w, peer))
        for at, (peer, slot) in enumerate(((y_right, 3), (y_left, 1), (y_far, 2)))
    ]

    def table(tab, his_ref, vals_ref, spots_in, lane_at, first_spot):
        lanes = pl.ds(pl.multiple_of(lane_at, 128), 128)
        picks = his_ref.shape[0]
        his = [jnp.broadcast_to(his_ref[j : j + 1, lanes], (16, 128)) for j in range(picks)]
        vals = [jnp.broadcast_to(vals_ref[j : j + 1, lanes], (16, 128)) for j in range(picks)]
        base = lax.broadcasted_iota(I32, (16, 128), 0) + first_spot
        for part in range(min(spots_in, 128) // 16):
            spots = base + part * 16
            words = [words_of(spots, his[at : at + 8], vals[at : at + 8]) for at in range(0, picks, 8)]
            for field, counts_part in enumerate(fields_of(words)):
                row = pl.multiple_of(field * spots_in + part * 16 + first_spot, 16)
                tab[pl.ds(row, 16), lanes] = counts_part

    far_spots = codes // 8
    far_bits = far_spots.bit_length() - 1
    near_spots = grp // 8
    near_bits = near_spots.bit_length() - 1
    node_bits = n.bit_length() - 1
    own_ids = idx_own[8:24, :]
    hi_f[...] = own_ids & (far_spots - 1)
    val_f[...] = jnp.int32(1) << ((own_ids >> far_bits) * 4)
    own_ids = idx_own[0:8, :]
    own_ids = ((((own_ids >> node_bits) - y) & (narrow - 1)) << node_bits) | (own_ids & (n - 1))
    hi_n[...] = own_ids & (near_spots - 1)
    val_n[...] = jnp.int32(1) << ((own_ids >> near_bits) * 4)

    def far_tile(tile, carry):
        table(tab_far, hi_f, val_f, far_spots, (tile // (far_spots // 128)) * 128, (tile % (far_spots // 128)) * 128)
        return carry

    def near_tile(tile, carry):
        table(tab_near, hi_n, val_n, near_spots, (tile // (near_spots // 128)) * 128, (tile % (near_spots // 128)) * 128)
        return carry

    far_tiles = (n // 128) * (far_spots // 128)
    lax.fori_loop(0, far_tiles // 2, far_tile, 0)
    arrived(featg, f_s, f_r, 0)
    f_copies[4].start()
    arrived(featg, f_s, f_r, 1)
    f_copies[5].start()
    for copy in i_copies:
        copy.start()
    lax.fori_loop(far_tiles // 2, far_tiles, far_tile, 0)
    width = sums.shape[1]
    for at in range(4, 9):
        fetched[at].wait()
    blocks = codes // 128
    inverse = jnp.transpose(jnp.concatenate([1.0 / counts[...]] * (128 // blocks), 0))
    for block in range(blocks):
        column = jnp.broadcast_to(inverse[:, block : block + 1], (128, 128))
        for part in range(width // 128):
            at = (slice(block * 128, block * 128 + 128), slice(part * 128, part * 128 + 128))
            codebook[at] = (sums[at] * column).astype(BF16)
    far[...] = jnp.zeros_like(far)
    near_tiles = (n // 128) * (near_spots // 128)
    step_codes = codes // near_tiles

    def near_step(tile, carry):
        near_tile(tile, 0)
        rows = pl.ds(pl.multiple_of(tile * step_codes, step_codes), step_codes)
        far[...] += dot_tn(tab_far[rows, :], codebook[rows, :])
        return carry

    lax.fori_loop(0, near_tiles, near_step, 0)
    hid[...] = dot(feat[...], ws[...])
    near[...] = dot_tn(tab_near[0:n, :], feat[...])
    arrived(featg, f_s, f_r, 2)
    near[...] += dot_tn(tab_near[3 * n : 4 * n, :], featg[3 * n : 4 * n, :])
    arrived(featg, f_s, f_r, 3)
    near[...] += dot_tn(tab_near[n : 2 * n, :], featg[n : 2 * n, :])
    arrived(featg, f_s, f_r, 4)
    arrived(featg, f_s, f_r, 5)

    d_copies = gather_copies(daggg, d_s, d_r)
    for at in range(2):
        rows = pl.ds(at * half, half)
        total = near[rows, :] + dot_tn(tab_near[2 * n : 3 * n, at * half : at * half + half], featg[2 * n : 3 * n, :])
        agg = (total * (1.0 / 8) + far[rows, :] * (1.0 / 16)).astype(BF16)
        agg_all[rows, :] = agg
        z = hid[rows, :] + dot(agg, wn[...])
        s = jax.nn.sigmoid(z)
        out[rows, :] = (z * s).astype(BF16)
        dz = (cot[rows, :].astype(F32) * s * (1.0 + z * (1.0 - s))).astype(BF16)
        dz_all[rows, :] = dz
        daggg[rows, :] = dot_nt(dz, wn[...]).astype(BF16)
        d_copies[(0, 1)[at]].start()
        d_copies[(3, 2)[at]].start()

    def weight_half(which, x):
        wg_f[which] = dot_tn(x, dz_all[...])

    weight_half(0, feat[...])
    weight_half(1, agg_all[...])
    wg_tx[...] = wg_f[1 - core].astype(BF16)
    wa = rcopy(wg_tx, wg_rx, wa_s, wa_r, (other, y))
    wa.start()

    for at in range(3):
        i_copies[at].wait_recv()
    shard_bits = shard.bit_length() - 1
    narrow_bits = narrow.bit_length() - 1
    mine_spots = mine // 8
    mine_bits = mine_spots.bit_length() - 1
    ret_spots = n // 8
    ret_bits = ret_spots.bit_length() - 1

    def place(k):
        kw = k >> (shard_bits + narrow_bits)
        kc = kw >> 1
        step = ((((kc >> (x_chips.bit_length() - 1)) - chip_z) & (z_chips - 1)) * x_chips) | ((kc - chip_x) & (x_chips - 1))
        row = ((((kw & 1) ^ core) * chips + step) << shard_bits) | (k & (shard - 1))
        return row, ((k >> shard_bits) & (narrow - 1)) == y

    for slot in range(narrow):
        lanes = pl.ds(slot * n, n)
        block = idxg[slot].astype(I32)
        ids = block[0:8, :]
        hi_r[:, lanes] = ids & (ret_spots - 1)
        local = ids & (n - 1)
        val_r[:, lanes] = jnp.where((ids >> node_bits) == y, jnp.int32(1) << ((local >> ret_bits) * 4), 0)
        row, hit = place(block[8:24, :])
        hi_t[:, lanes] = row & (mine_spots - 1)
        val_t[:, lanes] = jnp.where(hit, jnp.int32(1) << ((row >> mine_bits) * 4), 0)
        row, hit = place(block[24:32, :])
        row_a[:, lanes] = jnp.where(hit, row, -1)

    def asn_part(part, carry):
        rows = pl.ds(pl.multiple_of(part * 16, 16), 16)
        spots = lax.broadcasted_iota(I32, (16, 128), 0) + part * 16
        total = None
        for tile in range(grp // 128):
            lanes = slice(tile * 128, tile * 128 + 128)
            hit = jnp.where(jnp.broadcast_to(row_a[0:1, lanes], (16, 128)) == spots, 1.0, 0.0)
            tab_asn[rows, lanes] = hit.astype(BF16)
            total = hit if total is None else total + hit
        as_acc[rows, :] = total.astype(BF16)
        return carry

    def code_tile(tile, carry):
        table(tab_code, hi_t, val_t, mine_spots, tile * 128, 0)
        return carry

    def ret_tile(tile, carry):
        table(tab_ret, hi_r, val_r, ret_spots, tile * 128, 0)
        return carry

    def split_count(count):
        big = jnp.floor(count * (1.0 / 256)) * 256.0
        lane = lax.broadcasted_iota(I32, count.shape, 1)
        return jnp.where(lane < 64, big, count - big).astype(BF16)

    def join_count(pair):
        pair = pair.astype(F32)
        return pair + pltpu.roll(pair, 64, 1)

    lax.fori_loop(0, mine // 64, asn_part, 0)

    wa.wait_recv()
    wg_own = wg_f[core] + wg_rx[...].astype(F32)
    wg_f[core] = wg_own
    wgb_tx[...] = wg_own.astype(BF16)
    wrows = wg_own.shape[0]
    part_rows = wrows // chips

    def wg_rows(at):
        return pl.ds(pl.multiple_of(at * part_rows, part_rows), part_rows)

    wb = {}
    for step in steps_out:
        wb[step] = rcopy(
            wgb_tx.at[wg_rows(chip_at(step)), :], wgb_rx.at[step], wb_s.at[step], wb_r.at[step], (chip_dev(step), y)
        )
        wb[step].start()
    lax.fori_loop(mine // 64, mine // 16, asn_part, 0)

    as_f[...] = jnp.zeros_like(as_f)

    def code_step(step, carry):
        code_tile(2 * step, 0)
        code_tile(2 * step + 1, 0)
        nodes = pl.ds(pl.multiple_of(step * 256, 256), 256)
        as_f[...] += dot(tab_asn[:, nodes], featg[nodes, :])
        return carry

    steps = grp // 256
    lax.fori_loop(0, steps // 2, code_step, 0)
    arrived(daggg, d_s, d_r, 0)
    d_copies[4].start()
    arrived(daggg, d_s, d_r, 1)
    d_copies[5].start()
    lax.fori_loop(steps // 2, steps, code_step, 0)

    as_cnt[...] = dot(as_acc[...], jnp.ones((128, 128), BF16))
    as_tx[:, 0:width] = as_f[own_half:, :].astype(BF16)
    as_tx[:, width:] = split_count(as_cnt[own_half:, :])
    aa = rcopy(as_tx, as_rx, aa_s, aa_r, (other, y))
    aa.start()

    for step in steps_out:
        wb[step].wait_recv()
    share = wg_f[core, wg_rows(chip), :]
    for step in steps_out:
        share = share + wgb_rx[step].astype(F32)
    wgc[0] = share
    wc = []
    for at, (peer, slot) in enumerate(((y_right, 3), (y_left, 1), (y_far, 2))):
        wc.append(rcopy(wgc.at[0], wgc.at[slot], wc_s.at[at], wc_r.at[at], (w, peer)))
        wc[-1].start()

    aa.wait_recv()
    as_f[0:own_half, :] += as_rx[:, 0:width].astype(F32)
    as_cnt[0:own_half, :] += join_count(as_rx[:, width:])
    ab = {}
    for step in steps_out:
        rows = pl.ds(step * shard, shard)
        asb_tx[step, :, 0:width] = as_f[rows, :].astype(BF16)
        asb_tx[step, :, width:] = split_count(as_cnt[rows, :])
        ab[step] = rcopy(asb_tx.at[step], asb_rx.at[step], ab_s.at[step], ab_r.at[step], (chip_dev(step), y))
        ab[step].start()

    acc[...] = dot(tab_code[:, 0:n], daggg[0:n, :])
    arrived(daggg, d_s, d_r, 2)
    arrived(daggg, d_s, d_r, 3)
    acc[...] += dot(tab_code[:, n : 2 * n], daggg[n : 2 * n, :]) + dot(tab_code[:, 3 * n :], daggg[3 * n :, :])
    arrived(daggg, d_s, d_r, 4)
    arrived(daggg, d_s, d_r, 5)
    last = daggg[2 * n : 3 * n, :]
    block = own_half // 2

    def finished(first):
        rows = slice(first, first + block)
        return (acc[rows, :] + dot(tab_code[rows, 2 * n : 3 * n], last)) * (1.0 / 16)

    ca = {}
    for part in (1, 0):
        rows = pl.ds(part * block, block)
        cg_tx[rows, :] = finished(own_half + part * block).astype(BF16)
        ca[part] = rcopy(cg_tx.at[rows, :], cg_rx.at[rows, :], ca_s.at[part], ca_r.at[part], (other, y))
        ca[part].start()
    for part in (1, 0):
        acc[part * block : part * block + block, :] = finished(part * block)

    for at in range(3):
        wc[at].wait_recv()

    def share_rows(at):
        return pl.ds(pl.multiple_of(core * wrows + at * part_rows, part_rows), part_rows)

    wgd[share_rows(chip), :] = (wgc[0] + wgc[1] + wgc[2] + wgc[3]).astype(BF16)
    wd = {}
    for step in steps_out:
        mine_rows = wgd.at[share_rows(chip), :]
        wd[step] = rcopy(mine_rows, mine_rows, wd_s.at[step], wd_r.at[step], (chip_dev(step), y))
        wd[step].start()

    cb = {}
    for part in (1, 0):
        ca[part].wait_recv()
        for step in steps_out:
            if step * shard // block != part:
                continue
            rows = pl.ds(step * shard, shard)
            cgb_tx[step] = (acc[rows, :] + cg_rx[rows, :].astype(F32)).astype(BF16)
            cb[step] = rcopy(cgb_tx.at[step], cgb_rx.at[step], cb_s.at[step], cb_r.at[step], (chip_dev(step), y))
            cb[step].start()

    lax.fori_loop(0, grp // 128, ret_tile, 0)
    fgrad[...] = (dot_nt(dz_all[...], ws[...]) + dot(tab_ret[...], daggg[...]) * (1.0 / 8)).astype(BF16)

    own_sum = as_f[0:shard, :]
    own_cnt = as_cnt[0:shard, :]
    for step in steps_out:
        ab[step].wait_recv()
        own_sum = own_sum + asb_rx[step, :, 0:width].astype(F32)
        own_cnt = own_cnt + join_count(asb_rx[step, :, width:])
    first = (w * narrow + y) * shard
    cnt_row = counts[pl.ds(first // 128, 1), :]
    cnt_col[...] = jnp.transpose(jnp.broadcast_to(cnt_row, (128, 128)))
    if shard <= 128:
        old_cnt = cnt_col[pl.ds(pl.multiple_of(first % 128, shard), shard), :]
    else:
        old_cnt = jnp.concatenate(
            [jnp.transpose(jnp.broadcast_to(counts[pl.ds(first // 128 + b, 1), :], (128, 128))) for b in range(shard // 128)], 0
        )
    scale = 1.0 / (decay_rate * old_cnt + (1.0 - decay_rate) * own_cnt)
    old = sums[pl.ds(pl.multiple_of(first, shard), shard), :]
    for part in range(width // 128):
        lanes = slice(part * 128, part * 128 + 128)
        newcb[:, lanes] = (decay_rate * old[:, lanes] + (1.0 - decay_rate) * own_sum[:, lanes]) * scale

    for step in steps_out:
        source = wgd.at[share_rows(chip_at(step, -1)), :]
        rcopy(source, source, wd_s.at[step], wd_r.at[step], (chip_dev(step), y)).wait_recv()
    own_rows = wgd.at[pl.ds(pl.multiple_of(core * wrows, wrows), wrows), :]
    other_rows = wgd.at[pl.ds(pl.multiple_of((1 - core) * wrows, wrows), wrows), :]
    we = rcopy(own_rows, own_rows, we_s, we_r, (other, y))
    we.start()
    rcopy(other_rows, other_rows, we_s, we_r, (other, y)).wait_recv()
    sgrad[...] = wgd[0:wrows, :].astype(F32)
    ngrad[...] = wgd[wrows:, :].astype(F32)

    own = acc[0:shard, :] + cg_rx[0:shard, :].astype(F32)
    for step in steps_out:
        cb[step].wait_recv()
        own = own + cgb_rx[step].astype(F32)
    cgrad[...] = own

    for copy in (*f_copies, *d_copies, *i_copies, wa, aa, *ca.values(), *wc, we):
        copy.wait_send()
    for step in steps_out:
        for copies in (wb, ab, wd, cb):
            copies[step].wait_send()


def copy_kernel(count, *refs):
    copies = [pltpu.make_async_copy(refs[at], refs[count + at], refs[-1].at[at]) for at in range(count)]
    for copy in copies:
        copy.start()
    for copy in copies:
        copy.wait()


def on_device(
    wide, narrow,
    features, neighbours, code_ids, assignment, cotangent, code_sums, code_counts, self_weight, neighbour_weight,
):
    n, width = features.shape
    codes = code_sums.shape[0]
    chips = wide // 2
    shard = codes // (wide * narrow)
    mine = codes // narrow
    grp = n * narrow
    hbm = pl.BlockSpec(memory_space=pltpu.HBM)
    dma = pltpu.SemaphoreType.DMA
    wide_rows = self_weight.shape[0]
    scratch = [
        pltpu.VMEM((n, width), BF16),
        pltpu.VMEM((codes, width), F32),
        pltpu.VMEM((codes // 128, 128), F32),
        pltpu.VMEM(self_weight.shape, BF16),
        pltpu.VMEM(neighbour_weight.shape, BF16),
        pltpu.VMEM((codes, width), BF16),
        pltpu.VMEM((grp, width), BF16),
        pltpu.VMEM((grp, width), BF16),
        pltpu.VMEM((IDX_ROWS, n), I32),
        pltpu.VMEM((narrow, IDX_ROWS, n), jnp.int16),
        pltpu.VMEM((codes, n), BF16),
        pltpu.VMEM((grp, n), BF16),
        pltpu.VMEM((mine, grp), BF16),
        pltpu.VMEM((n, grp), BF16),
        pltpu.VMEM((mine, grp), BF16),
        pltpu.VMEM((16, n), I32),
        pltpu.VMEM((16, n), I32),
        pltpu.VMEM((8, n), I32),
        pltpu.VMEM((8, n), I32),
        pltpu.VMEM((16, grp), I32),
        pltpu.VMEM((16, grp), I32),
        pltpu.VMEM((8, grp), I32),
        pltpu.VMEM((8, grp), I32),
        pltpu.VMEM((8, grp), I32),
        pltpu.VMEM((n, width), F32),
        pltpu.VMEM((n, width), F32),
        pltpu.VMEM((n, width), F32),
        pltpu.VMEM((n, width), BF16),
        pltpu.VMEM((n, width), BF16),
        pltpu.VMEM((mine, width), F32),
        pltpu.VMEM((2, wide_rows, width), F32),
        pltpu.VMEM((wide_rows, width), BF16),
        pltpu.VMEM((wide_rows, width), BF16),
        pltpu.VMEM((wide_rows, width), BF16),
        pltpu.VMEM((chips, wide_rows // chips, width), BF16),
        pltpu.VMEM((narrow, wide_rows // chips, width), F32),
        pltpu.VMEM((2 * wide_rows, width), BF16),
        pltpu.VMEM((mine, width), F32),
        pltpu.VMEM((mine, 128), F32),
        pltpu.VMEM((mine, 128), BF16),
        pltpu.VMEM((mine // 2, width + 128), BF16),
        pltpu.VMEM((mine // 2, width + 128), BF16),
        pltpu.VMEM((chips, shard, width + 128), BF16),
        pltpu.VMEM((chips, shard, width + 128), BF16),
        pltpu.VMEM((mine // 2, width), BF16),
        pltpu.VMEM((mine // 2, width), BF16),
        pltpu.VMEM((chips, shard, width), BF16),
        pltpu.VMEM((chips, shard, width), BF16),
        pltpu.VMEM((128, 128), F32),
        dma((9,)),
        dma((6,)), dma((6,)), dma((6,)), dma((6,)), dma((3,)), dma((3,)),
        dma, dma, dma((chips,)), dma((chips,)), dma((3,)), dma((3,)), dma((chips,)), dma((chips,)), dma, dma,
        dma, dma, dma((chips,)), dma((chips,)), dma((2,)), dma((2,)), dma((chips,)), dma((chips,)),
    ]
    shapes = (
        jax.ShapeDtypeStruct((n, width), BF16),
        jax.ShapeDtypeStruct((n, width), BF16),
        jax.ShapeDtypeStruct(self_weight.shape, F32),
        jax.ShapeDtypeStruct(neighbour_weight.shape, F32),
        jax.ShapeDtypeStruct((shard, width), F32),
        jax.ShapeDtypeStruct((shard, width), F32),
    )
    vm = pl.BlockSpec(memory_space=pltpu.VMEM)
    operands = (
        features, neighbours.T, code_ids.T, assignment.reshape(1, n), cotangent,
        code_sums, code_counts.reshape(codes // 128, 128), self_weight, neighbour_weight,
    )
    results = pl.pallas_call(
        functools.partial(kernel, wide, narrow, shard),
        out_shape=tuple(pltpu.VMEM(shape.shape, shape.dtype) for shape in shapes),
        in_specs=[hbm] * 9,
        out_specs=(vm,) * 6,
        scratch_shapes=scratch,
        compiler_params=pltpu.CompilerParams(
            collective_id=0, has_side_effects=True, vmem_limit_bytes=48 * 1024 * 1024
        ),
    )(*(pltpu.with_memory_space_constraint(operand, pltpu.HBM) for operand in operands))
    return pl.pallas_call(
        functools.partial(copy_kernel, len(shapes)),
        out_shape=shapes,
        in_specs=[vm] * 6,
        out_specs=(hbm,) * 6,
        scratch_shapes=[dma((6,))],
        compiler_params=pltpu.CompilerParams(vmem_limit_bytes=8 * 1024 * 1024),
    )(*results)


def solution(mesh):
    both = ("wide", "narrow")
    return jax.shard_map(
        functools.partial(on_device, mesh.shape["wide"], mesh.shape["narrow"]),
        mesh=mesh,
        in_specs=(P(both, None), P(both, None), P(both, None), P(both), P(both, None), P(), P(), P(), P()),
        out_specs=(P(both, None), P(both, None), P(), P(), P(both, None), P(both, None)),
        check_vma=False,
    )
```

```python
import functools

import jax
import jax.numpy as jnp
from jax import lax
from jax.experimental import pallas as pl
from jax.experimental.pallas import tpu as pltpu
from jax.sharding import PartitionSpec as P

MESH = pl.DeviceIdType.MESH
F32, BF16, I32 = jnp.float32, jnp.bfloat16, jnp.int32
decay_rate = 0.5
IDX_ROWS = 32
NIBBLES = 0x0F0F0F0F


def dot(a, b):
    return jnp.dot(a, b, preferred_element_type=F32)


def dot_nt(a, b):
    return lax.dot_general(a, b, (((1,), (1,)), ((), ())), preferred_element_type=F32)


def dot_tn(a, b):
    return lax.dot_general(a, b, (((0,), (0,)), ((), ())), preferred_element_type=F32)


def words_of(spots, his, vals):
    word = None
    for hi, val in zip(his, vals):
        term = jnp.where(spots == hi, val, 0)
        word = term if word is None else word + term
    return word


def fields_of(words):
    even = odd = None
    for word in words:
        low, high = word & NIBBLES, (word >> 4) & NIBBLES
        even = low if even is None else even + low
        odd = high if odd is None else odd + high
    out = []
    for field in range(8):
        part = (even, odd)[field % 2]
        shift = 8 * (field // 2)
        if shift:
            part = part >> shift
        if shift < 24:
            part = part & 255
        out.append(part.astype(F32).astype(BF16))
    return out


def kernel(
    wide, narrow, shard,
    feat_hbm, nb_hbm, code_hbm, assign_hbm, cot_hbm, sums_hbm, counts_hbm, ws_hbm, wn_hbm,
    out, fgrad, sgrad, ngrad, newcb, cgrad,
    cot, sums, counts, ws, wn,
    codebook, featg, daggg, idx_own, idxg, tab_far, tab_near, tab_code, tab_ret, tab_asn,
    hi_f, val_f, hi_n, val_n, hi_t, val_t, hi_r, val_r, row_a, asn_hi, asn_lo, far, near, hid, dz_all, taken, acc,
    wg_f, wg_tx, wg_rx, wgb_tx, wgb_rx, wgc, wgd, as_f, as_cnt, as_acc, as_tx, as_rx, asb_tx, asb_rx,
    cg_tx, cg_rx, cgb_tx, cgb_rx, cnt_col,
    in_sem, f_s, f_r, d_s, d_r, i_s, i_r, wa_s, wa_r, wb_s, wb_r, wc_s, wc_r, wd_s, wd_r, we_s, we_r,
    aa_s, aa_r, ab_s, ab_r, ca_s, ca_r, cb_s, cb_r,
):
    n = cot.shape[0]
    half = n // 2
    chips = wide // 2
    codes = sums.shape[0]
    mine = codes // narrow
    own_half = mine // 2
    grp = n * narrow
    w = lax.axis_index("wide")
    y = lax.axis_index("narrow")
    core = w % 2
    chip = w // 2
    y_right, y_left, y_far = (y + 1) % narrow, (y + 3) % narrow, (y + 2) % narrow
    other = chip * 2 + (1 - core)

    x_chips = min(4, chips)
    z_chips = chips // x_chips
    chip_z, chip_x = chip // x_chips, chip % x_chips

    def chip_at(step, sign=1):
        step_z, step_x = step // x_chips, step % x_chips
        at_z = (chip_z + (step_z if sign > 0 else z_chips - step_z)) % z_chips
        at_x = (chip_x + (step_x if sign > 0 else x_chips - step_x)) % x_chips
        return at_z * x_chips + at_x

    def chip_dev(step):
        return chip_at(step) * 2 + core

    def hops(step):
        step_z, step_x = step // x_chips, step % x_chips
        return min(step_z, z_chips - step_z) + min(step_x, x_chips - step_x)

    steps_out = sorted(range(1, chips), key=lambda step: -hops(step))

    def rcopy(src, dst, ssem, rsem, dev):
        return pltpu.make_async_remote_copy(
            src_ref=src, dst_ref=dst, send_sem=ssem, recv_sem=rsem, device_id=dev, device_id_type=MESH
        )

    feat = featg.at[pl.ds(0, n), :]
    idx_own[24:32, :] = jnp.zeros((8, n), I32)
    fetched = [
        pltpu.make_async_copy(src, dst, in_sem.at[at])
        for at, (src, dst) in enumerate(
            (
                (feat_hbm, feat),
                (nb_hbm, idx_own.at[pl.ds(0, 8), :]),
                (code_hbm, idx_own.at[pl.ds(8, 16), :]),
                (assign_hbm, idx_own.at[pl.ds(24, 1), :]),
                (counts_hbm, counts),
                (sums_hbm, sums),
                (ws_hbm, ws),
                (wn_hbm, wn),
                (cot_hbm, cot),
            )
        )
    ]
    for copy in fetched:
        copy.start()

    barrier = pltpu.get_barrier_semaphore()
    for peer in (y_right, y_left, y_far):
        pl.semaphore_signal(barrier, inc=1, device_id=(w, peer), device_id_type=MESH)

    for peer in (*(chip_dev(step) for step in steps_out), other):
        pl.semaphore_signal(barrier, inc=1, device_id=(peer, y), device_id_type=MESH)
    for at in range(4):
        fetched[at].wait()
    pl.semaphore_wait(barrier, narrow - 1 + chips)

    def low(slot):
        return pl.ds(slot * n, half)

    def high(slot):
        return pl.ds(slot * n + half, half)

    def gather_copies(buf, ssem, rsem):
        right, left = (w, y_right), (w, y_left)

        def make(src, dst, at, dev):
            return rcopy(buf.at[src, :], buf.at[dst, :], ssem.at[at], rsem.at[at], dev)

        return (
            make(low(0), low(3), 0, right),
            make(high(0), high(1), 1, left),
            make(high(0), high(3), 2, right),
            make(low(0), low(1), 3, left),
            make(low(3), low(2), 4, right),
            make(high(1), high(2), 5, left),
        )

    def arrived(buf, ssem, rsem, at):
        region = (low(3), high(1), high(3), low(1), low(2), high(2))[at]
        rcopy(buf.at[region, :], buf.at[region, :], ssem.at[at], rsem.at[at], (w, y_right)).wait_recv()

    f_copies = gather_copies(featg, f_s, f_r)
    for at in range(4):
        f_copies[at].start()
    idxg[0] = idx_own[...].astype(jnp.int16)
    i_copies = [
        rcopy(idxg.at[0], idxg.at[slot], i_s.at[at], i_r.at[at], (w, peer))
        for at, (peer, slot) in enumerate(((y_right, 3), (y_left, 1), (y_far, 2)))
    ]

    def table(tab, his_ref, vals_ref, spots_in, lane_at, first_spot):
        lanes = pl.ds(pl.multiple_of(lane_at, 128), 128)
        picks = his_ref.shape[0]
        his = [jnp.broadcast_to(his_ref[j : j + 1, lanes], (16, 128)) for j in range(picks)]
        vals = [jnp.broadcast_to(vals_ref[j : j + 1, lanes], (16, 128)) for j in range(picks)]
        base = lax.broadcasted_iota(I32, (16, 128), 0) + first_spot
        for part in range(min(spots_in, 128) // 16):
            spots = base + part * 16
            words = [words_of(spots, his[at : at + 8], vals[at : at + 8]) for at in range(0, picks, 8)]
            for field, counts_part in enumerate(fields_of(words)):
                row = pl.multiple_of(field * spots_in + part * 16 + first_spot, 16)
                tab[pl.ds(row, 16), lanes] = counts_part

    far_spots = codes // 8
    far_bits = far_spots.bit_length() - 1
    near_spots = grp // 8
    near_bits = near_spots.bit_length() - 1
    node_bits = n.bit_length() - 1
    own_ids = idx_own[8:24, :]
    hi_f[...] = own_ids & (far_spots - 1)
    val_f[...] = jnp.int32(1) << ((own_ids >> far_bits) * 4)
    own_ids = idx_own[0:8, :]
    own_ids = ((((own_ids >> node_bits) - y) & (narrow - 1)) << node_bits) | (own_ids & (n - 1))
    hi_n[...] = own_ids & (near_spots - 1)
    val_n[...] = jnp.int32(1) << ((own_ids >> near_bits) * 4)

    def far_tile(tile, carry):
        table(tab_far, hi_f, val_f, far_spots, (tile // (far_spots // 128)) * 128, (tile % (far_spots // 128)) * 128)
        return carry

    def near_tile(tile, carry):
        table(tab_near, hi_n, val_n, near_spots, (tile // (near_spots // 128)) * 128, (tile % (near_spots // 128)) * 128)
        return carry

    far_tiles = (n // 128) * (far_spots // 128)
    lax.fori_loop(0, far_tiles, far_tile, 0)
    width = sums.shape[1]
    for at in range(4, 9):
        fetched[at].wait()
    blocks = codes // 128
    inverse = jnp.transpose(jnp.concatenate([1.0 / counts[...]] * (128 // blocks), 0))
    for block in range(blocks):
        column = jnp.broadcast_to(inverse[:, block : block + 1], (128, 128))
        for part in range(width // 128):
            at = (slice(block * 128, block * 128 + 128), slice(part * 128, part * 128 + 128))
            codebook[at] = (sums[at] * column).astype(BF16)
    far[...] = jnp.zeros_like(far)
    arrived(featg, f_s, f_r, 0)
    f_copies[4].start()
    arrived(featg, f_s, f_r, 1)
    f_copies[5].start()
    for copy in i_copies:
        copy.start()
    near_tiles = (n // 128) * (near_spots // 128)
    step_codes = codes // near_tiles

    def near_step(tile, carry):
        near_tile(tile, 0)
        rows = pl.ds(pl.multiple_of(tile * step_codes, step_codes), step_codes)
        far[...] += dot_tn(tab_far[rows, :], codebook[rows, :])
        return carry

    lax.fori_loop(0, near_tiles, near_step, 0)
    hid[...] = dot(feat[...], ws[...])
    taken[:, 0:width] = feat[...]
    near[...] = dot_tn(tab_near[0:n, :], feat[...])
    arrived(featg, f_s, f_r, 2)
    near[...] += dot_tn(tab_near[3 * n : 4 * n, :], featg[3 * n : 4 * n, :])
    arrived(featg, f_s, f_r, 3)
    near[...] += dot_tn(tab_near[n : 2 * n, :], featg[n : 2 * n, :])
    arrived(featg, f_s, f_r, 4)
    arrived(featg, f_s, f_r, 5)

    d_copies = gather_copies(daggg, d_s, d_r)
    for at in range(2):
        rows = pl.ds(at * half, half)
        total = near[rows, :] + dot_tn(tab_near[2 * n : 3 * n, at * half : at * half + half], featg[2 * n : 3 * n, :])
        agg = (total * (1.0 / 8) + far[rows, :] * (1.0 / 16)).astype(BF16)
        taken[rows, width:] = agg
        z = hid[rows, :] + dot(agg, wn[...])
        s = jax.nn.sigmoid(z)
        out[rows, :] = (z * s).astype(BF16)
        dz = (cot[rows, :].astype(F32) * s * (1.0 + z * (1.0 - s))).astype(BF16)
        dz_all[rows, :] = dz
        daggg[rows, :] = dot_nt(dz, wn[...]).astype(BF16)
        d_copies[(0, 1)[at]].start()
        d_copies[(3, 2)[at]].start()

    wrows = ws.shape[0]
    local = dot_tn(taken[...], dz_all[...])
    wg_f[0] = local[0:wrows, :]
    wg_f[1] = local[wrows:, :]
    wg_tx[...] = wg_f[1 - core].astype(BF16)
    wa = rcopy(wg_tx, wg_rx, wa_s, wa_r, (other, y))
    wa.start()

    for at in range(3):
        i_copies[at].wait_recv()
    shard_bits = shard.bit_length() - 1
    narrow_bits = narrow.bit_length() - 1
    mine_spots = mine // 8
    mine_bits = mine_spots.bit_length() - 1
    ret_spots = n // 8
    ret_bits = ret_spots.bit_length() - 1

    def place(k):
        kw = k >> (shard_bits + narrow_bits)
        kc = kw >> 1
        step = ((((kc >> (x_chips.bit_length() - 1)) - chip_z) & (z_chips - 1)) * x_chips) | ((kc - chip_x) & (x_chips - 1))
        row = ((((kw & 1) ^ core) * chips + step) << shard_bits) | (k & (shard - 1))
        return row, ((k >> shard_bits) & (narrow - 1)) == y

    for slot in range(narrow):
        lanes = pl.ds(slot * n, n)
        block = idxg[slot].astype(I32)
        ids = block[0:8, :]
        hi_r[:, lanes] = ids & (ret_spots - 1)
        local = ids & (n - 1)
        val_r[:, lanes] = jnp.where((ids >> node_bits) == y, jnp.int32(1) << ((local >> ret_bits) * 4), 0)
        row, hit = place(block[8:24, :])
        hi_t[:, lanes] = row & (mine_spots - 1)
        val_t[:, lanes] = jnp.where(hit, jnp.int32(1) << ((row >> mine_bits) * 4), 0)
        row, hit = place(block[24:32, :])
        row_a[:, lanes] = jnp.where(hit, row, -1)

    all_rows = row_a[0:1, :]
    asn_hi[...] = jnp.where(lax.broadcasted_iota(I32, asn_hi.shape, 0) == (all_rows >> 4), 1.0, 0.0)
    asn_lo[...] = jnp.where(lax.broadcasted_iota(I32, (16, grp), 0) == (all_rows & 15), 1.0, 0.0).astype(BF16)

    def asn_part(group, carry):
        totals = [None] * 8
        for tile in range(grp // 128):
            lanes = slice(tile * 128, tile * 128 + 128)
            fits = asn_hi[pl.ds(pl.multiple_of(group * 8, 8), 8), lanes]
            low = asn_lo[:, lanes]
            for part in range(8):
                hit = jnp.broadcast_to(fits[part : part + 1, :], (16, 128)).astype(BF16) * low
                tab_asn[pl.ds(pl.multiple_of(group * 128 + part * 16, 16), 16), lanes] = hit
                totals[part] = hit if tile == 0 else totals[part] + hit
        for part in range(8):
            as_acc[pl.ds(pl.multiple_of(group * 128 + part * 16, 16), 16), :] = totals[part]
        return carry

    def code_tile(tile, carry):
        table(tab_code, hi_t, val_t, mine_spots, tile * 128, 0)
        return carry

    def ret_tile(tile, carry):
        table(tab_ret, hi_r, val_r, ret_spots, tile * 128, 0)
        return carry

    def split_count(count):
        big = jnp.floor(count * (1.0 / 256)) * 256.0
        lane = lax.broadcasted_iota(I32, count.shape, 1)
        return jnp.where(lane < 64, big, count - big).astype(BF16)

    def join_count(pair):
        pair = pair.astype(F32)
        return pair + pltpu.roll(pair, 64, 1)

    lax.fori_loop(0, mine // 512, asn_part, 0)

    wa.wait_recv()
    wg_own = wg_f[core] + wg_rx[...].astype(F32)
    wg_f[core] = wg_own
    wgb_tx[...] = wg_own.astype(BF16)
    part_rows = wrows // chips

    def wg_rows(at):
        return pl.ds(pl.multiple_of(at * part_rows, part_rows), part_rows)

    wb = {}
    for step in steps_out:
        wb[step] = rcopy(
            wgb_tx.at[wg_rows(chip_at(step)), :], wgb_rx.at[step], wb_s.at[step], wb_r.at[step], (chip_dev(step), y)
        )
        wb[step].start()
    lax.fori_loop(mine // 512, mine // 128, asn_part, 0)

    as_f[...] = jnp.zeros_like(as_f)

    def code_step(step, carry):
        code_tile(2 * step, 0)
        code_tile(2 * step + 1, 0)
        nodes = pl.ds(pl.multiple_of(step * 256, 256), 256)
        as_f[...] += dot(tab_asn[:, nodes], featg[nodes, :])
        return carry

    steps = grp // 256
    lax.fori_loop(0, steps // 2, code_step, 0)
    arrived(daggg, d_s, d_r, 0)
    d_copies[4].start()
    arrived(daggg, d_s, d_r, 1)
    d_copies[5].start()
    lax.fori_loop(steps // 2, steps, code_step, 0)

    as_cnt[...] = dot(as_acc[...], jnp.ones((128, 128), BF16))
    as_tx[:, 0:width] = as_f[own_half:, :].astype(BF16)
    as_tx[:, width:] = split_count(as_cnt[own_half:, :])
    aa = rcopy(as_tx, as_rx, aa_s, aa_r, (other, y))
    aa.start()

    for step in steps_out:
        wb[step].wait_recv()
    share = wg_f[core, wg_rows(chip), :]
    for step in steps_out:
        share = share + wgb_rx[step].astype(F32)
    wgc[0] = share
    wc = []
    for at, (peer, slot) in enumerate(((y_right, 3), (y_left, 1), (y_far, 2))):
        wc.append(rcopy(wgc.at[0], wgc.at[slot], wc_s.at[at], wc_r.at[at], (w, peer)))
        wc[-1].start()

    aa.wait_recv()
    as_f[0:own_half, :] += as_rx[:, 0:width].astype(F32)
    as_cnt[0:own_half, :] += join_count(as_rx[:, width:])
    ab = {}
    for step in steps_out:
        rows = pl.ds(step * shard, shard)
        asb_tx[step, :, 0:width] = as_f[rows, :].astype(BF16)
        asb_tx[step, :, width:] = split_count(as_cnt[rows, :])
        ab[step] = rcopy(asb_tx.at[step], asb_rx.at[step], ab_s.at[step], ab_r.at[step], (chip_dev(step), y))
        ab[step].start()

    arrived(daggg, d_s, d_r, 2)
    arrived(daggg, d_s, d_r, 3)
    acc[...] = dot(tab_code[:, 0 : 2 * n], daggg[0 : 2 * n, :]) + dot(tab_code[:, 3 * n :], daggg[3 * n :, :])
    arrived(daggg, d_s, d_r, 4)
    arrived(daggg, d_s, d_r, 5)
    last = daggg[2 * n : 3 * n, :]
    block = own_half // 2

    def finished(first):
        rows = slice(first, first + block)
        return (acc[rows, :] + dot(tab_code[rows, 2 * n : 3 * n], last)) * (1.0 / 16)

    ca = {}
    for part in (1, 0):
        rows = pl.ds(part * block, block)
        cg_tx[rows, :] = finished(own_half + part * block).astype(BF16)
        ca[part] = rcopy(cg_tx.at[rows, :], cg_rx.at[rows, :], ca_s.at[part], ca_r.at[part], (other, y))
        ca[part].start()
    for part in (1, 0):
        acc[part * block : part * block + block, :] = finished(part * block)

    for at in range(3):
        wc[at].wait_recv()

    def share_rows(at):
        return pl.ds(pl.multiple_of(core * wrows + at * part_rows, part_rows), part_rows)

    wgd[share_rows(chip), :] = (wgc[0] + wgc[1] + wgc[2] + wgc[3]).astype(BF16)
    wd = {}
    for step in steps_out:
        mine_rows = wgd.at[share_rows(chip), :]
        wd[step] = rcopy(mine_rows, mine_rows, wd_s.at[step], wd_r.at[step], (chip_dev(step), y))
        wd[step].start()

    cb = {}
    for part in (1, 0):
        ca[part].wait_recv()
        for step in steps_out:
            if step * shard // block != part:
                continue
            rows = pl.ds(step * shard, shard)
            cgb_tx[step] = (acc[rows, :] + cg_rx[rows, :].astype(F32)).astype(BF16)
            cb[step] = rcopy(cgb_tx.at[step], cgb_rx.at[step], cb_s.at[step], cb_r.at[step], (chip_dev(step), y))
            cb[step].start()

    lax.fori_loop(0, grp // 128, ret_tile, 0)
    fgrad[...] = (dot_nt(dz_all[...], ws[...]) + dot(tab_ret[...], daggg[...]) * (1.0 / 8)).astype(BF16)

    own_sum = as_f[0:shard, :]
    own_cnt = as_cnt[0:shard, :]
    for step in steps_out:
        ab[step].wait_recv()
        own_sum = own_sum + asb_rx[step, :, 0:width].astype(F32)
        own_cnt = own_cnt + join_count(asb_rx[step, :, width:])
    first = (w * narrow + y) * shard
    cnt_row = counts[pl.ds(first // 128, 1), :]
    cnt_col[...] = jnp.transpose(jnp.broadcast_to(cnt_row, (128, 128)))
    if shard <= 128:
        old_cnt = cnt_col[pl.ds(pl.multiple_of(first % 128, shard), shard), :]
    else:
        old_cnt = jnp.concatenate(
            [jnp.transpose(jnp.broadcast_to(counts[pl.ds(first // 128 + b, 1), :], (128, 128))) for b in range(shard // 128)], 0
        )
    scale = 1.0 / (decay_rate * old_cnt + (1.0 - decay_rate) * own_cnt)
    old = sums[pl.ds(pl.multiple_of(first, shard), shard), :]
    for part in range(width // 128):
        lanes = slice(part * 128, part * 128 + 128)
        newcb[:, lanes] = (decay_rate * old[:, lanes] + (1.0 - decay_rate) * own_sum[:, lanes]) * scale

    for step in steps_out:
        source = wgd.at[share_rows(chip_at(step, -1)), :]
        rcopy(source, source, wd_s.at[step], wd_r.at[step], (chip_dev(step), y)).wait_recv()
    own_rows = wgd.at[pl.ds(pl.multiple_of(core * wrows, wrows), wrows), :]
    other_rows = wgd.at[pl.ds(pl.multiple_of((1 - core) * wrows, wrows), wrows), :]
    we = rcopy(own_rows, own_rows, we_s, we_r, (other, y))
    we.start()
    rcopy(other_rows, other_rows, we_s, we_r, (other, y)).wait_recv()
    sgrad[...] = wgd[0:wrows, :].astype(F32)
    ngrad[...] = wgd[wrows:, :].astype(F32)

    own = acc[0:shard, :] + cg_rx[0:shard, :].astype(F32)
    for step in steps_out:
        cb[step].wait_recv()
        own = own + cgb_rx[step].astype(F32)
    cgrad[...] = own

    for copy in (*f_copies, *d_copies, *i_copies, wa, aa, *ca.values(), *wc, we):
        copy.wait_send()
    for step in steps_out:
        for copies in (wb, ab, wd, cb):
            copies[step].wait_send()


def copy_kernel(count, *refs):
    copies = [pltpu.make_async_copy(refs[at], refs[count + at], refs[-1].at[at]) for at in range(count)]
    for copy in copies:
        copy.start()
    for copy in copies:
        copy.wait()


def on_device(
    wide, narrow,
    features, neighbours, code_ids, assignment, cotangent, code_sums, code_counts, self_weight, neighbour_weight,
):
    n, width = features.shape
    codes = code_sums.shape[0]
    chips = wide // 2
    shard = codes // (wide * narrow)
    mine = codes // narrow
    grp = n * narrow
    hbm = pl.BlockSpec(memory_space=pltpu.HBM)
    dma = pltpu.SemaphoreType.DMA
    wide_rows = self_weight.shape[0]
    scratch = [
        pltpu.VMEM((n, width), BF16),
        pltpu.VMEM((codes, width), F32),
        pltpu.VMEM((codes // 128, 128), F32),
        pltpu.VMEM(self_weight.shape, BF16),
        pltpu.VMEM(neighbour_weight.shape, BF16),
        pltpu.VMEM((codes, width), BF16),
        pltpu.VMEM((grp, width), BF16),
        pltpu.VMEM((grp, width), BF16),
        pltpu.VMEM((IDX_ROWS, n), I32),
        pltpu.VMEM((narrow, IDX_ROWS, n), jnp.int16),
        pltpu.VMEM((codes, n), BF16),
        pltpu.VMEM((grp, n), BF16),
        pltpu.VMEM((mine, grp), BF16),
        pltpu.VMEM((n, grp), BF16),
        pltpu.VMEM((mine, grp), BF16),
        pltpu.VMEM((16, n), I32),
        pltpu.VMEM((16, n), I32),
        pltpu.VMEM((8, n), I32),
        pltpu.VMEM((8, n), I32),
        pltpu.VMEM((16, grp), I32),
        pltpu.VMEM((16, grp), I32),
        pltpu.VMEM((8, grp), I32),
        pltpu.VMEM((8, grp), I32),
        pltpu.VMEM((8, grp), I32),
        pltpu.VMEM((mine // 16, grp), F32),
        pltpu.VMEM((16, grp), BF16),
        pltpu.VMEM((n, width), F32),
        pltpu.VMEM((n, width), F32),
        pltpu.VMEM((n, width), F32),
        pltpu.VMEM((n, width), BF16),
        pltpu.VMEM((n, 2 * width), BF16),
        pltpu.VMEM((mine, width), F32),
        pltpu.VMEM((2, wide_rows, width), F32),
        pltpu.VMEM((wide_rows, width), BF16),
        pltpu.VMEM((wide_rows, width), BF16),
        pltpu.VMEM((wide_rows, width), BF16),
        pltpu.VMEM((chips, wide_rows // chips, width), BF16),
        pltpu.VMEM((narrow, wide_rows // chips, width), F32),
        pltpu.VMEM((2 * wide_rows, width), BF16),
        pltpu.VMEM((mine, width), F32),
        pltpu.VMEM((mine, 128), F32),
        pltpu.VMEM((mine, 128), BF16),
        pltpu.VMEM((mine // 2, width + 128), BF16),
        pltpu.VMEM((mine // 2, width + 128), BF16),
        pltpu.VMEM((chips, shard, width + 128), BF16),
        pltpu.VMEM((chips, shard, width + 128), BF16),
        pltpu.VMEM((mine // 2, width), BF16),
        pltpu.VMEM((mine // 2, width), BF16),
        pltpu.VMEM((chips, shard, width), BF16),
        pltpu.VMEM((chips, shard, width), BF16),
        pltpu.VMEM((128, 128), F32),
        dma((9,)),
        dma((6,)), dma((6,)), dma((6,)), dma((6,)), dma((3,)), dma((3,)),
        dma, dma, dma((chips,)), dma((chips,)), dma((3,)), dma((3,)), dma((chips,)), dma((chips,)), dma, dma,
        dma, dma, dma((chips,)), dma((chips,)), dma((2,)), dma((2,)), dma((chips,)), dma((chips,)),
    ]
    shapes = (
        jax.ShapeDtypeStruct((n, width), BF16),
        jax.ShapeDtypeStruct((n, width), BF16),
        jax.ShapeDtypeStruct(self_weight.shape, F32),
        jax.ShapeDtypeStruct(neighbour_weight.shape, F32),
        jax.ShapeDtypeStruct((shard, width), F32),
        jax.ShapeDtypeStruct((shard, width), F32),
    )
    vm = pl.BlockSpec(memory_space=pltpu.VMEM)
    operands = (
        features, neighbours.T, code_ids.T, assignment.reshape(1, n), cotangent,
        code_sums, code_counts.reshape(codes // 128, 128), self_weight, neighbour_weight,
    )
    results = pl.pallas_call(
        functools.partial(kernel, wide, narrow, shard),
        out_shape=tuple(pltpu.VMEM(shape.shape, shape.dtype) for shape in shapes),
        in_specs=[hbm] * 9,
        out_specs=(vm,) * 6,
        scratch_shapes=scratch,
        compiler_params=pltpu.CompilerParams(
            collective_id=0, has_side_effects=True, vmem_limit_bytes=48 * 1024 * 1024
        ),
    )(*(pltpu.with_memory_space_constraint(operand, pltpu.HBM) for operand in operands))
    return pl.pallas_call(
        functools.partial(copy_kernel, len(shapes)),
        out_shape=shapes,
        in_specs=[vm] * 6,
        out_specs=(hbm,) * 6,
        scratch_shapes=[dma((6,))],
        compiler_params=pltpu.CompilerParams(vmem_limit_bytes=8 * 1024 * 1024),
    )(*results)


def solution(mesh):
    both = ("wide", "narrow")
    return jax.shard_map(
        functools.partial(on_device, mesh.shape["wide"], mesh.shape["narrow"]),
        mesh=mesh,
        in_specs=(P(both, None), P(both, None), P(both, None), P(both), P(both, None), P(), P(), P(), P()),
        out_specs=(P(both, None), P(both, None), P(), P(), P(both, None), P(both, None)),
        check_vma=False,
    )
```

```python
import functools

import jax
import jax.numpy as jnp
from jax import lax
from jax.experimental import pallas as pl
from jax.experimental.pallas import tpu as pltpu
from jax.sharding import PartitionSpec as P

MESH = pl.DeviceIdType.MESH
F32, BF16, I32 = jnp.float32, jnp.bfloat16, jnp.int32
decay_rate = 0.5
IDX_ROWS = 32
NIBBLES = 0x0F0F0F0F


def dot(a, b):
    return jnp.dot(a, b, preferred_element_type=F32)


def dot_nt(a, b):
    return lax.dot_general(a, b, (((1,), (1,)), ((), ())), preferred_element_type=F32)


def dot_tn(a, b):
    return lax.dot_general(a, b, (((0,), (0,)), ((), ())), preferred_element_type=F32)


def words_of(spots, his, vals):
    word = None
    for hi, val in zip(his, vals):
        term = jnp.where(spots == hi, val, 0)
        word = term if word is None else word + term
    return word


def fields_of(words):
    even = odd = None
    for word in words:
        low, high = word & NIBBLES, (word >> 4) & NIBBLES
        even = low if even is None else even + low
        odd = high if odd is None else odd + high
    out = []
    for field in range(8):
        part = (even, odd)[field % 2]
        shift = 8 * (field // 2)
        if shift:
            part = part >> shift
        if shift < 24:
            part = part & 255
        out.append(part.astype(F32).astype(BF16))
    return out


def kernel(
    wide, narrow, shard,
    feat_hbm, nb_hbm, code_hbm, assign_hbm, cot_hbm, sums_hbm, counts_hbm, ws_hbm, wn_hbm,
    out, fgrad, sgrad, ngrad, newcb, cgrad,
    cot, sums, counts, ws, wn,
    codebook, featg, daggg, idx_own, idxg, tab_far, tab_near, tab_code, tab_ret, tab_asn,
    hi_f, val_f, hi_n, val_n, hi_t, val_t, hi_r, val_r, row_a, asn_hi, asn_lo, far, near, hid, dz_all, taken, acc,
    wg_f, wg_tx, wg_rx, wgb_tx, wgb_rx, wgc, wgd, as_f, as_cnt, as_acc, as_tx, as_rx, asb_tx, asb_rx,
    cg_tx, cg_rx, cgb_tx, cgb_rx, cnt_col,
    in_sem, f_s, f_r, d_s, d_r, i_s, i_r, wa_s, wa_r, wb_s, wb_r, wc_s, wc_r, wd_s, wd_r, we_s, we_r,
    aa_s, aa_r, ab_s, ab_r, ca_s, ca_r, cb_s, cb_r,
):
    n = cot.shape[0]
    half = n // 2
    chips = wide // 2
    codes = sums.shape[0]
    mine = codes // narrow
    own_half = mine // 2
    grp = n * narrow
    w = lax.axis_index("wide")
    y = lax.axis_index("narrow")
    core = w % 2
    chip = w // 2
    y_right, y_left, y_far = (y + 1) % narrow, (y + 3) % narrow, (y + 2) % narrow
    other = chip * 2 + (1 - core)

    x_chips = min(4, chips)
    z_chips = chips // x_chips
    chip_z, chip_x = chip // x_chips, chip % x_chips

    def chip_at(step, sign=1):
        step_z, step_x = step // x_chips, step % x_chips
        at_z = (chip_z + (step_z if sign > 0 else z_chips - step_z)) % z_chips
        at_x = (chip_x + (step_x if sign > 0 else x_chips - step_x)) % x_chips
        return at_z * x_chips + at_x

    def chip_dev(step):
        return chip_at(step) * 2 + core

    def hops(step):
        step_z, step_x = step // x_chips, step % x_chips
        return min(step_z, z_chips - step_z) + min(step_x, x_chips - step_x)

    steps_out = sorted(range(1, chips), key=lambda step: -hops(step))

    def rcopy(src, dst, ssem, rsem, dev):
        return pltpu.make_async_remote_copy(
            src_ref=src, dst_ref=dst, send_sem=ssem, recv_sem=rsem, device_id=dev, device_id_type=MESH
        )

    feat = featg.at[pl.ds(0, n), :]
    idx_own[24:32, :] = jnp.zeros((8, n), I32)
    fetched = [
        pltpu.make_async_copy(src, dst, in_sem.at[at])
        for at, (src, dst) in enumerate(
            (
                (feat_hbm, feat),
                (nb_hbm, idx_own.at[pl.ds(0, 8), :]),
                (code_hbm, idx_own.at[pl.ds(8, 16), :]),
                (assign_hbm, idx_own.at[pl.ds(24, 1), :]),
                (counts_hbm, counts),
                (sums_hbm, sums),
                (ws_hbm, ws),
                (wn_hbm, wn),
                (cot_hbm, cot),
            )
        )
    ]
    for copy in fetched:
        copy.start()

    barrier = pltpu.get_barrier_semaphore()
    for peer in (y_right, y_left, y_far):
        pl.semaphore_signal(barrier, inc=1, device_id=(w, peer), device_id_type=MESH)

    for peer in (*(chip_dev(step) for step in steps_out), other):
        pl.semaphore_signal(barrier, inc=1, device_id=(peer, y), device_id_type=MESH)
    for at in range(4):
        fetched[at].wait()
    pl.semaphore_wait(barrier, narrow - 1 + chips)

    def low(slot):
        return pl.ds(slot * n, half)

    def high(slot):
        return pl.ds(slot * n + half, half)

    def gather_copies(buf, ssem, rsem):
        right, left = (w, y_right), (w, y_left)

        def make(src, dst, at, dev):
            return rcopy(buf.at[src, :], buf.at[dst, :], ssem.at[at], rsem.at[at], dev)

        return (
            make(low(0), low(3), 0, right),
            make(high(0), high(1), 1, left),
            make(high(0), high(3), 2, right),
            make(low(0), low(1), 3, left),
            make(low(3), low(2), 4, right),
            make(high(1), high(2), 5, left),
        )

    def arrived(buf, ssem, rsem, at):
        region = (low(3), high(1), high(3), low(1), low(2), high(2))[at]
        rcopy(buf.at[region, :], buf.at[region, :], ssem.at[at], rsem.at[at], (w, y_right)).wait_recv()

    f_copies = gather_copies(featg, f_s, f_r)
    for at in range(4):
        f_copies[at].start()
    idxg[0] = idx_own[...].astype(jnp.int16)
    i_copies = [
        rcopy(idxg.at[0], idxg.at[slot], i_s.at[at], i_r.at[at], (w, peer))
        for at, (peer, slot) in enumerate(((y_right, 3), (y_left, 1), (y_far, 2)))
    ]

    def table(tab, his_ref, vals_ref, spots_in, lane_at, first_spot):
        lanes = pl.ds(pl.multiple_of(lane_at, 128), 128)
        picks = his_ref.shape[0]
        his = [jnp.broadcast_to(his_ref[j : j + 1, lanes], (16, 128)) for j in range(picks)]
        vals = [jnp.broadcast_to(vals_ref[j : j + 1, lanes], (16, 128)) for j in range(picks)]
        base = lax.broadcasted_iota(I32, (16, 128), 0) + first_spot
        for part in range(min(spots_in, 128) // 16):
            spots = base + part * 16
            words = [words_of(spots, his[at : at + 8], vals[at : at + 8]) for at in range(0, picks, 8)]
            for field, counts_part in enumerate(fields_of(words)):
                row = pl.multiple_of(field * spots_in + part * 16 + first_spot, 16)
                tab[pl.ds(row, 16), lanes] = counts_part

    far_spots = codes // 8
    far_bits = far_spots.bit_length() - 1
    near_spots = grp // 8
    near_bits = near_spots.bit_length() - 1
    node_bits = n.bit_length() - 1
    own_ids = idx_own[8:24, :]
    hi_f[...] = own_ids & (far_spots - 1)
    val_f[...] = jnp.int32(1) << ((own_ids >> far_bits) * 4)
    own_ids = idx_own[0:8, :]
    own_ids = ((((own_ids >> node_bits) - y) & (narrow - 1)) << node_bits) | (own_ids & (n - 1))
    hi_n[...] = own_ids & (near_spots - 1)
    val_n[...] = jnp.int32(1) << ((own_ids >> near_bits) * 4)

    def far_tile(tile, carry):
        table(tab_far, hi_f, val_f, far_spots, (tile // (far_spots // 128)) * 128, (tile % (far_spots // 128)) * 128)
        return carry

    def near_tile(tile, carry):
        table(tab_near, hi_n, val_n, near_spots, (tile // (near_spots // 128)) * 128, (tile % (near_spots // 128)) * 128)
        return carry

    far_tiles = (n // 128) * (far_spots // 128)
    lax.fori_loop(0, far_tiles, far_tile, 0)
    width = sums.shape[1]
    for at in range(4, 9):
        fetched[at].wait()
    blocks = codes // 128
    inverse = jnp.transpose(jnp.concatenate([1.0 / counts[...]] * (128 // blocks), 0))
    for block in range(blocks):
        column = jnp.broadcast_to(inverse[:, block : block + 1], (128, 128))
        for part in range(width // 128):
            at = (slice(block * 128, block * 128 + 128), slice(part * 128, part * 128 + 128))
            codebook[at] = (sums[at] * column).astype(BF16)
    far[...] = jnp.zeros_like(far)
    arrived(featg, f_s, f_r, 0)
    f_copies[4].start()
    arrived(featg, f_s, f_r, 1)
    f_copies[5].start()
    for copy in i_copies:
        copy.start()
    near_tiles = (n // 128) * (near_spots // 128)
    step_codes = codes // near_tiles

    def near_step(tile, carry):
        near_tile(tile, 0)
        rows = pl.ds(pl.multiple_of(tile * step_codes, step_codes), step_codes)
        far[...] += dot_tn(tab_far[rows, :], codebook[rows, :])
        return carry

    lax.fori_loop(0, near_tiles, near_step, 0)
    for kw in range(wide):
        kc = kw // 2
        step = ((kc // x_chips + z_chips - chip_z) % z_chips) * x_chips + (kc % x_chips + x_chips - chip_x) % x_chips
        to = ((kw + core) % 2) * own_half + step * shard
        rows = pl.ds(pl.multiple_of((kw * narrow + y) * shard, shard), shard)
        tab_code[pl.ds(pl.multiple_of(to, shard), shard), 0:n] = tab_far[rows, :]
    hid[...] = dot(feat[...], ws[...])
    taken[:, 0:width] = feat[...]
    near[...] = dot_tn(tab_near[0:n, :], feat[...])
    arrived(featg, f_s, f_r, 2)
    near[...] += dot_tn(tab_near[3 * n : 4 * n, :], featg[3 * n : 4 * n, :])
    arrived(featg, f_s, f_r, 3)
    near[...] += dot_tn(tab_near[n : 2 * n, :], featg[n : 2 * n, :])
    arrived(featg, f_s, f_r, 4)
    arrived(featg, f_s, f_r, 5)

    d_copies = gather_copies(daggg, d_s, d_r)
    for at in range(2):
        rows = pl.ds(at * half, half)
        total = near[rows, :] + dot_tn(tab_near[2 * n : 3 * n, at * half : at * half + half], featg[2 * n : 3 * n, :])
        agg = (total * (1.0 / 8) + far[rows, :] * (1.0 / 16)).astype(BF16)
        taken[rows, width:] = agg
        z = hid[rows, :] + dot(agg, wn[...])
        s = jax.nn.sigmoid(z)
        out[rows, :] = (z * s).astype(BF16)
        dz = (cot[rows, :].astype(F32) * s * (1.0 + z * (1.0 - s))).astype(BF16)
        dz_all[rows, :] = dz
        daggg[rows, :] = dot_nt(dz, wn[...]).astype(BF16)
        d_copies[(0, 1)[at]].start()
        d_copies[(3, 2)[at]].start()

    wrows = ws.shape[0]
    local = dot_tn(taken[...], dz_all[...])
    wg_f[0] = local[0:wrows, :]
    wg_f[1] = local[wrows:, :]
    wg_tx[...] = wg_f[1 - core].astype(BF16)
    wa = rcopy(wg_tx, wg_rx, wa_s, wa_r, (other, y))
    wa.start()

    for at in range(3):
        i_copies[at].wait_recv()
    shard_bits = shard.bit_length() - 1
    narrow_bits = narrow.bit_length() - 1
    mine_spots = mine // 8
    mine_bits = mine_spots.bit_length() - 1
    ret_spots = n // 8
    ret_bits = ret_spots.bit_length() - 1

    def place(k):
        kw = k >> (shard_bits + narrow_bits)
        kc = kw >> 1
        step = ((((kc >> (x_chips.bit_length() - 1)) - chip_z) & (z_chips - 1)) * x_chips) | ((kc - chip_x) & (x_chips - 1))
        row = ((((kw & 1) ^ core) * chips + step) << shard_bits) | (k & (shard - 1))
        return row, ((k >> shard_bits) & (narrow - 1)) == y

    for slot in range(narrow):
        lanes = pl.ds(slot * n, n)
        block = idxg[slot].astype(I32)
        ids = block[0:8, :]
        hi_r[:, lanes] = ids & (ret_spots - 1)
        local = ids & (n - 1)
        val_r[:, lanes] = jnp.where((ids >> node_bits) == y, jnp.int32(1) << ((local >> ret_bits) * 4), 0)
        row, hit = place(block[8:24, :])
        hi_t[:, lanes] = row & (mine_spots - 1)
        val_t[:, lanes] = jnp.where(hit, jnp.int32(1) << ((row >> mine_bits) * 4), 0)
        row, hit = place(block[24:32, :])
        row_a[:, lanes] = jnp.where(hit, row, -1)

    all_rows = row_a[0:1, :]
    asn_hi[...] = jnp.where(lax.broadcasted_iota(I32, asn_hi.shape, 0) == (all_rows >> 4), 1.0, 0.0)
    asn_lo[...] = jnp.where(lax.broadcasted_iota(I32, (16, grp), 0) == (all_rows & 15), 1.0, 0.0).astype(BF16)

    def asn_part(group, carry):
        totals = [None] * 8
        for tile in range(grp // 128):
            lanes = slice(tile * 128, tile * 128 + 128)
            fits = asn_hi[pl.ds(pl.multiple_of(group * 8, 8), 8), lanes]
            low = asn_lo[:, lanes]
            for part in range(8):
                hit = jnp.broadcast_to(fits[part : part + 1, :], (16, 128)).astype(BF16) * low
                tab_asn[pl.ds(pl.multiple_of(group * 128 + part * 16, 16), 16), lanes] = hit
                totals[part] = hit if tile == 0 else totals[part] + hit
        for part in range(8):
            as_acc[pl.ds(pl.multiple_of(group * 128 + part * 16, 16), 16), :] = totals[part]
        return carry

    def code_tile(tile, carry):
        table(tab_code, hi_t, val_t, mine_spots, tile * 128, 0)
        return carry

    def ret_tile(tile, carry):
        table(tab_ret, hi_r, val_r, ret_spots, tile * 128, 0)
        return carry

    def split_count(count):
        big = jnp.floor(count * (1.0 / 256)) * 256.0
        lane = lax.broadcasted_iota(I32, count.shape, 1)
        return jnp.where(lane < 64, big, count - big).astype(BF16)

    def join_count(pair):
        pair = pair.astype(F32)
        return pair + pltpu.roll(pair, 64, 1)

    def assigned(first):
        rows = pl.ds(first, own_half)
        lax.fori_loop(first // 128, (first + own_half) // 128, asn_part, 0)
        as_f[rows, :] = dot(tab_asn[rows, :], featg[...])
        as_cnt[rows, :] = dot(as_acc[rows, :], jnp.ones((128, 128), BF16))

    assigned(own_half)
    as_tx[:, 0:width] = as_f[own_half:, :].astype(BF16)
    as_tx[:, width:] = split_count(as_cnt[own_half:, :])
    aa = rcopy(as_tx, as_rx, aa_s, aa_r, (other, y))
    aa.start()

    wa.wait_recv()
    wg_own = wg_f[core] + wg_rx[...].astype(F32)
    wg_f[core] = wg_own
    wgb_tx[...] = wg_own.astype(BF16)
    part_rows = wrows // chips

    def wg_rows(at):
        return pl.ds(pl.multiple_of(at * part_rows, part_rows), part_rows)

    wb = {}
    for step in steps_out:
        wb[step] = rcopy(
            wgb_tx.at[wg_rows(chip_at(step)), :], wgb_rx.at[step], wb_s.at[step], wb_r.at[step], (chip_dev(step), y)
        )
        wb[step].start()
    assigned(0)

    aa.wait_recv()
    as_f[0:own_half, :] += as_rx[:, 0:width].astype(F32)
    as_cnt[0:own_half, :] += join_count(as_rx[:, width:])
    ab = {}
    for step in steps_out:
        rows = pl.ds(step * shard, shard)
        asb_tx[step, :, 0:width] = as_f[rows, :].astype(BF16)
        asb_tx[step, :, width:] = split_count(as_cnt[rows, :])
        ab[step] = rcopy(asb_tx.at[step], asb_rx.at[step], ab_s.at[step], ab_r.at[step], (chip_dev(step), y))
        ab[step].start()

    first_tile, tiles = n // 128, grp // 128
    middle = (first_tile + tiles) // 2
    lax.fori_loop(first_tile, middle, code_tile, 0)
    arrived(daggg, d_s, d_r, 0)
    d_copies[4].start()
    arrived(daggg, d_s, d_r, 1)
    d_copies[5].start()
    lax.fori_loop(middle, tiles, code_tile, 0)

    for step in steps_out:
        wb[step].wait_recv()
    share = wg_f[core, wg_rows(chip), :]
    for step in steps_out:
        share = share + wgb_rx[step].astype(F32)
    wgc[0] = share
    wc = []
    for at, (peer, slot) in enumerate(((y_right, 3), (y_left, 1), (y_far, 2))):
        wc.append(rcopy(wgc.at[0], wgc.at[slot], wc_s.at[at], wc_r.at[at], (w, peer)))
        wc[-1].start()

    arrived(daggg, d_s, d_r, 2)
    arrived(daggg, d_s, d_r, 3)
    acc[...] = dot(tab_code[:, 0 : 2 * n], daggg[0 : 2 * n, :]) + dot(tab_code[:, 3 * n :], daggg[3 * n :, :])
    arrived(daggg, d_s, d_r, 4)
    arrived(daggg, d_s, d_r, 5)
    last = daggg[2 * n : 3 * n, :]
    block = own_half // 2

    def finished(first):
        rows = slice(first, first + block)
        return (acc[rows, :] + dot(tab_code[rows, 2 * n : 3 * n], last)) * (1.0 / 16)

    ca = {}
    for part in (1, 0):
        rows = pl.ds(part * block, block)
        cg_tx[rows, :] = finished(own_half + part * block).astype(BF16)
        ca[part] = rcopy(cg_tx.at[rows, :], cg_rx.at[rows, :], ca_s.at[part], ca_r.at[part], (other, y))
        ca[part].start()
    for part in (1, 0):
        acc[part * block : part * block + block, :] = finished(part * block)

    for at in range(3):
        wc[at].wait_recv()

    def share_rows(at):
        return pl.ds(pl.multiple_of(core * wrows + at * part_rows, part_rows), part_rows)

    wgd[share_rows(chip), :] = (wgc[0] + wgc[1] + wgc[2] + wgc[3]).astype(BF16)
    wd = {}
    for step in steps_out:
        mine_rows = wgd.at[share_rows(chip), :]
        wd[step] = rcopy(mine_rows, mine_rows, wd_s.at[step], wd_r.at[step], (chip_dev(step), y))
        wd[step].start()

    cb = {}
    for part in (1, 0):
        ca[part].wait_recv()
        for step in steps_out:
            if step * shard // block != part:
                continue
            rows = pl.ds(step * shard, shard)
            cgb_tx[step] = (acc[rows, :] + cg_rx[rows, :].astype(F32)).astype(BF16)
            cb[step] = rcopy(cgb_tx.at[step], cgb_rx.at[step], cb_s.at[step], cb_r.at[step], (chip_dev(step), y))
            cb[step].start()

    lax.fori_loop(0, grp // 128, ret_tile, 0)
    fgrad[...] = (dot_nt(dz_all[...], ws[...]) + dot(tab_ret[...], daggg[...]) * (1.0 / 8)).astype(BF16)

    own_sum = as_f[0:shard, :]
    own_cnt = as_cnt[0:shard, :]
    for step in steps_out:
        ab[step].wait_recv()
        own_sum = own_sum + asb_rx[step, :, 0:width].astype(F32)
        own_cnt = own_cnt + join_count(asb_rx[step, :, width:])
    first = (w * narrow + y) * shard
    cnt_row = counts[pl.ds(first // 128, 1), :]
    cnt_col[...] = jnp.transpose(jnp.broadcast_to(cnt_row, (128, 128)))
    if shard <= 128:
        old_cnt = cnt_col[pl.ds(pl.multiple_of(first % 128, shard), shard), :]
    else:
        old_cnt = jnp.concatenate(
            [jnp.transpose(jnp.broadcast_to(counts[pl.ds(first // 128 + b, 1), :], (128, 128))) for b in range(shard // 128)], 0
        )
    scale = 1.0 / (decay_rate * old_cnt + (1.0 - decay_rate) * own_cnt)
    old = sums[pl.ds(pl.multiple_of(first, shard), shard), :]
    for part in range(width // 128):
        lanes = slice(part * 128, part * 128 + 128)
        newcb[:, lanes] = (decay_rate * old[:, lanes] + (1.0 - decay_rate) * own_sum[:, lanes]) * scale

    for step in steps_out:
        source = wgd.at[share_rows(chip_at(step, -1)), :]
        rcopy(source, source, wd_s.at[step], wd_r.at[step], (chip_dev(step), y)).wait_recv()
    own_rows = wgd.at[pl.ds(pl.multiple_of(core * wrows, wrows), wrows), :]
    other_rows = wgd.at[pl.ds(pl.multiple_of((1 - core) * wrows, wrows), wrows), :]
    we = rcopy(own_rows, own_rows, we_s, we_r, (other, y))
    we.start()
    rcopy(other_rows, other_rows, we_s, we_r, (other, y)).wait_recv()
    sgrad[...] = wgd[0:wrows, :].astype(F32)
    ngrad[...] = wgd[wrows:, :].astype(F32)

    own = acc[0:shard, :] + cg_rx[0:shard, :].astype(F32)
    for step in steps_out:
        cb[step].wait_recv()
        own = own + cgb_rx[step].astype(F32)
    cgrad[...] = own

    for copy in (*f_copies, *d_copies, *i_copies, wa, aa, *ca.values(), *wc, we):
        copy.wait_send()
    for step in steps_out:
        for copies in (wb, ab, wd, cb):
            copies[step].wait_send()


def copy_kernel(count, *refs):
    copies = [pltpu.make_async_copy(refs[at], refs[count + at], refs[-1].at[at]) for at in range(count)]
    for copy in copies:
        copy.start()
    for copy in copies:
        copy.wait()


def on_device(
    wide, narrow,
    features, neighbours, code_ids, assignment, cotangent, code_sums, code_counts, self_weight, neighbour_weight,
):
    n, width = features.shape
    codes = code_sums.shape[0]
    chips = wide // 2
    shard = codes // (wide * narrow)
    mine = codes // narrow
    grp = n * narrow
    hbm = pl.BlockSpec(memory_space=pltpu.HBM)
    dma = pltpu.SemaphoreType.DMA
    wide_rows = self_weight.shape[0]
    scratch = [
        pltpu.VMEM((n, width), BF16),
        pltpu.VMEM((codes, width), F32),
        pltpu.VMEM((codes // 128, 128), F32),
        pltpu.VMEM(self_weight.shape, BF16),
        pltpu.VMEM(neighbour_weight.shape, BF16),
        pltpu.VMEM((codes, width), BF16),
        pltpu.VMEM((grp, width), BF16),
        pltpu.VMEM((grp, width), BF16),
        pltpu.VMEM((IDX_ROWS, n), I32),
        pltpu.VMEM((narrow, IDX_ROWS, n), jnp.int16),
        pltpu.VMEM((codes, n), BF16),
        pltpu.VMEM((grp, n), BF16),
        pltpu.VMEM((mine, grp), BF16),
        pltpu.VMEM((n, grp), BF16),
        pltpu.VMEM((mine, grp), BF16),
        pltpu.VMEM((16, n), I32),
        pltpu.VMEM((16, n), I32),
        pltpu.VMEM((8, n), I32),
        pltpu.VMEM((8, n), I32),
        pltpu.VMEM((16, grp), I32),
        pltpu.VMEM((16, grp), I32),
        pltpu.VMEM((8, grp), I32),
        pltpu.VMEM((8, grp), I32),
        pltpu.VMEM((8, grp), I32),
        pltpu.VMEM((mine // 16, grp), F32),
        pltpu.VMEM((16, grp), BF16),
        pltpu.VMEM((n, width), F32),
        pltpu.VMEM((n, width), F32),
        pltpu.VMEM((n, width), F32),
        pltpu.VMEM((n, width), BF16),
        pltpu.VMEM((n, 2 * width), BF16),
        pltpu.VMEM((mine, width), F32),
        pltpu.VMEM((2, wide_rows, width), F32),
        pltpu.VMEM((wide_rows, width), BF16),
        pltpu.VMEM((wide_rows, width), BF16),
        pltpu.VMEM((wide_rows, width), BF16),
        pltpu.VMEM((chips, wide_rows // chips, width), BF16),
        pltpu.VMEM((narrow, wide_rows // chips, width), F32),
        pltpu.VMEM((2 * wide_rows, width), BF16),
        pltpu.VMEM((mine, width), F32),
        pltpu.VMEM((mine, 128), F32),
        pltpu.VMEM((mine, 128), BF16),
        pltpu.VMEM((mine // 2, width + 128), BF16),
        pltpu.VMEM((mine // 2, width + 128), BF16),
        pltpu.VMEM((chips, shard, width + 128), BF16),
        pltpu.VMEM((chips, shard, width + 128), BF16),
        pltpu.VMEM((mine // 2, width), BF16),
        pltpu.VMEM((mine // 2, width), BF16),
        pltpu.VMEM((chips, shard, width), BF16),
        pltpu.VMEM((chips, shard, width), BF16),
        pltpu.VMEM((128, 128), F32),
        dma((9,)),
        dma((6,)), dma((6,)), dma((6,)), dma((6,)), dma((3,)), dma((3,)),
        dma, dma, dma((chips,)), dma((chips,)), dma((3,)), dma((3,)), dma((chips,)), dma((chips,)), dma, dma,
        dma, dma, dma((chips,)), dma((chips,)), dma((2,)), dma((2,)), dma((chips,)), dma((chips,)),
    ]
    shapes = (
        jax.ShapeDtypeStruct((n, width), BF16),
        jax.ShapeDtypeStruct((n, width), BF16),
        jax.ShapeDtypeStruct(self_weight.shape, F32),
        jax.ShapeDtypeStruct(neighbour_weight.shape, F32),
        jax.ShapeDtypeStruct((shard, width), F32),
        jax.ShapeDtypeStruct((shard, width), F32),
    )
    vm = pl.BlockSpec(memory_space=pltpu.VMEM)
    operands = (
        features, neighbours.T, code_ids.T, assignment.reshape(1, n), cotangent,
        code_sums, code_counts.reshape(codes // 128, 128), self_weight, neighbour_weight,
    )
    results = pl.pallas_call(
        functools.partial(kernel, wide, narrow, shard),
        out_shape=tuple(pltpu.VMEM(shape.shape, shape.dtype) for shape in shapes),
        in_specs=[hbm] * 9,
        out_specs=(vm,) * 6,
        scratch_shapes=scratch,
        compiler_params=pltpu.CompilerParams(
            collective_id=0, has_side_effects=True, vmem_limit_bytes=48 * 1024 * 1024
        ),
    )(*(pltpu.with_memory_space_constraint(operand, pltpu.HBM) for operand in operands))
    return pl.pallas_call(
        functools.partial(copy_kernel, len(shapes)),
        out_shape=shapes,
        in_specs=[vm] * 6,
        out_specs=(hbm,) * 6,
        scratch_shapes=[dma((6,))],
        compiler_params=pltpu.CompilerParams(vmem_limit_bytes=8 * 1024 * 1024),
    )(*results)


def solution(mesh):
    both = ("wide", "narrow")
    return jax.shard_map(
        functools.partial(on_device, mesh.shape["wide"], mesh.shape["narrow"]),
        mesh=mesh,
        in_specs=(P(both, None), P(both, None), P(both, None), P(both), P(both, None), P(), P(), P(), P()),
        out_specs=(P(both, None), P(both, None), P(), P(), P(both, None), P(both, None)),
        check_vma=False,
    )
```

```python
import functools

import jax
import jax.numpy as jnp
from jax import lax
from jax.experimental import pallas as pl
from jax.experimental.pallas import tpu as pltpu
from jax.sharding import PartitionSpec as P

MESH = pl.DeviceIdType.MESH
F32, BF16, I32 = jnp.float32, jnp.bfloat16, jnp.int32
decay_rate = 0.5
IDX_ROWS = 32
NIBBLES = 0x0F0F0F0F


def dot(a, b):
    return jnp.dot(a, b, preferred_element_type=F32)


def dot_nt(a, b):
    return lax.dot_general(a, b, (((1,), (1,)), ((), ())), preferred_element_type=F32)


def dot_tn(a, b):
    return lax.dot_general(a, b, (((0,), (0,)), ((), ())), preferred_element_type=F32)


def words_of(spots, his, vals):
    word = None
    for hi, val in zip(his, vals):
        term = jnp.where(spots == hi, val, 0)
        word = term if word is None else word + term
    return word


def fields_of(words):
    even = odd = None
    for word in words:
        low, high = word & NIBBLES, (word >> 4) & NIBBLES
        even = low if even is None else even + low
        odd = high if odd is None else odd + high
    out = []
    for field in range(8):
        part = (even, odd)[field % 2]
        shift = 8 * (field // 2)
        if shift:
            part = part >> shift
        if shift < 24:
            part = part & 255
        out.append(part.astype(F32).astype(BF16))
    return out


def kernel(
    wide, narrow, shard,
    feat_hbm, nb_hbm, code_hbm, assign_hbm, cot_hbm, sums_hbm, counts_hbm, ws_hbm, wn_hbm,
    out, fgrad, sgrad, ngrad, newcb, cgrad,
    cot, sums, counts, ws, wn,
    codebook, featg, daggg, idx_own, idxg, asg, tab_far, tab_near, tab_code, tab_ret, tab_asn,
    hi_f, val_f, hi_n, val_n, hi_t, val_t, hi_r, val_r, row_a, asn_hi, asn_lo, far, near, hid, dz_all, taken, acc,
    wg_f, wg_tx, wg_rx, wgb_tx, wgb_rx, wgc, wgd, as_f, as_cnt, as_acc, as_tx, as_rx, asb_tx, asb_rx,
    cg_tx, cg_rx, cgb_tx, cgb_rx, cnt_col,
    in_sem, f_s, f_r, d_s, d_r, i_s, i_r, g_s, g_r, wa_s, wa_r, wb_s, wb_r, wc_s, wc_r, wd_s, wd_r, we_s, we_r,
    aa_s, aa_r, ab_s, ab_r, ca_s, ca_r, cb_s, cb_r,
):
    n = cot.shape[0]
    half = n // 2
    chips = wide // 2
    codes = sums.shape[0]
    mine = codes // narrow
    own_half = mine // 2
    grp = n * narrow
    w = lax.axis_index("wide")
    y = lax.axis_index("narrow")
    core = w % 2
    chip = w // 2
    y_right, y_left, y_far = (y + 1) % narrow, (y + 3) % narrow, (y + 2) % narrow
    other = chip * 2 + (1 - core)

    x_chips = min(4, chips)
    z_chips = chips // x_chips
    chip_z, chip_x = chip // x_chips, chip % x_chips

    def chip_at(step, sign=1):
        step_z, step_x = step // x_chips, step % x_chips
        at_z = (chip_z + (step_z if sign > 0 else z_chips - step_z)) % z_chips
        at_x = (chip_x + (step_x if sign > 0 else x_chips - step_x)) % x_chips
        return at_z * x_chips + at_x

    def chip_dev(step):
        return chip_at(step) * 2 + core

    def hops(step):
        step_z, step_x = step // x_chips, step % x_chips
        return min(step_z, z_chips - step_z) + min(step_x, x_chips - step_x)

    steps_out = sorted(range(1, chips), key=lambda step: -hops(step))

    def rcopy(src, dst, ssem, rsem, dev):
        return pltpu.make_async_remote_copy(
            src_ref=src, dst_ref=dst, send_sem=ssem, recv_sem=rsem, device_id=dev, device_id_type=MESH
        )

    feat = featg.at[pl.ds(0, n), :]
    idx_own[24:32, :] = jnp.zeros((8, n), I32)
    fetched = [
        pltpu.make_async_copy(src, dst, in_sem.at[at])
        for at, (src, dst) in enumerate(
            (
                (feat_hbm, feat),
                (nb_hbm, idx_own.at[pl.ds(0, 8), :]),
                (code_hbm, idx_own.at[pl.ds(8, 16), :]),
                (assign_hbm, asg.at[0]),
                (counts_hbm, counts),
                (sums_hbm, sums),
                (ws_hbm, ws),
                (wn_hbm, wn),
                (cot_hbm, cot),
            )
        )
    ]
    for copy in fetched:
        copy.start()

    barrier = pltpu.get_barrier_semaphore()
    for peer in (y_right, y_left, y_far):
        pl.semaphore_signal(barrier, inc=1, device_id=(w, peer), device_id_type=MESH)

    for peer in (*(chip_dev(step) for step in steps_out), other):
        pl.semaphore_signal(barrier, inc=1, device_id=(peer, y), device_id_type=MESH)
    for at in range(4):
        fetched[at].wait()
    pl.semaphore_wait(barrier, narrow - 1 + chips)

    def low(slot):
        return pl.ds(slot * n, half)

    def high(slot):
        return pl.ds(slot * n + half, half)

    def gather_copies(buf, ssem, rsem):
        right, left = (w, y_right), (w, y_left)

        def make(src, dst, at, dev):
            return rcopy(buf.at[src, :], buf.at[dst, :], ssem.at[at], rsem.at[at], dev)

        return (
            make(low(0), low(3), 0, right),
            make(high(0), high(1), 1, left),
            make(high(0), high(3), 2, right),
            make(low(0), low(1), 3, left),
            make(low(3), low(2), 4, right),
            make(high(1), high(2), 5, left),
        )

    def arrived(buf, ssem, rsem, at):
        region = (low(3), high(1), high(3), low(1), low(2), high(2))[at]
        rcopy(buf.at[region, :], buf.at[region, :], ssem.at[at], rsem.at[at], (w, y_right)).wait_recv()

    f_copies = gather_copies(featg, f_s, f_r)
    for at in range(4):
        f_copies[at].start()
    g_copies = [
        rcopy(asg.at[0], asg.at[slot], g_s.at[at], g_r.at[at], (w, peer))
        for at, (peer, slot) in enumerate(((y_right, 3), (y_left, 1), (y_far, 2)))
    ]
    for copy in g_copies:
        copy.start()
    idxg[0] = idx_own[...].astype(jnp.int16)
    i_copies = [
        rcopy(idxg.at[0], idxg.at[slot], i_s.at[at], i_r.at[at], (w, peer))
        for at, (peer, slot) in enumerate(((y_right, 3), (y_left, 1), (y_far, 2)))
    ]

    def table(tab, his_ref, vals_ref, spots_in, lane_at, first_spot):
        lanes = pl.ds(pl.multiple_of(lane_at, 128), 128)
        picks = his_ref.shape[0]
        his = [jnp.broadcast_to(his_ref[j : j + 1, lanes], (16, 128)) for j in range(picks)]
        vals = [jnp.broadcast_to(vals_ref[j : j + 1, lanes], (16, 128)) for j in range(picks)]
        base = lax.broadcasted_iota(I32, (16, 128), 0) + first_spot
        for part in range(min(spots_in, 128) // 16):
            spots = base + part * 16
            words = [words_of(spots, his[at : at + 8], vals[at : at + 8]) for at in range(0, picks, 8)]
            for field, counts_part in enumerate(fields_of(words)):
                row = pl.multiple_of(field * spots_in + part * 16 + first_spot, 16)
                tab[pl.ds(row, 16), lanes] = counts_part

    far_spots = codes // 8
    far_bits = far_spots.bit_length() - 1
    near_spots = grp // 8
    near_bits = near_spots.bit_length() - 1
    node_bits = n.bit_length() - 1
    own_ids = idx_own[8:24, :]
    hi_f[...] = own_ids & (far_spots - 1)
    val_f[...] = jnp.int32(1) << ((own_ids >> far_bits) * 4)
    own_ids = idx_own[0:8, :]
    own_ids = ((((own_ids >> node_bits) - y) & (narrow - 1)) << node_bits) | (own_ids & (n - 1))
    hi_n[...] = own_ids & (near_spots - 1)
    val_n[...] = jnp.int32(1) << ((own_ids >> near_bits) * 4)

    def far_tile(tile, carry):
        table(tab_far, hi_f, val_f, far_spots, (tile // (far_spots // 128)) * 128, (tile % (far_spots // 128)) * 128)
        return carry

    def near_tile(tile, carry):
        table(tab_near, hi_n, val_n, near_spots, (tile // (near_spots // 128)) * 128, (tile % (near_spots // 128)) * 128)
        return carry

    far_tiles = (n // 128) * (far_spots // 128)
    lax.fori_loop(0, far_tiles, far_tile, 0)
    width = sums.shape[1]
    for at in range(4, 9):
        fetched[at].wait()
    blocks = codes // 128
    inverse = jnp.transpose(jnp.concatenate([1.0 / counts[...]] * (128 // blocks), 0))
    for block in range(blocks):
        column = jnp.broadcast_to(inverse[:, block : block + 1], (128, 128))
        for part in range(width // 128):
            at = (slice(block * 128, block * 128 + 128), slice(part * 128, part * 128 + 128))
            codebook[at] = (sums[at] * column).astype(BF16)
    far[...] = jnp.zeros_like(far)
    arrived(featg, f_s, f_r, 0)
    f_copies[4].start()
    arrived(featg, f_s, f_r, 1)
    f_copies[5].start()
    near_tiles = (n // 128) * (near_spots // 128)
    step_codes = codes // near_tiles

    def near_step(tile, carry):
        near_tile(tile, 0)
        rows = pl.ds(pl.multiple_of(tile * step_codes, step_codes), step_codes)
        far[...] += dot_tn(tab_far[rows, :], codebook[rows, :])
        return carry

    lax.fori_loop(0, near_tiles, near_step, 0)
    for kw in range(wide):
        kc = kw // 2
        step = ((kc // x_chips + z_chips - chip_z) % z_chips) * x_chips + (kc % x_chips + x_chips - chip_x) % x_chips
        to = ((kw + core) % 2) * own_half + step * shard
        rows = pl.ds(pl.multiple_of((kw * narrow + y) * shard, shard), shard)
        tab_code[pl.ds(pl.multiple_of(to, shard), shard), 0:n] = tab_far[rows, :]
    hid[...] = dot(feat[...], ws[...])
    taken[:, 0:width] = feat[...]
    near[...] = dot_tn(tab_near[0:n, :], feat[...])
    for copy in g_copies:
        copy.wait_recv()
    shard_bits = shard.bit_length() - 1
    narrow_bits = narrow.bit_length() - 1
    mine_spots = mine // 8
    mine_bits = mine_spots.bit_length() - 1
    ret_spots = n // 8
    ret_bits = ret_spots.bit_length() - 1

    def place(k):
        kw = k >> (shard_bits + narrow_bits)
        kc = kw >> 1
        step = ((((kc >> (x_chips.bit_length() - 1)) - chip_z) & (z_chips - 1)) * x_chips) | ((kc - chip_x) & (x_chips - 1))
        row = ((((kw & 1) ^ core) * chips + step) << shard_bits) | (k & (shard - 1))
        return row, ((k >> shard_bits) & (narrow - 1)) == y

    for slot in range(narrow):
        row, hit = place(asg[slot])
        row_a[:, slot * n : slot * n + n] = jnp.where(hit, row, -1)

    all_rows = row_a[...]
    asn_hi[...] = jnp.where(lax.broadcasted_iota(I32, asn_hi.shape, 0) == (all_rows >> 4), 1.0, 0.0)
    asn_lo[...] = jnp.where(lax.broadcasted_iota(I32, (16, grp), 0) == (all_rows & 15), 1.0, 0.0).astype(BF16)

    def asn_part(group, carry):
        totals = [None] * 8
        for tile in range(grp // 128):
            lanes = slice(tile * 128, tile * 128 + 128)
            fits = asn_hi[pl.ds(pl.multiple_of(group * 8, 8), 8), lanes]
            low = asn_lo[:, lanes]
            for part in range(8):
                hit = jnp.broadcast_to(fits[part : part + 1, :], (16, 128)).astype(BF16) * low
                tab_asn[pl.ds(pl.multiple_of(group * 128 + part * 16, 16), 16), lanes] = hit
                totals[part] = hit if tile == 0 else totals[part] + hit
        for part in range(8):
            as_acc[pl.ds(pl.multiple_of(group * 128 + part * 16, 16), 16), :] = totals[part]
        return carry

    lax.fori_loop(0, mine // 128, asn_part, 0)

    for copy in i_copies:
        copy.start()
    arrived(featg, f_s, f_r, 2)
    near[...] += dot_tn(tab_near[3 * n : 4 * n, :], featg[3 * n : 4 * n, :])
    arrived(featg, f_s, f_r, 3)
    near[...] += dot_tn(tab_near[n : 2 * n, :], featg[n : 2 * n, :])
    arrived(featg, f_s, f_r, 4)
    arrived(featg, f_s, f_r, 5)

    d_copies = gather_copies(daggg, d_s, d_r)
    for at in range(2):
        rows = pl.ds(at * half, half)
        total = near[rows, :] + dot_tn(tab_near[2 * n : 3 * n, at * half : at * half + half], featg[2 * n : 3 * n, :])
        agg = (total * (1.0 / 8) + far[rows, :] * (1.0 / 16)).astype(BF16)
        taken[rows, width:] = agg
        z = hid[rows, :] + dot(agg, wn[...])
        s = jax.nn.sigmoid(z)
        out[rows, :] = (z * s).astype(BF16)
        dz = (cot[rows, :].astype(F32) * s * (1.0 + z * (1.0 - s))).astype(BF16)
        dz_all[rows, :] = dz
        daggg[rows, :] = dot_nt(dz, wn[...]).astype(BF16)
        d_copies[(0, 1)[at]].start()
        d_copies[(3, 2)[at]].start()

    wrows = ws.shape[0]
    local = dot_tn(taken[...], dz_all[...])
    wg_f[0] = local[0:wrows, :]
    wg_f[1] = local[wrows:, :]
    wg_tx[...] = wg_f[1 - core].astype(BF16)
    wa = rcopy(wg_tx, wg_rx, wa_s, wa_r, (other, y))
    wa.start()

    def split_count(count):
        big = jnp.floor(count * (1.0 / 256)) * 256.0
        lane = lax.broadcasted_iota(I32, count.shape, 1)
        return jnp.where(lane < 64, big, count - big).astype(BF16)

    def join_count(pair):
        pair = pair.astype(F32)
        return pair + pltpu.roll(pair, 64, 1)

    def assigned(first):
        rows = pl.ds(first, own_half)
        as_f[rows, :] = dot(tab_asn[rows, :], featg[...])
        as_cnt[rows, :] = dot(as_acc[rows, :], jnp.ones((128, 128), BF16))

    assigned(own_half)
    as_tx[:, 0:width] = as_f[own_half:, :].astype(BF16)
    as_tx[:, width:] = split_count(as_cnt[own_half:, :])
    aa = rcopy(as_tx, as_rx, aa_s, aa_r, (other, y))
    aa.start()

    wa.wait_recv()
    wg_own = wg_f[core] + wg_rx[...].astype(F32)
    wg_f[core] = wg_own
    wgb_tx[...] = wg_own.astype(BF16)
    part_rows = wrows // chips

    def wg_rows(at):
        return pl.ds(pl.multiple_of(at * part_rows, part_rows), part_rows)

    wb = {}
    for step in steps_out:
        wb[step] = rcopy(
            wgb_tx.at[wg_rows(chip_at(step)), :], wgb_rx.at[step], wb_s.at[step], wb_r.at[step], (chip_dev(step), y)
        )
        wb[step].start()
    assigned(0)

    aa.wait_recv()
    as_f[0:own_half, :] += as_rx[:, 0:width].astype(F32)
    as_cnt[0:own_half, :] += join_count(as_rx[:, width:])
    ab = {}
    for step in steps_out:
        rows = pl.ds(step * shard, shard)
        asb_tx[step, :, 0:width] = as_f[rows, :].astype(BF16)
        asb_tx[step, :, width:] = split_count(as_cnt[rows, :])
        ab[step] = rcopy(asb_tx.at[step], asb_rx.at[step], ab_s.at[step], ab_r.at[step], (chip_dev(step), y))
        ab[step].start()

    for at in range(3):
        i_copies[at].wait_recv()
    for slot in range(narrow):
        lanes = pl.ds(slot * n, n)
        block = idxg[slot].astype(I32)
        ids = block[0:8, :]
        hi_r[:, lanes] = ids & (ret_spots - 1)
        local = ids & (n - 1)
        val_r[:, lanes] = jnp.where((ids >> node_bits) == y, jnp.int32(1) << ((local >> ret_bits) * 4), 0)
        row, hit = place(block[8:24, :])
        hi_t[:, lanes] = row & (mine_spots - 1)
        val_t[:, lanes] = jnp.where(hit, jnp.int32(1) << ((row >> mine_bits) * 4), 0)

    def code_tile(tile, carry):
        table(tab_code, hi_t, val_t, mine_spots, tile * 128, 0)
        return carry

    def ret_tile(tile, carry):
        table(tab_ret, hi_r, val_r, ret_spots, tile * 128, 0)
        return carry

    first_tile, tiles = n // 128, grp // 128
    middle = (first_tile + tiles) // 2
    lax.fori_loop(first_tile, middle, code_tile, 0)
    arrived(daggg, d_s, d_r, 0)
    d_copies[4].start()
    arrived(daggg, d_s, d_r, 1)
    d_copies[5].start()
    lax.fori_loop(middle, tiles, code_tile, 0)

    for step in steps_out:
        wb[step].wait_recv()
    share = wg_f[core, wg_rows(chip), :]
    for step in steps_out:
        share = share + wgb_rx[step].astype(F32)
    wgc[0] = share
    wc = []
    for at, (peer, slot) in enumerate(((y_right, 3), (y_left, 1), (y_far, 2))):
        wc.append(rcopy(wgc.at[0], wgc.at[slot], wc_s.at[at], wc_r.at[at], (w, peer)))
        wc[-1].start()

    arrived(daggg, d_s, d_r, 2)
    arrived(daggg, d_s, d_r, 3)
    acc[...] = dot(tab_code[:, 0 : 2 * n], daggg[0 : 2 * n, :]) + dot(tab_code[:, 3 * n :], daggg[3 * n :, :])
    arrived(daggg, d_s, d_r, 4)
    arrived(daggg, d_s, d_r, 5)
    last = daggg[2 * n : 3 * n, :]
    block = own_half // 2

    def finished(first):
        rows = slice(first, first + block)
        return (acc[rows, :] + dot(tab_code[rows, 2 * n : 3 * n], last)) * (1.0 / 16)

    ca = {}
    for part in (1, 0):
        rows = pl.ds(part * block, block)
        cg_tx[rows, :] = finished(own_half + part * block).astype(BF16)
        ca[part] = rcopy(cg_tx.at[rows, :], cg_rx.at[rows, :], ca_s.at[part], ca_r.at[part], (other, y))
        ca[part].start()
    for part in (1, 0):
        acc[part * block : part * block + block, :] = finished(part * block)

    for at in range(3):
        wc[at].wait_recv()

    def share_rows(at):
        return pl.ds(pl.multiple_of(core * wrows + at * part_rows, part_rows), part_rows)

    wgd[share_rows(chip), :] = (wgc[0] + wgc[1] + wgc[2] + wgc[3]).astype(BF16)
    wd = {}
    for step in steps_out:
        mine_rows = wgd.at[share_rows(chip), :]
        wd[step] = rcopy(mine_rows, mine_rows, wd_s.at[step], wd_r.at[step], (chip_dev(step), y))
        wd[step].start()

    cb = {}
    for part in (1, 0):
        ca[part].wait_recv()
        for step in steps_out:
            if step * shard // block != part:
                continue
            rows = pl.ds(step * shard, shard)
            cgb_tx[step] = (acc[rows, :] + cg_rx[rows, :].astype(F32)).astype(BF16)
            cb[step] = rcopy(cgb_tx.at[step], cgb_rx.at[step], cb_s.at[step], cb_r.at[step], (chip_dev(step), y))
            cb[step].start()

    lax.fori_loop(0, grp // 128, ret_tile, 0)
    fgrad[...] = (dot_nt(dz_all[...], ws[...]) + dot(tab_ret[...], daggg[...]) * (1.0 / 8)).astype(BF16)

    own_sum = as_f[0:shard, :]
    own_cnt = as_cnt[0:shard, :]
    for step in steps_out:
        ab[step].wait_recv()
        own_sum = own_sum + asb_rx[step, :, 0:width].astype(F32)
        own_cnt = own_cnt + join_count(asb_rx[step, :, width:])
    first = (w * narrow + y) * shard
    cnt_row = counts[pl.ds(first // 128, 1), :]
    cnt_col[...] = jnp.transpose(jnp.broadcast_to(cnt_row, (128, 128)))
    if shard <= 128:
        old_cnt = cnt_col[pl.ds(pl.multiple_of(first % 128, shard), shard), :]
    else:
        old_cnt = jnp.concatenate(
            [jnp.transpose(jnp.broadcast_to(counts[pl.ds(first // 128 + b, 1), :], (128, 128))) for b in range(shard // 128)], 0
        )
    scale = 1.0 / (decay_rate * old_cnt + (1.0 - decay_rate) * own_cnt)
    old = sums[pl.ds(pl.multiple_of(first, shard), shard), :]
    for part in range(width // 128):
        lanes = slice(part * 128, part * 128 + 128)
        newcb[:, lanes] = (decay_rate * old[:, lanes] + (1.0 - decay_rate) * own_sum[:, lanes]) * scale

    for step in steps_out:
        source = wgd.at[share_rows(chip_at(step, -1)), :]
        rcopy(source, source, wd_s.at[step], wd_r.at[step], (chip_dev(step), y)).wait_recv()
    own_rows = wgd.at[pl.ds(pl.multiple_of(core * wrows, wrows), wrows), :]
    other_rows = wgd.at[pl.ds(pl.multiple_of((1 - core) * wrows, wrows), wrows), :]
    we = rcopy(own_rows, own_rows, we_s, we_r, (other, y))
    we.start()
    rcopy(other_rows, other_rows, we_s, we_r, (other, y)).wait_recv()
    sgrad[...] = wgd[0:wrows, :].astype(F32)
    ngrad[...] = wgd[wrows:, :].astype(F32)

    own = acc[0:shard, :] + cg_rx[0:shard, :].astype(F32)
    for step in steps_out:
        cb[step].wait_recv()
        own = own + cgb_rx[step].astype(F32)
    cgrad[...] = own

    for copy in (*f_copies, *d_copies, *i_copies, *g_copies, wa, aa, *ca.values(), *wc, we):
        copy.wait_send()
    for step in steps_out:
        for copies in (wb, ab, wd, cb):
            copies[step].wait_send()


def copy_kernel(count, *refs):
    copies = [pltpu.make_async_copy(refs[at], refs[count + at], refs[-1].at[at]) for at in range(count)]
    for copy in copies:
        copy.start()
    for copy in copies:
        copy.wait()


def on_device(
    wide, narrow,
    features, neighbours, code_ids, assignment, cotangent, code_sums, code_counts, self_weight, neighbour_weight,
):
    n, width = features.shape
    codes = code_sums.shape[0]
    chips = wide // 2
    shard = codes // (wide * narrow)
    mine = codes // narrow
    grp = n * narrow
    hbm = pl.BlockSpec(memory_space=pltpu.HBM)
    dma = pltpu.SemaphoreType.DMA
    wide_rows = self_weight.shape[0]
    scratch = [
        pltpu.VMEM((n, width), BF16),
        pltpu.VMEM((codes, width), F32),
        pltpu.VMEM((codes // 128, 128), F32),
        pltpu.VMEM(self_weight.shape, BF16),
        pltpu.VMEM(neighbour_weight.shape, BF16),
        pltpu.VMEM((codes, width), BF16),
        pltpu.VMEM((grp, width), BF16),
        pltpu.VMEM((grp, width), BF16),
        pltpu.VMEM((IDX_ROWS, n), I32),
        pltpu.VMEM((narrow, IDX_ROWS, n), jnp.int16),
        pltpu.VMEM((narrow, 1, n), I32),
        pltpu.VMEM((codes, n), BF16),
        pltpu.VMEM((grp, n), BF16),
        pltpu.VMEM((mine, grp), BF16),
        pltpu.VMEM((n, grp), BF16),
        pltpu.VMEM((mine, grp), BF16),
        pltpu.VMEM((16, n), I32),
        pltpu.VMEM((16, n), I32),
        pltpu.VMEM((8, n), I32),
        pltpu.VMEM((8, n), I32),
        pltpu.VMEM((16, grp), I32),
        pltpu.VMEM((16, grp), I32),
        pltpu.VMEM((8, grp), I32),
        pltpu.VMEM((8, grp), I32),
        pltpu.VMEM((1, grp), I32),
        pltpu.VMEM((mine // 16, grp), F32),
        pltpu.VMEM((16, grp), BF16),
        pltpu.VMEM((n, width), F32),
        pltpu.VMEM((n, width), F32),
        pltpu.VMEM((n, width), F32),
        pltpu.VMEM((n, width), BF16),
        pltpu.VMEM((n, 2 * width), BF16),
        pltpu.VMEM((mine, width), F32),
        pltpu.VMEM((2, wide_rows, width), F32),
        pltpu.VMEM((wide_rows, width), BF16),
        pltpu.VMEM((wide_rows, width), BF16),
        pltpu.VMEM((wide_rows, width), BF16),
        pltpu.VMEM((chips, wide_rows // chips, width), BF16),
        pltpu.VMEM((narrow, wide_rows // chips, width), F32),
        pltpu.VMEM((2 * wide_rows, width), BF16),
        pltpu.VMEM((mine, width), F32),
        pltpu.VMEM((mine, 128), F32),
        pltpu.VMEM((mine, 128), BF16),
        pltpu.VMEM((mine // 2, width + 128), BF16),
        pltpu.VMEM((mine // 2, width + 128), BF16),
        pltpu.VMEM((chips, shard, width + 128), BF16),
        pltpu.VMEM((chips, shard, width + 128), BF16),
        pltpu.VMEM((mine // 2, width), BF16),
        pltpu.VMEM((mine // 2, width), BF16),
        pltpu.VMEM((chips, shard, width), BF16),
        pltpu.VMEM((chips, shard, width), BF16),
        pltpu.VMEM((128, 128), F32),
        dma((9,)),
        dma((6,)), dma((6,)), dma((6,)), dma((6,)), dma((3,)), dma((3,)), dma((3,)), dma((3,)),
        dma, dma, dma((chips,)), dma((chips,)), dma((3,)), dma((3,)), dma((chips,)), dma((chips,)), dma, dma,
        dma, dma, dma((chips,)), dma((chips,)), dma((2,)), dma((2,)), dma((chips,)), dma((chips,)),
    ]
    shapes = (
        jax.ShapeDtypeStruct((n, width), BF16),
        jax.ShapeDtypeStruct((n, width), BF16),
        jax.ShapeDtypeStruct(self_weight.shape, F32),
        jax.ShapeDtypeStruct(neighbour_weight.shape, F32),
        jax.ShapeDtypeStruct((shard, width), F32),
        jax.ShapeDtypeStruct((shard, width), F32),
    )
    vm = pl.BlockSpec(memory_space=pltpu.VMEM)
    operands = (
        features, neighbours.T, code_ids.T, assignment.reshape(1, n), cotangent,
        code_sums, code_counts.reshape(codes // 128, 128), self_weight, neighbour_weight,
    )
    results = pl.pallas_call(
        functools.partial(kernel, wide, narrow, shard),
        out_shape=tuple(pltpu.VMEM(shape.shape, shape.dtype) for shape in shapes),
        in_specs=[hbm] * 9,
        out_specs=(vm,) * 6,
        scratch_shapes=scratch,
        compiler_params=pltpu.CompilerParams(
            collective_id=0, has_side_effects=True, vmem_limit_bytes=48 * 1024 * 1024
        ),
    )(*(pltpu.with_memory_space_constraint(operand, pltpu.HBM) for operand in operands))
    return pl.pallas_call(
        functools.partial(copy_kernel, len(shapes)),
        out_shape=shapes,
        in_specs=[vm] * 6,
        out_specs=(hbm,) * 6,
        scratch_shapes=[dma((6,))],
        compiler_params=pltpu.CompilerParams(vmem_limit_bytes=8 * 1024 * 1024),
    )(*results)


def solution(mesh):
    both = ("wide", "narrow")
    return jax.shard_map(
        functools.partial(on_device, mesh.shape["wide"], mesh.shape["narrow"]),
        mesh=mesh,
        in_specs=(P(both, None), P(both, None), P(both, None), P(both), P(both, None), P(), P(), P(), P()),
        out_specs=(P(both, None), P(both, None), P(), P(), P(both, None), P(both, None)),
        check_vma=False,
    )
```

```python
import functools

import jax
import jax.numpy as jnp
from jax import lax
from jax.experimental import pallas as pl
from jax.experimental.pallas import tpu as pltpu
from jax.sharding import PartitionSpec as P

MESH = pl.DeviceIdType.MESH
F32, BF16, I32 = jnp.float32, jnp.bfloat16, jnp.int32
decay_rate = 0.5
IDX_ROWS = 32
NIBBLES = 0x0F0F0F0F


def dot(a, b):
    return jnp.dot(a, b, preferred_element_type=F32)


def dot_nt(a, b):
    return lax.dot_general(a, b, (((1,), (1,)), ((), ())), preferred_element_type=F32)


def dot_tn(a, b):
    return lax.dot_general(a, b, (((0,), (0,)), ((), ())), preferred_element_type=F32)


def words_of(spots, his, vals):
    word = None
    for hi, val in zip(his, vals):
        term = jnp.where(spots == hi, val, 0)
        word = term if word is None else word + term
    return word


def fields_of(words):
    even = odd = None
    for word in words:
        low, high = word & NIBBLES, (word >> 4) & NIBBLES
        even = low if even is None else even + low
        odd = high if odd is None else odd + high
    out = []
    for field in range(8):
        part = (even, odd)[field % 2]
        shift = 8 * (field // 2)
        if shift:
            part = part >> shift
        if shift < 24:
            part = part & 255
        out.append(part.astype(F32).astype(BF16))
    return out


def kernel(
    wide, narrow, shard,
    feat_hbm, nb_hbm, code_hbm, assign_hbm, cot_hbm, sums_hbm, counts_hbm, ws_hbm, wn_hbm,
    out, fgrad, sgrad, ngrad, newcb, cgrad,
    cot, sums, counts, ws, wn,
    codebook, featg, daggg, idx_own, idxg, asg, tab_far, tab_near, tab_code, tab_ret, tab_asn,
    hi_f, val_f, hi_n, val_n, hi_t, val_t, hi_r, val_r, row_a, asn_hi, asn_lo, far, near, hid, dz_all, taken, acc,
    wg_f, wg_tx, wg_rx, wgb_tx, wgb_rx, wgc, wgd, as_f, as_cnt, as_acc, as_tx, as_rx, asb_tx, asb_rx,
    cg_tx, cg_rx, cgb_tx, cgb_rx, cnt_col,
    in_sem, f_s, f_r, d_s, d_r, i_s, i_r, g_s, g_r, wa_s, wa_r, wb_s, wb_r, wc_s, wc_r, wd_s, wd_r, we_s, we_r,
    aa_s, aa_r, ab_s, ab_r, ca_s, ca_r, cb_s, cb_r,
):
    n = cot.shape[0]
    half = n // 2
    chips = wide // 2
    codes = sums.shape[0]
    mine = codes // narrow
    own_half = mine // 2
    grp = n * narrow
    w = lax.axis_index("wide")
    y = lax.axis_index("narrow")
    core = w % 2
    chip = w // 2
    y_right, y_left, y_far = (y + 1) % narrow, (y + 3) % narrow, (y + 2) % narrow
    other = chip * 2 + (1 - core)

    x_chips = min(4, chips)
    z_chips = chips // x_chips
    chip_z, chip_x = chip // x_chips, chip % x_chips

    def chip_at(step, sign=1):
        step_z, step_x = step // x_chips, step % x_chips
        at_z = (chip_z + (step_z if sign > 0 else z_chips - step_z)) % z_chips
        at_x = (chip_x + (step_x if sign > 0 else x_chips - step_x)) % x_chips
        return at_z * x_chips + at_x

    def chip_dev(step):
        return chip_at(step) * 2 + core

    def hops(step):
        step_z, step_x = step // x_chips, step % x_chips
        return min(step_z, z_chips - step_z) + min(step_x, x_chips - step_x)

    steps_out = sorted(range(1, chips), key=lambda step: -hops(step))

    def rcopy(src, dst, ssem, rsem, dev):
        return pltpu.make_async_remote_copy(
            src_ref=src, dst_ref=dst, send_sem=ssem, recv_sem=rsem, device_id=dev, device_id_type=MESH
        )

    feat = featg.at[pl.ds(0, n), :]
    idx_own[24:32, :] = jnp.zeros((8, n), I32)
    fetched = [
        pltpu.make_async_copy(src, dst, in_sem.at[at])
        for at, (src, dst) in enumerate(
            (
                (feat_hbm, feat),
                (nb_hbm, idx_own.at[pl.ds(0, 8), :]),
                (code_hbm, idx_own.at[pl.ds(8, 16), :]),
                (assign_hbm, asg.at[0]),
                (counts_hbm, counts),
                (sums_hbm, sums),
                (ws_hbm, ws),
                (wn_hbm, wn),
                (cot_hbm, cot),
            )
        )
    ]
    for copy in fetched:
        copy.start()

    barrier = pltpu.get_barrier_semaphore()
    for peer in (y_right, y_left, y_far):
        pl.semaphore_signal(barrier, inc=1, device_id=(w, peer), device_id_type=MESH)

    for peer in (*(chip_dev(step) for step in steps_out), other):
        pl.semaphore_signal(barrier, inc=1, device_id=(peer, y), device_id_type=MESH)
    for at in range(4):
        fetched[at].wait()
    pl.semaphore_wait(barrier, narrow - 1 + chips)

    def low(slot):
        return pl.ds(slot * n, half)

    def high(slot):
        return pl.ds(slot * n + half, half)

    def quarter(slot, at):
        return pl.ds(slot * n + at * (half // 2), half // 2)

    def gather_copies(buf, ssem, rsem):
        right, left = (w, y_right), (w, y_left)

        def make(src, dst, at, dev):
            return rcopy(buf.at[src, :], buf.at[dst, :], ssem.at[at], rsem.at[at], dev)

        return (
            make(quarter(0, 0), quarter(3, 0), 0, right),
            make(quarter(0, 2), quarter(1, 2), 1, left),
            make(high(0), high(3), 2, right),
            make(low(0), low(1), 3, left),
            make(quarter(3, 0), quarter(2, 0), 4, right),
            make(quarter(1, 2), quarter(2, 2), 5, left),
            make(quarter(0, 1), quarter(3, 1), 6, right),
            make(quarter(0, 3), quarter(1, 3), 7, left),
            make(quarter(3, 1), quarter(2, 1), 8, right),
            make(quarter(1, 3), quarter(2, 3), 9, left),
        )

    def arrived(buf, ssem, rsem, at):
        region = (
            quarter(3, 0), quarter(1, 2), high(3), low(1), quarter(2, 0), quarter(2, 2),
            quarter(3, 1), quarter(1, 3), quarter(2, 1), quarter(2, 3),
        )[at]
        rcopy(buf.at[region, :], buf.at[region, :], ssem.at[at], rsem.at[at], (w, y_right)).wait_recv()

    f_copies = gather_copies(featg, f_s, f_r)
    for at in (0, 1, 6, 7, 2, 3):
        f_copies[at].start()
    g_copies = [
        rcopy(asg.at[0], asg.at[slot], g_s.at[at], g_r.at[at], (w, peer))
        for at, (peer, slot) in enumerate(((y_right, 3), (y_left, 1), (y_far, 2)))
    ]
    for copy in g_copies:
        copy.start()
    idxg[0] = idx_own[...].astype(jnp.int16)
    i_copies = [
        rcopy(idxg.at[0], idxg.at[slot], i_s.at[at], i_r.at[at], (w, peer))
        for at, (peer, slot) in enumerate(((y_right, 3), (y_left, 1), (y_far, 2)))
    ]

    def table(tab, his_ref, vals_ref, spots_in, lane_at, first_spot):
        lanes = pl.ds(pl.multiple_of(lane_at, 128), 128)
        picks = his_ref.shape[0]
        his = [jnp.broadcast_to(his_ref[j : j + 1, lanes], (16, 128)) for j in range(picks)]
        vals = [jnp.broadcast_to(vals_ref[j : j + 1, lanes], (16, 128)) for j in range(picks)]
        base = lax.broadcasted_iota(I32, (16, 128), 0) + first_spot
        for part in range(min(spots_in, 128) // 16):
            spots = base + part * 16
            words = [words_of(spots, his[at : at + 8], vals[at : at + 8]) for at in range(0, picks, 8)]
            for field, counts_part in enumerate(fields_of(words)):
                row = pl.multiple_of(field * spots_in + part * 16 + first_spot, 16)
                tab[pl.ds(row, 16), lanes] = counts_part

    far_spots = codes // 8
    far_bits = far_spots.bit_length() - 1
    near_spots = grp // 8
    near_bits = near_spots.bit_length() - 1
    node_bits = n.bit_length() - 1
    own_ids = idx_own[8:24, :]
    hi_f[...] = own_ids & (far_spots - 1)
    val_f[...] = jnp.int32(1) << ((own_ids >> far_bits) * 4)
    own_ids = idx_own[0:8, :]
    own_ids = ((((own_ids >> node_bits) - y) & (narrow - 1)) << node_bits) | (own_ids & (n - 1))
    hi_n[...] = own_ids & (near_spots - 1)
    val_n[...] = jnp.int32(1) << ((own_ids >> near_bits) * 4)

    def far_tile(tile, carry):
        table(tab_far, hi_f, val_f, far_spots, (tile // (far_spots // 128)) * 128, (tile % (far_spots // 128)) * 128)
        return carry

    def near_tile(tile, carry):
        table(tab_near, hi_n, val_n, near_spots, (tile // (near_spots // 128)) * 128, (tile % (near_spots // 128)) * 128)
        return carry

    far_tiles = (n // 128) * (far_spots // 128)
    lax.fori_loop(0, far_tiles, far_tile, 0)
    width = sums.shape[1]
    for at in range(4, 9):
        fetched[at].wait()
    blocks = codes // 128
    inverse = jnp.transpose(jnp.concatenate([1.0 / counts[...]] * (128 // blocks), 0))
    for block in range(blocks):
        column = jnp.broadcast_to(inverse[:, block : block + 1], (128, 128))
        for part in range(width // 128):
            at = (slice(block * 128, block * 128 + 128), slice(part * 128, part * 128 + 128))
            codebook[at] = (sums[at] * column).astype(BF16)
    far[...] = jnp.zeros_like(far)
    arrived(featg, f_s, f_r, 0)
    f_copies[4].start()
    arrived(featg, f_s, f_r, 1)
    f_copies[5].start()
    near_tiles = (n // 128) * (near_spots // 128)
    step_codes = codes // near_tiles

    def near_step(tile, carry):
        near_tile(tile, 0)
        rows = pl.ds(pl.multiple_of(tile * step_codes, step_codes), step_codes)
        far[...] += dot_tn(tab_far[rows, :], codebook[rows, :])
        return carry

    lax.fori_loop(0, near_tiles // 4, near_step, 0)
    arrived(featg, f_s, f_r, 6)
    f_copies[8].start()
    arrived(featg, f_s, f_r, 7)
    f_copies[9].start()
    lax.fori_loop(near_tiles // 4, near_tiles, near_step, 0)
    for kw in range(wide):
        kc = kw // 2
        step = ((kc // x_chips + z_chips - chip_z) % z_chips) * x_chips + (kc % x_chips + x_chips - chip_x) % x_chips
        to = ((kw + core) % 2) * own_half + step * shard
        rows = pl.ds(pl.multiple_of((kw * narrow + y) * shard, shard), shard)
        tab_code[pl.ds(pl.multiple_of(to, shard), shard), 0:n] = tab_far[rows, :]
    hid[...] = dot(feat[...], ws[...])
    taken[:, 0:width] = feat[...]
    near[...] = dot_tn(tab_near[0:n, :], feat[...])
    for copy in g_copies:
        copy.wait_recv()
    shard_bits = shard.bit_length() - 1
    narrow_bits = narrow.bit_length() - 1
    mine_spots = mine // 8
    mine_bits = mine_spots.bit_length() - 1
    ret_spots = n // 8
    ret_bits = ret_spots.bit_length() - 1

    def place(k):
        kw = k >> (shard_bits + narrow_bits)
        kc = kw >> 1
        step = ((((kc >> (x_chips.bit_length() - 1)) - chip_z) & (z_chips - 1)) * x_chips) | ((kc - chip_x) & (x_chips - 1))
        row = ((((kw & 1) ^ core) * chips + step) << shard_bits) | (k & (shard - 1))
        return row, ((k >> shard_bits) & (narrow - 1)) == y

    for slot in range(narrow):
        row, hit = place(asg[slot])
        row_a[:, slot * n : slot * n + n] = jnp.where(hit, row, -1)

    all_rows = row_a[...]
    asn_hi[...] = jnp.where(lax.broadcasted_iota(I32, asn_hi.shape, 0) == (all_rows >> 4), 1.0, 0.0)
    asn_lo[...] = jnp.where(lax.broadcasted_iota(I32, (16, grp), 0) == (all_rows & 15), 1.0, 0.0).astype(BF16)

    def asn_part(group, carry):
        totals = [None] * 8
        for tile in range(grp // 128):
            lanes = slice(tile * 128, tile * 128 + 128)
            fits = asn_hi[pl.ds(pl.multiple_of(group * 8, 8), 8), lanes]
            low = asn_lo[:, lanes]
            for part in range(8):
                hit = jnp.broadcast_to(fits[part : part + 1, :], (16, 128)).astype(BF16) * low
                tab_asn[pl.ds(pl.multiple_of(group * 128 + part * 16, 16), 16), lanes] = hit
                totals[part] = hit if tile == 0 else totals[part] + hit
        for part in range(8):
            as_acc[pl.ds(pl.multiple_of(group * 128 + part * 16, 16), 16), :] = totals[part]
        return carry

    lax.fori_loop(0, mine // 128, asn_part, 0)

    for copy in i_copies:
        copy.start()
    arrived(featg, f_s, f_r, 2)
    near[...] += dot_tn(tab_near[3 * n : 4 * n, :], featg[3 * n : 4 * n, :])
    arrived(featg, f_s, f_r, 3)
    near[...] += dot_tn(tab_near[n : 2 * n, :], featg[n : 2 * n, :])
    for at in (4, 5, 8, 9):
        arrived(featg, f_s, f_r, at)

    d_copies = gather_copies(daggg, d_s, d_r)
    for at in range(2):
        rows = pl.ds(at * half, half)
        total = near[rows, :] + dot_tn(tab_near[2 * n : 3 * n, at * half : at * half + half], featg[2 * n : 3 * n, :])
        agg = (total * (1.0 / 8) + far[rows, :] * (1.0 / 16)).astype(BF16)
        taken[rows, width:] = agg
        z = hid[rows, :] + dot(agg, wn[...])
        s = jax.nn.sigmoid(z)
        out[rows, :] = (z * s).astype(BF16)
        dz = (cot[rows, :].astype(F32) * s * (1.0 + z * (1.0 - s))).astype(BF16)
        dz_all[rows, :] = dz
        daggg[rows, :] = dot_nt(dz, wn[...]).astype(BF16)
        for part in ((0, 6, 3), (1, 7, 2))[at]:
            d_copies[part].start()

    wrows = ws.shape[0]
    local = dot_tn(taken[...], dz_all[...])
    wg_f[0] = local[0:wrows, :]
    wg_f[1] = local[wrows:, :]
    wg_tx[...] = wg_f[1 - core].astype(BF16)
    wa = rcopy(wg_tx, wg_rx, wa_s, wa_r, (other, y))
    wa.start()

    def split_count(count):
        big = jnp.floor(count * (1.0 / 256)) * 256.0
        lane = lax.broadcasted_iota(I32, count.shape, 1)
        return jnp.where(lane < 64, big, count - big).astype(BF16)

    def join_count(pair):
        pair = pair.astype(F32)
        return pair + pltpu.roll(pair, 64, 1)

    def assigned(first):
        rows = pl.ds(first, own_half)
        as_f[rows, :] = dot(tab_asn[rows, :], featg[...])
        as_cnt[rows, :] = dot(as_acc[rows, :], jnp.ones((128, 128), BF16))

    wa.wait_recv()
    wg_own = wg_f[core] + wg_rx[...].astype(F32)
    wg_f[core] = wg_own
    wgb_tx[...] = wg_own.astype(BF16)
    part_rows = wrows // chips

    def wg_rows(at):
        return pl.ds(pl.multiple_of(at * part_rows, part_rows), part_rows)

    wb = {}
    for step in steps_out:
        wb[step] = rcopy(
            wgb_tx.at[wg_rows(chip_at(step)), :], wgb_rx.at[step], wb_s.at[step], wb_r.at[step], (chip_dev(step), y)
        )
        wb[step].start()
    assigned(own_half)
    as_tx[:, 0:width] = as_f[own_half:, :].astype(BF16)
    as_tx[:, width:] = split_count(as_cnt[own_half:, :])
    aa = rcopy(as_tx, as_rx, aa_s, aa_r, (other, y))
    aa.start()

    assigned(0)

    aa.wait_recv()
    as_f[0:own_half, :] += as_rx[:, 0:width].astype(F32)
    as_cnt[0:own_half, :] += join_count(as_rx[:, width:])
    ab = {}
    for step in steps_out:
        rows = pl.ds(step * shard, shard)
        asb_tx[step, :, 0:width] = as_f[rows, :].astype(BF16)
        asb_tx[step, :, width:] = split_count(as_cnt[rows, :])
        ab[step] = rcopy(asb_tx.at[step], asb_rx.at[step], ab_s.at[step], ab_r.at[step], (chip_dev(step), y))
        ab[step].start()

    for at in range(3):
        i_copies[at].wait_recv()
    for slot in range(narrow):
        lanes = pl.ds(slot * n, n)
        block = idxg[slot].astype(I32)
        ids = block[0:8, :]
        hi_r[:, lanes] = ids & (ret_spots - 1)
        local = ids & (n - 1)
        val_r[:, lanes] = jnp.where((ids >> node_bits) == y, jnp.int32(1) << ((local >> ret_bits) * 4), 0)
        row, hit = place(block[8:24, :])
        hi_t[:, lanes] = row & (mine_spots - 1)
        val_t[:, lanes] = jnp.where(hit, jnp.int32(1) << ((row >> mine_bits) * 4), 0)

    def code_tile(tile, carry):
        table(tab_code, hi_t, val_t, mine_spots, tile * 128, 0)
        return carry

    def ret_tile(tile, carry):
        table(tab_ret, hi_r, val_r, ret_spots, tile * 128, 0)
        return carry

    first_tile, tiles = n // 128, grp // 128
    middle = (first_tile + tiles) // 2
    lax.fori_loop(first_tile, middle - 1, code_tile, 0)
    arrived(daggg, d_s, d_r, 0)
    d_copies[4].start()
    arrived(daggg, d_s, d_r, 1)
    d_copies[5].start()
    lax.fori_loop(middle - 1, middle + 1, code_tile, 0)
    arrived(daggg, d_s, d_r, 6)
    d_copies[8].start()
    arrived(daggg, d_s, d_r, 7)
    d_copies[9].start()
    lax.fori_loop(middle + 1, tiles, code_tile, 0)

    for step in steps_out:
        wb[step].wait_recv()
    share = wg_f[core, wg_rows(chip), :]
    for step in steps_out:
        share = share + wgb_rx[step].astype(F32)
    wgc[0] = share
    wc = []
    for at, (peer, slot) in enumerate(((y_right, 3), (y_left, 1), (y_far, 2))):
        wc.append(rcopy(wgc.at[0], wgc.at[slot], wc_s.at[at], wc_r.at[at], (w, peer)))
        wc[-1].start()

    arrived(daggg, d_s, d_r, 2)
    arrived(daggg, d_s, d_r, 3)
    acc[...] = dot(tab_code[:, 0 : 2 * n], daggg[0 : 2 * n, :]) + dot(tab_code[:, 3 * n :], daggg[3 * n :, :])
    for at in (4, 5, 8, 9):
        arrived(daggg, d_s, d_r, at)
    last = daggg[2 * n : 3 * n, :]
    block = own_half // 2

    def finished(first):
        rows = slice(first, first + block)
        return (acc[rows, :] + dot(tab_code[rows, 2 * n : 3 * n], last)) * (1.0 / 16)

    ca = {}
    for part in (1, 0):
        rows = pl.ds(part * block, block)
        cg_tx[rows, :] = finished(own_half + part * block).astype(BF16)
        ca[part] = rcopy(cg_tx.at[rows, :], cg_rx.at[rows, :], ca_s.at[part], ca_r.at[part], (other, y))
        ca[part].start()
    for part in (1, 0):
        acc[part * block : part * block + block, :] = finished(part * block)

    for at in range(3):
        wc[at].wait_recv()

    def share_rows(at):
        return pl.ds(pl.multiple_of(core * wrows + at * part_rows, part_rows), part_rows)

    wgd[share_rows(chip), :] = (wgc[0] + wgc[1] + wgc[2] + wgc[3]).astype(BF16)
    wd = {}
    for step in steps_out:
        mine_rows = wgd.at[share_rows(chip), :]
        wd[step] = rcopy(mine_rows, mine_rows, wd_s.at[step], wd_r.at[step], (chip_dev(step), y))
        wd[step].start()

    cb = {}
    for part in (1, 0):
        ca[part].wait_recv()
        for step in steps_out:
            if step * shard // block != part:
                continue
            rows = pl.ds(step * shard, shard)
            cgb_tx[step] = (acc[rows, :] + cg_rx[rows, :].astype(F32)).astype(BF16)
            cb[step] = rcopy(cgb_tx.at[step], cgb_rx.at[step], cb_s.at[step], cb_r.at[step], (chip_dev(step), y))
            cb[step].start()

    lax.fori_loop(0, grp // 128, ret_tile, 0)
    fgrad[...] = (dot_nt(dz_all[...], ws[...]) + dot(tab_ret[...], daggg[...]) * (1.0 / 8)).astype(BF16)

    own_sum = as_f[0:shard, :]
    own_cnt = as_cnt[0:shard, :]
    for step in steps_out:
        ab[step].wait_recv()
        own_sum = own_sum + asb_rx[step, :, 0:width].astype(F32)
        own_cnt = own_cnt + join_count(asb_rx[step, :, width:])
    first = (w * narrow + y) * shard
    cnt_row = counts[pl.ds(first // 128, 1), :]
    cnt_col[...] = jnp.transpose(jnp.broadcast_to(cnt_row, (128, 128)))
    if shard <= 128:
        old_cnt = cnt_col[pl.ds(pl.multiple_of(first % 128, shard), shard), :]
    else:
        old_cnt = jnp.concatenate(
            [jnp.transpose(jnp.broadcast_to(counts[pl.ds(first // 128 + b, 1), :], (128, 128))) for b in range(shard // 128)], 0
        )
    scale = 1.0 / (decay_rate * old_cnt + (1.0 - decay_rate) * own_cnt)
    old = sums[pl.ds(pl.multiple_of(first, shard), shard), :]
    for part in range(width // 128):
        lanes = slice(part * 128, part * 128 + 128)
        newcb[:, lanes] = (decay_rate * old[:, lanes] + (1.0 - decay_rate) * own_sum[:, lanes]) * scale

    for step in steps_out:
        source = wgd.at[share_rows(chip_at(step, -1)), :]
        rcopy(source, source, wd_s.at[step], wd_r.at[step], (chip_dev(step), y)).wait_recv()
    own_rows = wgd.at[pl.ds(pl.multiple_of(core * wrows, wrows), wrows), :]
    other_rows = wgd.at[pl.ds(pl.multiple_of((1 - core) * wrows, wrows), wrows), :]
    we = rcopy(own_rows, own_rows, we_s, we_r, (other, y))
    we.start()
    rcopy(other_rows, other_rows, we_s, we_r, (other, y)).wait_recv()
    sgrad[...] = wgd[0:wrows, :].astype(F32)
    ngrad[...] = wgd[wrows:, :].astype(F32)

    own = acc[0:shard, :] + cg_rx[0:shard, :].astype(F32)
    for step in steps_out:
        cb[step].wait_recv()
        own = own + cgb_rx[step].astype(F32)
    cgrad[...] = own

    for copy in (*f_copies, *d_copies, *i_copies, *g_copies, wa, aa, *ca.values(), *wc, we):
        copy.wait_send()
    for step in steps_out:
        for copies in (wb, ab, wd, cb):
            copies[step].wait_send()


def copy_kernel(count, *refs):
    copies = [pltpu.make_async_copy(refs[at], refs[count + at], refs[-1].at[at]) for at in range(count)]
    for copy in copies:
        copy.start()
    for copy in copies:
        copy.wait()


def on_device(
    wide, narrow,
    features, neighbours, code_ids, assignment, cotangent, code_sums, code_counts, self_weight, neighbour_weight,
):
    n, width = features.shape
    codes = code_sums.shape[0]
    chips = wide // 2
    shard = codes // (wide * narrow)
    mine = codes // narrow
    grp = n * narrow
    hbm = pl.BlockSpec(memory_space=pltpu.HBM)
    dma = pltpu.SemaphoreType.DMA
    wide_rows = self_weight.shape[0]
    scratch = [
        pltpu.VMEM((n, width), BF16),
        pltpu.VMEM((codes, width), F32),
        pltpu.VMEM((codes // 128, 128), F32),
        pltpu.VMEM(self_weight.shape, BF16),
        pltpu.VMEM(neighbour_weight.shape, BF16),
        pltpu.VMEM((codes, width), BF16),
        pltpu.VMEM((grp, width), BF16),
        pltpu.VMEM((grp, width), BF16),
        pltpu.VMEM((IDX_ROWS, n), I32),
        pltpu.VMEM((narrow, IDX_ROWS, n), jnp.int16),
        pltpu.VMEM((narrow, 1, n), I32),
        pltpu.VMEM((codes, n), BF16),
        pltpu.VMEM((grp, n), BF16),
        pltpu.VMEM((mine, grp), BF16),
        pltpu.VMEM((n, grp), BF16),
        pltpu.VMEM((mine, grp), BF16),
        pltpu.VMEM((16, n), I32),
        pltpu.VMEM((16, n), I32),
        pltpu.VMEM((8, n), I32),
        pltpu.VMEM((8, n), I32),
        pltpu.VMEM((16, grp), I32),
        pltpu.VMEM((16, grp), I32),
        pltpu.VMEM((8, grp), I32),
        pltpu.VMEM((8, grp), I32),
        pltpu.VMEM((1, grp), I32),
        pltpu.VMEM((mine // 16, grp), F32),
        pltpu.VMEM((16, grp), BF16),
        pltpu.VMEM((n, width), F32),
        pltpu.VMEM((n, width), F32),
        pltpu.VMEM((n, width), F32),
        pltpu.VMEM((n, width), BF16),
        pltpu.VMEM((n, 2 * width), BF16),
        pltpu.VMEM((mine, width), F32),
        pltpu.VMEM((2, wide_rows, width), F32),
        pltpu.VMEM((wide_rows, width), BF16),
        pltpu.VMEM((wide_rows, width), BF16),
        pltpu.VMEM((wide_rows, width), BF16),
        pltpu.VMEM((chips, wide_rows // chips, width), BF16),
        pltpu.VMEM((narrow, wide_rows // chips, width), F32),
        pltpu.VMEM((2 * wide_rows, width), BF16),
        pltpu.VMEM((mine, width), F32),
        pltpu.VMEM((mine, 128), F32),
        pltpu.VMEM((mine, 128), BF16),
        pltpu.VMEM((mine // 2, width + 128), BF16),
        pltpu.VMEM((mine // 2, width + 128), BF16),
        pltpu.VMEM((chips, shard, width + 128), BF16),
        pltpu.VMEM((chips, shard, width + 128), BF16),
        pltpu.VMEM((mine // 2, width), BF16),
        pltpu.VMEM((mine // 2, width), BF16),
        pltpu.VMEM((chips, shard, width), BF16),
        pltpu.VMEM((chips, shard, width), BF16),
        pltpu.VMEM((128, 128), F32),
        dma((9,)),
        dma((10,)), dma((10,)), dma((10,)), dma((10,)), dma((3,)), dma((3,)), dma((3,)), dma((3,)),
        dma, dma, dma((chips,)), dma((chips,)), dma((3,)), dma((3,)), dma((chips,)), dma((chips,)), dma, dma,
        dma, dma, dma((chips,)), dma((chips,)), dma((2,)), dma((2,)), dma((chips,)), dma((chips,)),
    ]
    shapes = (
        jax.ShapeDtypeStruct((n, width), BF16),
        jax.ShapeDtypeStruct((n, width), BF16),
        jax.ShapeDtypeStruct(self_weight.shape, F32),
        jax.ShapeDtypeStruct(neighbour_weight.shape, F32),
        jax.ShapeDtypeStruct((shard, width), F32),
        jax.ShapeDtypeStruct((shard, width), F32),
    )
    vm = pl.BlockSpec(memory_space=pltpu.VMEM)
    operands = (
        features, neighbours.T, code_ids.T, assignment.reshape(1, n), cotangent,
        code_sums, code_counts.reshape(codes // 128, 128), self_weight, neighbour_weight,
    )
    results = pl.pallas_call(
        functools.partial(kernel, wide, narrow, shard),
        out_shape=tuple(pltpu.VMEM(shape.shape, shape.dtype) for shape in shapes),
        in_specs=[hbm] * 9,
        out_specs=(vm,) * 6,
        scratch_shapes=scratch,
        compiler_params=pltpu.CompilerParams(
            collective_id=0, has_side_effects=True, vmem_limit_bytes=48 * 1024 * 1024
        ),
    )(*(pltpu.with_memory_space_constraint(operand, pltpu.HBM) for operand in operands))
    return pl.pallas_call(
        functools.partial(copy_kernel, len(shapes)),
        out_shape=shapes,
        in_specs=[vm] * 6,
        out_specs=(hbm,) * 6,
        scratch_shapes=[dma((6,))],
        compiler_params=pltpu.CompilerParams(vmem_limit_bytes=8 * 1024 * 1024),
    )(*results)


def solution(mesh):
    both = ("wide", "narrow")
    return jax.shard_map(
        functools.partial(on_device, mesh.shape["wide"], mesh.shape["narrow"]),
        mesh=mesh,
        in_specs=(P(both, None), P(both, None), P(both, None), P(both), P(both, None), P(), P(), P(), P()),
        out_specs=(P(both, None), P(both, None), P(), P(), P(both, None), P(both, None)),
        check_vma=False,
    )
```
